128 devices in a mesh: dp: 8 (over x, core), ctx: 16 (over y, z).
Axes of the slice: x: 4, y: 4, z: 4, core: 2. Of those that a mesh axis runs over, the one named last changes fastest.
Arguments:
- mixed_in: bfloat16 [8, 2048, 4096], P('dp', 'ctx'), may hold values from -6 to 6
- conv_weight: float32 [4, 4096], replicated, may hold values from -3 to 3
- gate_in: float32 [8, 2048, 32], P('dp', 'ctx'), may hold values from -9.7 to 9
- head_params: float32 [2, 16], replicated, may hold values from -3.5 to 1
- doc_lengths: int32 [8, 8], P('dp'), may hold values from 1 to 1024, 2048 in all within a row
- d_core: bfloat16 [8, 2048, 2048], P('dp', 'ctx'), may hold values from -6 to 6
Outputs:
- core_out: bfloat16 [8, 2048, 2048], P('dp', 'ctx')
- d_mixed: bfloat16 [8, 2048, 4096], P('dp', 'ctx')
- d_gates: float32 [8, 2048, 32], P('dp', 'ctx')
- d_conv: float32 [4, 4096], replicated
- d_head: float32 [2, 16], replicated
The draws below stay inside these ranges and needn't reach their ends.
Inputs may be any that keep to these rules, and one draw needn't show every extreme that they name: `doc_lengths`: the longest of a stream's 8 documents has exactly 1024 tokens.
All inputs are finite; a program needn't handle non-finite values.
Results may differ from the reference program's by a relative error of at most 0.0095.
Values may be sent and summed in bfloat16 or wider, within the bound.
A program may use at most 256 MiB of HBM per device.

```python
import math
import jax
import jax.numpy as jnp
import numpy as np
from jax import lax

VALUE_HEADS = 16
QK_HEADS = 8
DK = 128
DV = 128
KERNEL = 4
GROUP = 64
DOCS = 8
CH = 4096
STREAM_TOKENS = 2048
PACKED_COUNT = 8


def draw_gate_in(key, part):
    key = jax.random.fold_in(key, 11)
    every_key = jax.random.split(key, 6)
    slow_share = 0.5
    lagging_heads = jax.random.uniform(every_key[0], (PACKED_COUNT, 1, VALUE_HEADS)) < slow_share
    blocks = STREAM_TOKENS // GROUP
    block_shift = jax.random.uniform(every_key[1], (PACKED_COUNT, blocks, 1, VALUE_HEADS), jnp.float32, -0.7, 0.7)
    block_shift = jnp.broadcast_to(block_shift, (PACKED_COUNT, blocks, GROUP, VALUE_HEADS)).reshape(PACKED_COUNT, STREAM_TOKENS, VALUE_HEADS)
    rough = jax.random.uniform(every_key[2], (PACKED_COUNT, STREAM_TOKENS, VALUE_HEADS), jnp.float32, -1.0, 1.0)
    decay_logits = jnp.where(lagging_heads, -8.0, 1.0) + rough + block_shift
    spike_values = jax.random.uniform(every_key[3], (PACKED_COUNT, STREAM_TOKENS, 1)) < 4.0 / STREAM_TOKENS
    spike_value = 8.0 + jax.random.uniform(every_key[4], (PACKED_COUNT, STREAM_TOKENS, VALUE_HEADS), jnp.float32, -1.0, 1.0)
    decay_logits = jnp.where(spike_values & lagging_heads, spike_value, decay_logits)
    strength_raw = jnp.where(lagging_heads, -3.5, 0.0) + jax.random.uniform(every_key[5], (PACKED_COUNT, STREAM_TOKENS, VALUE_HEADS), jnp.float32, -1.5, 1.5)
    return jnp.concatenate([decay_logits, strength_raw], axis=-1).astype(jnp.float32)


def draw_head_params(key, part):
    key = jax.random.fold_in(key, 23)
    first, second = jax.random.split(key, 2)
    log_scale = jax.random.uniform(first, (1, VALUE_HEADS), jnp.float32, -3.5, -2.5)
    bias_row = jax.random.uniform(second, (1, VALUE_HEADS), jnp.float32, -1.0, 1.0)
    return jnp.concatenate([log_scale, bias_row], axis=0).astype(jnp.float32)


def block_scale(rng, shape, shards, least, largest):
    level = 1.0
    for axis_at, parts in shards:
        heights = jax.random.uniform(jax.random.fold_in(jax.random.fold_in(rng, 6), axis_at), (parts,), jnp.float32, least / len(shards), largest / len(shards))
        level = level * jnp.repeat(jnp.exp(heights), shape[axis_at] // parts).reshape((-1,) + (1,) * (len(shape) - 1 - axis_at))
    return level


def length_profile(number_of, total, reach, lean):
    loads = [(1 << 20) // math.isqrt(standing ** lean) + 1 for standing in range(2, number_of + 1)]
    rest, counts = total - reach - (number_of - 1), [1] * (number_of - 1)
    while rest > 0:
        free = [i for i in range(number_of - 1) if counts[i] < reach]
        pool, remaining = sum([loads[i] for i in free]), rest
        for i in free:
            extra = min(reach - counts[i], max(1, remaining * loads[i] // pool), rest)
            counts[i] = counts[i] + extra
            rest = rest - extra
    return np.array([reach] + counts)


def ragged_sizes(own_key, count, total, bound, lean):
    if count == 2:
        one = jax.random.randint(own_key, (), max(1, total - bound), min(bound, total - 1) + 1)
        return jnp.stack([one, total - one])
    sizes = jnp.asarray(length_profile(count, total, bound, lean), jnp.int32)
    twos = (count - 1) // 2
    donor, taker = sizes[1:1 + 2 * twos:2], sizes[2:2 + 2 * twos:2]
    room = jnp.minimum(donor - 1, bound - taker)
    shifted = jax.random.randint(jax.random.fold_in(own_key, 1), (twos,), 0, 1 << 20) % (room + 1)
    sizes = sizes.at[1:1 + 2 * twos:2].set(donor - shifted).at[2:2 + 2 * twos:2].set(taker + shifted)
    return sizes[jax.random.permutation(jax.random.fold_in(own_key, 2), count)]


def normal_values(rng, extent, width, limit, cuts=(), kind=jnp.bfloat16):
    entries = jax.random.normal(rng, extent, jnp.float32) * width
    if len(cuts) > 0:
        entries = block_scale(rng, extent, cuts, -0.22, 0.18) * entries
    return jnp.clip(entries, min=-limit, max=limit).astype(kind)


def setup_inputs(seed: int = 0) -> dict:
    streams_of = jax.random.split(jax.random.key(seed), 7)
    mixed_in = normal_values(streams_of[0], (PACKED_COUNT, STREAM_TOKENS, CH), 1.0, 6.0, ((0, 8), (1, 16)))
    conv_weight = normal_values(streams_of[1], (KERNEL, CH), KERNEL ** -0.5, 3.0, (), jnp.float32)
    gate_in = draw_gate_in(jax.random.fold_in(streams_of[6], 71), 0)
    head_params = draw_head_params(jax.random.fold_in(streams_of[6], 71), 0)
    doc_lengths = jax.vmap(lambda own: ragged_sizes(own, DOCS, STREAM_TOKENS, STREAM_TOKENS // 2, 2))(jax.random.split(streams_of[4], PACKED_COUNT)).reshape((PACKED_COUNT, DOCS)).astype(jnp.int32)
    d_core = normal_values(streams_of[5], (PACKED_COUNT, STREAM_TOKENS, VALUE_HEADS * DV), 1.0, 6.0, ((0, 8), (1, 16)))
    return dict(mixed_in=mixed_in, conv_weight=conv_weight, gate_in=gate_in, head_params=head_params, doc_lengths=doc_lengths, d_core=d_core)


def group_head(memory, queries, key_rows, value_rows, decays, beta_rows, doc_ids, doc_before):
    highest = lax.Precision.HIGHEST
    length = queries.shape[0]
    summed = jnp.cumsum(decays)
    row_idx = jnp.arange(length)[:, None]
    col_idx = jnp.arange(length)[None, :]
    linked = (doc_ids[:, None] == doc_ids[None, :]) & (row_idx >= col_idx)
    spans = jnp.where(linked, jnp.exp(jnp.minimum(summed[:, None] - summed[None, :], 0.0)), 0.0)
    carried = jnp.exp(summed) * (doc_ids == doc_before).astype(jnp.float32)
    key_prod = jnp.dot(key_rows, key_rows.T, precision=highest)
    strict = jnp.where(row_idx > col_idx, beta_rows[:, None] * spans * key_prod, 0.0)
    system = strict + jnp.eye(length, dtype=jnp.float32)
    right_side = beta_rows[:, None] * value_rows - (beta_rows * carried)[:, None] * jnp.dot(key_rows, memory.T, precision=highest)
    updates = lax.linalg.triangular_solve(system, right_side, left_side=True, lower=True, unit_diagonal=True)
    scores = spans * jnp.dot(queries, key_rows.T, precision=highest)
    outputs = carried[:, None] * jnp.dot(queries, memory.T, precision=highest) + jnp.dot(scores, updates, precision=highest)
    memory_new = carried[-1] * memory + jnp.dot((spans[-1][:, None] * updates).T, key_rows, precision=highest)
    return (memory_new, outputs)

def delta_core(queries, key_rows, value_rows, decays, beta_rows, doc_ext, memory):
    length = queries.shape[0]
    blocks = length // GROUP
    doc_ids = doc_ext[1:].reshape(blocks, GROUP)
    doc_before = doc_ext[:-1].reshape(blocks, GROUP)[:, 0]

    def folded(array):
        return array.reshape((blocks, GROUP) + array.shape[1:])
    per_head = jax.vmap(group_head, in_axes=(0, 1, 1, 1, 1, 1, None, None), out_axes=(0, 1))

    def advance(carry_state, inputs):
        return per_head(carry_state, *inputs)
    final, outputs = lax.scan(jax.checkpoint(advance), memory, (folded(queries), folded(key_rows), folded(value_rows), folded(decays), folded(beta_rows), doc_ids, doc_before))
    return (outputs.reshape((length,) + outputs.shape[2:]), final)

def prepare(x_ext, conv_w, gates, head_params, doc_all):
    taps = conv_w.shape[0]
    length = x_ext.shape[0] - taps + 1
    mixed = jnp.zeros((length, x_ext.shape[1]), jnp.float32)
    for offset in range(taps):
        linked = (doc_all[offset:offset + length] == doc_all[taps - 1:]).astype(jnp.float32)
        mixed = mixed + x_ext[offset:offset + length] * conv_w[offset] * linked[:, None]
    mixed = jax.nn.silu(mixed)
    width_qk = QK_HEADS * DK
    queries = mixed[:, :width_qk].reshape(length, QK_HEADS, DK)
    key_rows = mixed[:, width_qk:2 * width_qk].reshape(length, QK_HEADS, DK)
    value_rows = mixed[:, 2 * width_qk:].reshape(length, VALUE_HEADS, DV)
    queries = queries * lax.rsqrt(lax.optimization_barrier(jnp.sum(queries * queries, axis=-1, keepdims=True)) + 1e-06) * DK ** (-0.5)
    key_rows = key_rows * lax.rsqrt(lax.optimization_barrier(jnp.sum(key_rows * key_rows, axis=-1, keepdims=True)) + 1e-06)
    ratio = VALUE_HEADS // QK_HEADS
    queries = jnp.repeat(queries, ratio, axis=1)
    key_rows = jnp.repeat(key_rows, ratio, axis=1)
    decays = -jnp.exp(head_params[0]) * jax.nn.softplus(gates[:, :VALUE_HEADS] + head_params[1])
    beta_rows = jax.nn.sigmoid(gates[:, VALUE_HEADS:])
    return (queries, key_rows, value_rows, decays, beta_rows)

def stream_forward(mixed, conv_w, gates, head_params, lengths):
    taps = conv_w.shape[0]
    length = mixed.shape[0]
    ends = jnp.cumsum(lengths).astype(jnp.int32)
    positions = jnp.arange(length + taps - 1, dtype=jnp.int32) - (taps - 1)
    doc_all = lax.optimization_barrier(jnp.sum((ends[None, :] <= positions[:, None]).astype(jnp.int32), axis=1)).astype(jnp.int32)
    x_ext = jnp.concatenate([jnp.zeros((taps - 1, mixed.shape[1]), jnp.float32), mixed], axis=0)
    queries, key_rows, value_rows, decays, beta_rows = prepare(x_ext, conv_w, gates, head_params, doc_all)
    memory = jnp.zeros((VALUE_HEADS, DV, DK), jnp.float32)
    outputs, final = delta_core(queries, key_rows, value_rows, decays, beta_rows, doc_all[taps - 2:], memory)
    return outputs

def reference(mixed_in, conv_weight, gate_in, head_params, doc_lengths, d_core):

    def forward_all(mixed, conv_w, gates, params):
        return jax.vmap(stream_forward, in_axes=(0, None, 0, None, 0))(mixed, conv_w, gates, params, doc_lengths)
    outputs, pullback = jax.vjp(forward_all, mixed_in.astype(jnp.float32), conv_weight, gate_in, head_params)
    cotangent = d_core.astype(jnp.float32).reshape(outputs.shape)
    d_mixed, d_conv, d_gates, d_head = pullback(cotangent)
    core_out = outputs.reshape(outputs.shape[0], outputs.shape[1], VALUE_HEADS * DV).astype(jnp.bfloat16)
    return (core_out, d_mixed.astype(jnp.bfloat16), d_gates, d_conv, d_head)
```

```python
import jax
import jax.numpy as jnp
from jax import lax
from jax.experimental import pallas as pl
from jax.experimental.pallas import tpu as pltpu
from jax.sharding import PartitionSpec as P

HEADS = 16
QK = 8
D = 128
ROWS = 128
CH = 4096
BLOCKS = 16
PACK = 3 * D + 16
HG = 4
F32 = jnp.float32
BF = jnp.bfloat16
MESH = pl.DeviceIdType.MESH
HIGHEST = lax.Precision.HIGHEST


def dot(a, b, ca=1, cb=0):
    return lax.dot_general(a, b, (((ca,), (cb,)), ((), ())), preferred_element_type=F32)


def dot_full(a, b, ca=1, cb=0):
    return lax.dot_general(
        a, b, (((ca,), (cb,)), ((), ())), preferred_element_type=F32, precision=HIGHEST
    )


def split(a):
    high = a.astype(BF)
    return high, (a - high.astype(F32)).astype(BF)


def dot3(a, b, ca=1, cb=0):
    return dot(a[0], b[0], ca, cb) + (dot(a[0], b[1], ca, cb) + dot(a[1], b[0], ca, cb))


def iota(shape, dim):
    return lax.broadcasted_iota(jnp.int32, shape, dim)


def inverses(mats):
    row, col = iota((D, D), 0), iota((D, D), 1)
    eye = (row == col).astype(F32)

    def same(bits):
        return (row >> bits) == (col >> bits)

    near = same(3)
    a8 = [jnp.where(near, a, 0.0) for a in mats]
    a8s = [split(a) for a in a8]
    a2 = [dot3(s, s) for s in a8s]
    a2s = [split(a) for a in a2]
    a3 = [dot3(s, t) for s, t in zip(a8s, a2s)]
    a4s = [split(dot3(s, s)) for s in a2s]
    ys = [eye - a + b - c for a, b, c in zip(a8, a2, a3)]
    xs = [y + dot3(split(y), s) for y, s in zip(ys, a4s)]
    for bits in range(3, 7):
        mask = same(bits + 1) & jnp.logical_not(same(bits))
        cs = [split(jnp.where(mask, a, 0.0)) for a in mats]
        xss = [split(x) for x in xs]
        xc = [split(dot3(x, c)) for x, c in zip(xss, cs)]
        xs = [x - dot3(t, s) for x, t, s in zip(xs, xc, xss)]
    return xs


def kernel(
    x_ref, w_ref, gate_ref, hp_ref, len_ref, dcore_ref,
    core_ref, dmix_ref, dgate_ref, red_ref,
    xs, ys, qs, ks, links, lks, gt, gts, d_s, dkk_s, p_s, x_s, uv_s, wq_s, w2_s, r0_s, ol_s,
    snd, rcv, s_snd, g_snd, s_rcv, g_rcv, h_snd, h_rcv, e_snd, e_rcv, dgt,
    snd_sem, rcv_sem, s_ssem, s_rsem, g_ssem, g_rsem, h_sem, e_sem,
):
    me = lax.axis_index("ctx")
    first_pos = me * ROWS

    barrier = pltpu.get_barrier_semaphore()

    def greet(i, _):
        pl.semaphore_signal(
            barrier, inc=1, device_id={"ctx": lax.rem(me + i, BLOCKS)}, device_id_type=MESH
        )
        return 0

    lax.fori_loop(1, BLOCKS, greet, 0)

    xs[pl.ds(8, ROWS), :] = x_ref[...].astype(F32)
    tail = [
        xs[pl.ds(133 + r, 1), pl.ds(1024 * p, 1024)] for r in range(3) for p in range(4)
    ] + [jnp.zeros((4, 1024), F32)]
    h_snd[...] = jnp.concatenate(tail, axis=0).astype(BF)

    pl.semaphore_wait(barrier, BLOCKS - 1)

    def halo_copy():
        return pltpu.make_async_remote_copy(
            src_ref=h_snd, dst_ref=h_rcv, send_sem=h_sem.at[0], recv_sem=h_sem.at[1],
            device_id={"ctx": lax.rem(me + 1, BLOCKS)}, device_id_type=MESH,
        )

    halo_copy().start()

    row, col = iota((ROWS, D), 0), iota((ROWS, D), 1)
    low = row >= col
    strict = row > col
    ends = []
    total = 0
    for i in range(8):
        total = total + len_ref[0, i]
        ends.append(total)

    def doc_of(pos):
        found = jnp.zeros(pos.shape, jnp.int32)
        for e in ends:
            found = found + jnp.where(e <= pos, 1, 0)
        return found

    doc_col = doc_of(first_pos + row)
    doc_row = doc_of(first_pos + col)
    lks[...] = jnp.where((doc_col == doc_row) & low, 1.0, 0.0)
    for j in range(3):
        links[j] = jnp.where(doc_of(first_pos + row - 3 + j) == doc_col, 1.0, 0.0)
    doc_row16 = doc_row[:HEADS]
    doc_before = doc_of(jnp.full((HEADS, D), first_pos - 1, jnp.int32))
    doc_last = doc_of(jnp.full((HEADS, D), first_pos + ROWS - 1, jnp.int32))

    eye32 = (iota((32, 32), 0) == iota((32, 32), 1)).astype(F32)
    eye16 = (iota((16, 16), 0) == iota((16, 16), 1)).astype(F32)
    gates = dot_full(eye32, gate_ref[...], 1, 1)
    params = dot_full(eye16, hp_ref[...], 1, 1)
    scale = -jnp.exp(params[:, 0:1])
    z = gates[:HEADS] + params[:, 1:2]
    decay = scale * (jnp.maximum(z, 0.0) + jnp.log1p(jnp.exp(-jnp.abs(z))))
    ez = scale / (1.0 + jnp.exp(-z))
    beta = 1.0 / (1.0 + jnp.exp(-gates[HEADS:]))
    upto = jnp.where(row <= col, 1.0, 0.0)
    summed = dot_full(decay, upto)
    carried = jnp.exp(summed) * (doc_row16 == doc_before).astype(F32)
    to_end = jnp.exp(jnp.minimum(summed[:, D - 1 : D] - summed, 0.0)) * (
        doc_row16 == doc_last
    ).astype(F32)
    gts[0] = decay
    gts[1] = ez
    gts[2] = beta
    rows8 = jnp.stack(
        [summed, beta, carried, to_end, beta * carried, summed, summed, summed], axis=1
    )
    gt[...] = rows8

    halo_copy().wait()
    inside = jnp.where(me > 0, 1.0, 0.0)
    hv = h_rcv[...].astype(F32) * inside
    for r in range(3):
        for p in range(4):
            xs[pl.ds(5 + r, 1), pl.ds(1024 * p, 1024)] = hv[4 * r + p : 4 * r + p + 1]

    def lanes(block):
        return pl.ds(pl.multiple_of(block * D, D), D)

    def taps(j, block):
        t = xs[pl.ds(5 + j, ROWS), lanes(block)]
        return t if j == 3 else t * links[j]

    def conv(block):
        y = taps(3, block) * w_ref[3:4, lanes(block)]
        for j in range(3):
            y = y + taps(j, block) * w_ref[j : j + 1, lanes(block)]
        ys[:, lanes(block)] = y
        return y / (1.0 + jnp.exp(-y))

    def columns(h):
        t = jnp.transpose(gt[h])
        return [t[:, i : i + 1] for i in range(5)]

    def a_last(h):
        return gt[h][2:3, D - 1 : D]

    def pack_copy(h, source):
        return pltpu.make_async_remote_copy(
            src_ref=snd.at[h], dst_ref=rcv.at[source], send_sem=snd_sem.at[h],
            recv_sem=rcv_sem.at[source], device_id={"ctx": h}, device_id_type=MESH,
        )

    def forward(step, _):
        group = lax.rem(step + me, HEADS // HG)
        nq = HG // 2
        qk = [group * nq + i for i in range(nq)]
        heads = [group * HG + i for i in range(HG)]
        kk, qq, kf, qf = [], [], [], []
        for j in qk:
            m = conv(j)
            q = m * (lax.rsqrt(jnp.sum(m * m, axis=1, keepdims=True) + 1e-6) * D**-0.5)
            m = conv(QK + j)
            k = m * lax.rsqrt(jnp.sum(m * m, axis=1, keepdims=True) + 1e-6)
            qs[j] = q
            ks[j] = k
            k2, q2 = split(k), split(q)
            kk.append(dot3(k2, k2, 1, 1))
            qq.append(dot3(q2, k2, 1, 1))
            kf.append(k)
            qf.append(q)
        vs = [conv(2 * QK + h) for h in heads]
        cols = [columns(h) for h in heads]
        lk = lks[...]
        mats, ps = [], []
        for i, h in enumerate(heads):
            spans = lk * jnp.exp(jnp.minimum(cols[i][0] - gt[h][0:1], 0.0))
            dkk = jnp.where(strict, spans * kk[i // 2], 0.0)
            p = spans * qq[i // 2]
            d_s[h] = spans
            dkk_s[h] = dkk
            p_s[h] = p
            ps.append(p.astype(BF))
            mats.append(cols[i][1] * dkk)
        xinv = inverses(mats)
        for i, h in enumerate(heads):
            x_s[h] = xinv[i]
            right = jnp.concatenate([cols[i][1] * vs[i], cols[i][4] * kf[i // 2]], axis=1)
            uvw = dot3(split(xinv[i]), split(right))
            uvwb = uvw.astype(BF)
            uv_s[h] = uvw[:, :D]
            wq_s[h, 0:ROWS] = uvwb[:, D:]
            pw = dot(ps[i], uvwb)
            ol_s[h] = pw[:, :D]
            qc = (cols[i][2] * qf[i // 2] - pw[:, D:]).astype(BF)
            wq_s[h, ROWS : 2 * ROWS] = qc
            dk = (cols[i][3] * kf[i // 2]).astype(BF)
            nb = dot(uvwb, dk, 0, 0)
            gl = dot(dcore_ref[:, lanes(h)], qc, 0, 0)
            snd[h, 0:D] = nb[D:].astype(BF)
            snd[h, D : 2 * D] = nb[:D].astype(BF)
            snd[h, 2 * D : 3 * D] = gl.astype(BF)
            al = jnp.broadcast_to(a_last(h), (16, D))
            t0 = al.astype(BF).astype(F32)
            t1 = (al - t0).astype(BF).astype(F32)
            t2 = al - t0 - t1
            r16 = iota((16, D), 0)
            snd[h, 3 * D : PACK] = jnp.where(
                r16 == 0, t0, jnp.where(r16 == 1, t1, jnp.where(r16 == 2, t2, 0.0))
            ).astype(BF)
        for h in heads:
            @pl.when(h != me)
            def _():
                pack_copy(h, me).start()
        return 0

    lax.fori_loop(0, HEADS // HG, forward, 0)
    rcv[me] = snd[me]

    def aside(step, _):
        heads = [step * HG + i for i in range(HG)]
        for i, h in enumerate(heads):
            cols = columns(h)
            zz = dot(p_s[h].astype(BF), dcore_ref[:, lanes(h)], 0, 0)
            dk = cols[3] * ks[h // 2]
            out = dot3(split(x_s[h]), split(jnp.concatenate([zz, dk], axis=1)), 0, 0)
            r0_s[h] = out[:, :D]
            w2_s[h] = out[:, D:].astype(BF)
        return 0

    lax.fori_loop(0, HEADS // HG, aside, 0)

    def wait_pack(i, _):
        pack_copy(lax.rem(me + i, BLOCKS), lax.rem(me + i, BLOCKS)).wait_recv()
        return 0

    lax.fori_loop(1, BLOCKS, wait_pack, 0)

    def s_copy(block, head):
        return pltpu.make_async_remote_copy(
            src_ref=s_snd.at[block], dst_ref=s_rcv.at[head], send_sem=s_ssem.at[block],
            recv_sem=s_rsem.at[head], device_id={"ctx": block}, device_id_type=MESH,
        )

    def g_copy(block, head):
        return pltpu.make_async_remote_copy(
            src_ref=g_snd.at[block], dst_ref=g_rcv.at[head], send_sem=g_ssem.at[block],
            recv_sem=g_rsem.at[head], device_id={"ctx": block}, device_id_type=MESH,
        )

    def send_state(block, state):
        s_snd[block] = state

        @pl.when(block != me)
        def _():
            s_copy(block, me).start()

    def send_grad(block, grad):
        g_snd[block] = grad

        @pl.when(block != me)
        def _():
            g_copy(block, me).start()

    zero = jnp.zeros((D, D), F32)
    send_state(0, zero.astype(BF))
    send_grad(BLOCKS - 1, zero.astype(BF))

    def scalar_of(block):
        t = rcv[block, 3 * D : PACK].astype(F32)
        return t[0:1] + t[1:2] + t[2:3]

    def turn(i, carry):
        state, grad = carry
        b = BLOCKS - 1 - i
        state = (
            scalar_of(i) * state
            - dot(state.astype(BF), rcv[i, 0:D])
            + rcv[i, D : 2 * D].astype(F32)
        )
        grad = (
            scalar_of(b) * grad
            - dot(grad.astype(BF), rcv[b, 0:D], 1, 1)
            + rcv[b, 2 * D : 3 * D].astype(F32)
        )
        send_state(i + 1, state.astype(BF))
        send_grad(b - 1, grad.astype(BF))
        return state, grad

    lax.fori_loop(0, BLOCKS - 1, turn, (zero, zero))
    s_rcv[me] = s_snd[me]
    g_rcv[me] = g_snd[me]

    lane = col
    row8 = row[:8]

    def conv_back(block, dm):
        y = ys[:, lanes(block)]
        sig = 1.0 / (1.0 + jnp.exp(-y))
        dy = dm * (sig * (1.0 + y * (1.0 - sig)))
        red_ref[3:4, lanes(block)] = jnp.sum(dy * taps(3, block), axis=0, keepdims=True)
        own = dy * w_ref[3:4, lanes(block)]
        spill = jnp.zeros((8, D), F32)
        for j in range(3):
            ej = dy * links[j]
            red_ref[j : j + 1, lanes(block)] = jnp.sum(
                ej * xs[pl.ds(5 + j, ROWS), lanes(block)], axis=0, keepdims=True
            )
            turned = pltpu.roll(ej * w_ref[j : j + 1, lanes(block)], ROWS - 3 + j, 0)
            wrapped = row >= ROWS - 3 + j
            own = own + jnp.where(wrapped, 0.0, turned)
            spill = spill + jnp.where(row8 >= 5 + j, turned[ROWS - 8 :], 0.0)
        dmix_ref[:, lanes(block)] = own.astype(BF)
        e_snd[0:8, lanes(block)] = own[ROWS - 8 :]
        e_snd[8:16, lanes(block)] = spill

    def backward(step, _):
        group = lax.rem(step + me, HEADS // HG)
        nq = HG // 2
        qk = [group * nq + i for i in range(nq)]
        heads = [group * HG + i for i in range(HG)]
        for h in heads:
            @pl.when(h != me)
            def _():
                s_copy(h, h).wait_recv()
                g_copy(h, h).wait_recv()
        packed = jnp.zeros((ROWS, D), F32)
        colsums, lasts = [], []
        for n, j in enumerate(qk):
            k, q = ks[j], qs[j]
            bs = es = dq = dk = None
            for i in (2 * n, 2 * n + 1):
                h = heads[i]
                _, bet, car, end, bcar = columns(h)
                s, g = s_rcv[h], g_rcv[h]
                do = dcore_ref[:, lanes(h)]
                t = dot(wq_s[h], s, 1, 1)
                u = (uv_s[h] - t[:ROWS]).astype(BF)
                core_ref[:, lanes(h)] = (ol_s[h] + t[ROWS:]).astype(BF)
                r = r0_s[h] + dot(w2_s[h], g, 1, 1)
                dr = jnp.concatenate([do, r.astype(BF)], axis=0)
                t2 = dot(dr, s)
                dos, rs = t2[:ROWS], t2[ROWS:]
                t3 = dot(dr, u, 1, 1)
                dp, da = t3[:ROWS], -t3[ROWS:]
                ug = dot(u, g)
                spans = d_s[h]
                t1 = da * dkk_s[h]
                f = dp * p_s[h] + bet * t1
                yv = ys[:, lanes(2 * QK + h)]
                v = yv / (1.0 + jnp.exp(-yv))
                krs = car * k * rs
                dkug = end * k * ug
                dbeta = jnp.sum(r * v - krs + t1, axis=1, keepdims=True)
                dc = jnp.sum(f + car * q * dos - bet * krs - dkug, axis=1, keepdims=True)
                packed = packed + jnp.where(lane == 2 * i, dc, 0.0)
                packed = packed + jnp.where(lane == 2 * i + 1, dbeta, 0.0)
                colsums.append(jnp.sum(f, axis=0, keepdims=True))
                lasts.append(
                    jnp.sum(
                        jnp.sum(dkug, axis=0, keepdims=True)
                        + a_last(h)
                        * jnp.sum(g.astype(F32) * s.astype(F32), axis=0, keepdims=True),
                        axis=1, keepdims=True,
                    )
                )
                bq = dp * spans
                e = jnp.where(strict, bet * da * spans, 0.0)
                dqi = car * dos
                dki = end * ug - bcar * rs
                bs = bq if bs is None else bs + bq
                es = e if es is None else es + e
                dq = dqi if dq is None else dq + dqi
                dk = dki if dk is None else dk + dki
                conv_back(2 * QK + h, bet * r)
            be = jnp.concatenate([bs, es], axis=0).astype(BF)
            kb = k.astype(BF)
            t4 = dot(be, kb)
            t5 = dot(be, jnp.concatenate([q.astype(BF), kb], axis=0), 0, 0)
            dq = dq + t4[:ROWS]
            dk = dk + t4[ROWS:] + t5
            y = ys[:, lanes(j)]
            m = y / (1.0 + jnp.exp(-y))
            rq = lax.rsqrt(jnp.sum(m * m, axis=1, keepdims=True) + 1e-6)
            dm = rq * (D**-0.5) * (dq - m * (rq * rq * jnp.sum(m * dq, axis=1, keepdims=True)))
            conv_back(j, dm)
            y = ys[:, lanes(QK + j)]
            m = y / (1.0 + jnp.exp(-y))
            rk = lax.rsqrt(jnp.sum(m * m, axis=1, keepdims=True) + 1e-6)
            dm = rk * (dk - m * (rk * rk * jnp.sum(m * dk, axis=1, keepdims=True)))
            conv_back(QK + j, dm)
        rows = jnp.transpose(packed)
        lane1 = lane[:1]
        for i, h in enumerate(heads):
            dgt[0, pl.ds(h, 1), :] = (
                rows[2 * i : 2 * i + 1] - colsums[i] + jnp.where(lane1 == D - 1, lasts[i], 0.0)
            )
            dgt[1, pl.ds(h, 1), :] = rows[2 * i + 1 : 2 * i + 2]
        return 0

    lax.fori_loop(0, HEADS // HG, backward, 0)

    spill = e_snd[8:16, :]
    h_snd[...] = jnp.concatenate(
        [spill[5 + r : 6 + r, 1024 * p : 1024 * p + 1024] for r in range(3) for p in range(4)]
        + [jnp.zeros((4, 1024), F32)],
        axis=0,
    ).astype(BF)
    back = pltpu.make_async_remote_copy(
        src_ref=h_snd, dst_ref=e_rcv, send_sem=e_sem.at[0], recv_sem=e_sem.at[1],
        device_id={"ctx": lax.rem(me + BLOCKS - 1, BLOCKS)}, device_id_type=MESH,
    )
    back.start()

    dg = dot_full(dgt[0], jnp.where(row >= col, 1.0, 0.0))
    dz = dg * gts[1]
    bet = gts[2]
    both = jnp.concatenate([dz, dgt[1] * bet * (1.0 - bet)], axis=0)
    dgate_ref[...] = dot_full(jnp.where(row == col, 1.0, 0.0), both, 1, 1)
    ones = jnp.ones((1, D), F32)
    red_ref[4:8, :] = jnp.zeros((4, CH), F32)
    red_ref[4:5, 0:HEADS] = dot_full(ones, dg * gts[0], 1, 1)
    red_ref[5:6, 0:HEADS] = dot_full(ones, dz, 1, 1)

    back.wait()
    before_last = jnp.where(me < BLOCKS - 1, 1.0, 0.0)
    ev = e_rcv[...].astype(F32) * before_last
    for p in range(4):
        pieces = [jnp.zeros((5, 1024), F32)] + [ev[4 * r + p : 4 * r + p + 1] for r in range(3)]
        part = e_snd[0:8, 1024 * p : 1024 * p + 1024] + jnp.concatenate(pieces, axis=0)
        old = dmix_ref[ROWS - 16 :, 1024 * p : 1024 * p + 1024].astype(F32)
        dmix_ref[ROWS - 16 :, 1024 * p : 1024 * p + 1024] = jnp.concatenate(
            [old[:8], part], axis=0
        ).astype(BF)

    def drain(i, _):
        other = lax.rem(me + i, BLOCKS)
        pack_copy(other, me).wait_send()
        s_copy(other, me).wait_send()
        g_copy(other, me).wait_send()
        return 0

    lax.fori_loop(1, BLOCKS, drain, 0)


def on_device(mixed_in, conv_weight, gate_in, head_params, doc_lengths, d_core):
    vmem = pl.BlockSpec(memory_space=pltpu.VMEM)
    mat = (HEADS, D, D)
    scratch = [
        pltpu.VMEM((ROWS + 8, CH), F32),
        pltpu.VMEM((ROWS, CH), F32),
        pltpu.VMEM((QK, D, D), F32),
        pltpu.VMEM((QK, D, D), F32),
        pltpu.VMEM((3, ROWS, D), F32),
        pltpu.VMEM((ROWS, D), F32),
        pltpu.VMEM((HEADS, 8, D), F32),
        pltpu.VMEM((3, HEADS, D), F32),
        pltpu.VMEM(mat, F32),
        pltpu.VMEM(mat, F32),
        pltpu.VMEM(mat, F32),
        pltpu.VMEM(mat, F32),
        pltpu.VMEM(mat, F32),
        pltpu.VMEM((HEADS, 2 * D, D), BF),
        pltpu.VMEM(mat, BF),
        pltpu.VMEM(mat, F32),
        pltpu.VMEM(mat, F32),
        pltpu.VMEM((HEADS, PACK, D), BF),
        pltpu.VMEM((HEADS, PACK, D), BF),
        pltpu.VMEM(mat, BF),
        pltpu.VMEM(mat, BF),
        pltpu.VMEM(mat, BF),
        pltpu.VMEM(mat, BF),
        pltpu.VMEM((16, 1024), BF),
        pltpu.VMEM((16, 1024), BF),
        pltpu.VMEM((16, CH), F32),
        pltpu.VMEM((16, 1024), BF),
        pltpu.VMEM((2, HEADS, D), F32),
        pltpu.SemaphoreType.DMA((BLOCKS,)),
        pltpu.SemaphoreType.DMA((BLOCKS,)),
        pltpu.SemaphoreType.DMA((BLOCKS,)),
        pltpu.SemaphoreType.DMA((BLOCKS,)),
        pltpu.SemaphoreType.DMA((BLOCKS,)),
        pltpu.SemaphoreType.DMA((BLOCKS,)),
        pltpu.SemaphoreType.DMA((2,)),
        pltpu.SemaphoreType.DMA((2,)),
    ]
    core, dmix, dgate, red = pl.pallas_call(
        kernel,
        out_shape=(
            jax.ShapeDtypeStruct((ROWS, HEADS * D), BF),
            jax.ShapeDtypeStruct((ROWS, CH), BF),
            jax.ShapeDtypeStruct((ROWS, 2 * HEADS), F32),
            jax.ShapeDtypeStruct((8, CH), F32),
        ),
        in_specs=[vmem, vmem, vmem, vmem, pl.BlockSpec(memory_space=pltpu.SMEM), vmem],
        out_specs=(vmem, vmem, vmem, vmem),
        scratch_shapes=scratch,
        compiler_params=pltpu.CompilerParams(
            collective_id=0, has_side_effects=True, vmem_limit_bytes=56 * 1024 * 1024
        ),
        name="delta_mix",
    )(mixed_in[0], conv_weight, gate_in[0], head_params, doc_lengths, d_core[0])
    red = lax.psum(red, ("dp", "ctx"))
    return core[None], dmix[None], dgate[None], red[:4], red[4:6, :HEADS]


def solution(mesh):
    return jax.shard_map(
        on_device,
        mesh=mesh,
        in_specs=(
            P("dp", "ctx", None),
            P(),
            P("dp", "ctx", None),
            P(),
            P("dp", None),
            P("dp", "ctx", None),
        ),
        out_specs=(P("dp", "ctx", None), P("dp", "ctx", None), P("dp", "ctx", None), P(), P()),
        check_vma=False,
    )
```

```python
import jax
import jax.numpy as jnp
from jax import lax
from jax.experimental import pallas as pl
from jax.experimental.pallas import tpu as pltpu
from jax.sharding import PartitionSpec as P

HEADS = 16
QK = 8
D = 128
ROWS = 128
CH = 4096
BLOCKS = 16
PACK = 3 * D + 16
FG = 8
HG = 4
ASIDE = 2
DP = 8
PIECE = CH // BLOCKS
F32 = jnp.float32
BF = jnp.bfloat16
MESH = pl.DeviceIdType.MESH
HIGHEST = lax.Precision.HIGHEST


def dot(a, b, ca=1, cb=0):
    return lax.dot_general(a, b, (((ca,), (cb,)), ((), ())), preferred_element_type=F32)


def dot_full(a, b, ca=1, cb=0):
    return lax.dot_general(
        a, b, (((ca,), (cb,)), ((), ())), preferred_element_type=F32, precision=HIGHEST
    )


def split(a):
    high = a.astype(BF)
    return high, (a - high.astype(F32)).astype(BF)


def dot3(a, b, ca=1, cb=0):
    left = jnp.concatenate(a, axis=ca)
    wide = jnp.concatenate(b, axis=1 - cb)
    n = b[0].shape[1 - cb]
    t = dot(left, jnp.concatenate([wide, wide], axis=cb), ca, cb)
    return t[:, :n] + t[:, n:]


def iota(shape, dim):
    return lax.broadcasted_iota(jnp.int32, shape, dim)


def inverses(mats):
    row, col = iota((D, D), 0), iota((D, D), 1)
    eye = (row == col).astype(F32)

    def same(bits):
        return (row >> bits) == (col >> bits)

    near = same(3)
    a8 = [jnp.where(near, a, 0.0) for a in mats]
    a8s = [split(a) for a in a8]
    a2 = [dot3(s, s) for s in a8s]
    a2s = [split(a) for a in a2]
    a3 = [dot3(s, t) for s, t in zip(a8s, a2s)]
    a4s = [split(dot3(s, s)) for s in a2s]
    ys = [eye - a + b - c for a, b, c in zip(a8, a2, a3)]
    xs = [y + dot3(split(y), s) for y, s in zip(ys, a4s)]
    for bits in range(3, 7):
        mask = same(bits + 1) & jnp.logical_not(same(bits))
        cs = [split(jnp.where(mask, a, 0.0)) for a in mats]
        xss = [split(x) for x in xs]
        xc = [split(dot3(x, c)) for x, c in zip(xss, cs)]
        xs = [x - dot3(t, s) for x, t, s in zip(xs, xc, xss)]
    return xs


def kernel(
    x_ref, w_ref, gate_ref, hp_ref, len_ref, dcore_ref,
    core_ref, dmix_ref, dgate_ref, dconv_ref, dhead_ref,
    xs, ys, qs, ks, links, lks, gt, gts, d_s, dkk_s, p_s, x_s, uv_s, wq_s, w2_s, r0_s, ol_s,
    snd, rcv, s_snd, g_snd, s_rcv, g_rcv, h_snd, h_rcv, e_snd, e_rcv, dgo, u_s, dos_s, dp_s, red, r1, r2, r3,
    snd_sem, rcv_sem, s_ssem, s_rsem, g_ssem, g_rsem, h_sem, e_sem,
    r1_ssem, r1_rsem, r2_ssem, r2_rsem, r3_ssem, r3_rsem,
):
    me = lax.axis_index("ctx")
    mine = lax.axis_index("dp")
    first_pos = me * ROWS

    barrier = pltpu.get_barrier_semaphore()

    def greet(i, _):
        pl.semaphore_signal(
            barrier, inc=1, device_id={"ctx": lax.rem(me + i, BLOCKS)}, device_id_type=MESH
        )
        return 0

    lax.fori_loop(1, BLOCKS, greet, 0)

    def greet_dp(i, _):
        pl.semaphore_signal(
            barrier, inc=1, device_id={"dp": lax.rem(mine + i, DP)}, device_id_type=MESH
        )
        return 0

    lax.fori_loop(1, DP, greet_dp, 0)

    xs[pl.ds(8, ROWS), :] = x_ref[...].astype(F32)
    tail = [
        xs[pl.ds(133 + r, 1), pl.ds(1024 * p, 1024)] for r in range(3) for p in range(4)
    ] + [jnp.zeros((4, 1024), F32)]
    h_snd[...] = jnp.concatenate(tail, axis=0).astype(BF)

    pl.semaphore_wait(barrier, BLOCKS + DP - 2)

    def halo_copy():
        return pltpu.make_async_remote_copy(
            src_ref=h_snd, dst_ref=h_rcv, send_sem=h_sem.at[0], recv_sem=h_sem.at[1],
            device_id={"ctx": lax.rem(me + 1, BLOCKS)}, device_id_type=MESH,
        )

    halo_copy().start()

    row, col = iota((ROWS, D), 0), iota((ROWS, D), 1)
    low = row >= col
    strict = row > col
    ends = []
    total = 0
    for i in range(8):
        total = total + len_ref[0, i]
        ends.append(total)

    def doc_of(pos):
        found = jnp.zeros(pos.shape, jnp.int32)
        for e in ends:
            found = found + jnp.where(e <= pos, 1, 0)
        return found

    doc_col = doc_of(first_pos + row)
    doc_row = doc_of(first_pos + col)
    lks[...] = jnp.where((doc_col == doc_row) & low, 1.0, 0.0)
    for j in range(3):
        links[j] = jnp.where(doc_of(first_pos + row - 3 + j) == doc_col, 1.0, 0.0)
    doc_row16 = doc_row[:HEADS]
    doc_before = doc_of(jnp.full((HEADS, D), first_pos - 1, jnp.int32))
    doc_last = doc_of(jnp.full((HEADS, D), first_pos + ROWS - 1, jnp.int32))

    eye16 = (iota((16, 16), 0) == iota((16, 16), 1)).astype(F32)
    gates = gate_ref[...]
    params = dot_full(eye16, hp_ref[...], 1, 1)
    scale = -jnp.exp(params[:, 0:1])
    z = gates[:HEADS] + params[:, 1:2]
    decay = scale * (jnp.maximum(z, 0.0) + jnp.log1p(jnp.exp(-jnp.abs(z))))
    ez = scale / (1.0 + jnp.exp(-z))
    beta = 1.0 / (1.0 + jnp.exp(-gates[HEADS:]))
    upto = jnp.where(row <= col, 1.0, 0.0)
    summed = dot_full(decay, upto)
    carried = jnp.exp(summed) * (doc_row16 == doc_before).astype(F32)
    to_end = jnp.exp(jnp.minimum(summed[:, D - 1 : D] - summed, 0.0)) * (
        doc_row16 == doc_last
    ).astype(F32)
    for n in range(HEADS // HG):
        part = slice(n * HG, n * HG + HG)
        gts[0, n] = decay[part]
        gts[1, n] = ez[part]
        gts[2, n] = beta[part]
    rows8 = jnp.stack(
        [summed, beta, carried, to_end, beta * carried, summed, summed, summed], axis=1
    )
    gt[...] = rows8

    halo_copy().wait()
    inside = jnp.where(me > 0, 1.0, 0.0)
    hv = h_rcv[...].astype(F32) * inside
    for r in range(3):
        for p in range(4):
            xs[pl.ds(5 + r, 1), pl.ds(1024 * p, 1024)] = hv[4 * r + p : 4 * r + p + 1]

    def lanes(block):
        return pl.ds(pl.multiple_of(block * D, D), D)

    def taps(j, block):
        t = xs[pl.ds(5 + j, ROWS), lanes(block)]
        return t if j == 3 else t * links[j]

    def conv(block):
        y = taps(3, block) * w_ref[3:4, lanes(block)]
        for j in range(3):
            y = y + taps(j, block) * w_ref[j : j + 1, lanes(block)]
        ys[:, lanes(block)] = y
        return y / (1.0 + jnp.exp(-y))

    def columns(h):
        t = jnp.transpose(gt[h])
        return [t[:, i : i + 1] for i in range(5)]

    def a_last(h):
        return gt[h][2:3, D - 1 : D]

    def pack_copy(h, source):
        return pltpu.make_async_remote_copy(
            src_ref=snd.at[h], dst_ref=rcv.at[source], send_sem=snd_sem.at[h],
            recv_sem=rcv_sem.at[source], device_id={"ctx": h}, device_id_type=MESH,
        )

    def forward(step, _):
        group = lax.rem(step + me, HEADS // FG)
        nq = FG // 2
        qk = [group * nq + i for i in range(nq)]
        heads = [group * FG + i for i in range(FG)]
        kk, qq, kf, qf = [], [], [], []
        for j in qk:
            m = conv(j)
            q = m * (lax.rsqrt(jnp.sum(m * m, axis=1, keepdims=True) + 1e-6) * D**-0.5)
            m = conv(QK + j)
            k = m * lax.rsqrt(jnp.sum(m * m, axis=1, keepdims=True) + 1e-6)
            qs[j] = q
            ks[j] = k
            k2, q2 = split(k), split(q)
            kk.append(dot3(k2, k2, 1, 1))
            qq.append(dot3(q2, k2, 1, 1))
            kf.append(k)
            qf.append(q)
        vs = [conv(2 * QK + h) for h in heads]
        cols = [columns(h) for h in heads]
        lk = lks[...]
        mats, ps = [], []
        for i, h in enumerate(heads):
            spans = lk * jnp.exp(jnp.minimum(cols[i][0] - gt[h][0:1], 0.0))
            dkk = jnp.where(strict, spans * kk[i // 2], 0.0)
            p = spans * qq[i // 2]
            d_s[h] = spans
            dkk_s[h] = dkk
            p_s[h] = p
            ps.append(p.astype(BF))
            mats.append(cols[i][1] * dkk)
        xinv = inverses(mats)
        for i, h in enumerate(heads):
            x_s[h] = xinv[i]
            right = jnp.concatenate([cols[i][1] * vs[i], cols[i][4] * kf[i // 2]], axis=1)
            uvw = dot3(split(xinv[i]), split(right))
            uvwb = uvw.astype(BF)
            uv_s[h] = uvw[:, :D]
            wq_s[h, 0:ROWS] = uvwb[:, D:]
            pw = dot(ps[i], uvwb)
            ol_s[h] = pw[:, :D]
            qc = (cols[i][2] * qf[i // 2] - pw[:, D:]).astype(BF)
            wq_s[h, ROWS : 2 * ROWS] = qc
            dk = (cols[i][3] * kf[i // 2]).astype(BF)
            nb = dot(uvwb, dk, 0, 0)
            gl = dot(dcore_ref[:, lanes(h)], qc, 0, 0)
            snd[h, 0:D] = nb[D:].astype(BF)
            snd[h, D : 2 * D] = nb[:D].astype(BF)
            snd[h, 2 * D : 3 * D] = gl.astype(BF)
            al = jnp.broadcast_to(a_last(h), (16, D))
            t0 = al.astype(BF).astype(F32)
            t1 = (al - t0).astype(BF).astype(F32)
            t2 = al - t0 - t1
            r16 = iota((16, D), 0)
            snd[h, 3 * D : PACK] = jnp.where(
                r16 == 0, t0, jnp.where(r16 == 1, t1, jnp.where(r16 == 2, t2, 0.0))
            ).astype(BF)
        for h in heads:
            @pl.when(h != me)
            def _():
                pack_copy(h, me).start()
        return 0

    lax.fori_loop(0, HEADS // FG, forward, 0)
    rcv[me] = snd[me]

    def aside(step, _):
        heads = [step * HG + i for i in range(HG)]
        for i, h in enumerate(heads):
            cols = columns(h)
            zz = dot(p_s[h].astype(BF), dcore_ref[:, lanes(h)], 0, 0)
            dk = cols[3] * ks[h // 2]
            out = dot3(split(x_s[h]), split(jnp.concatenate([zz, dk], axis=1)), 0, 0)
            r0_s[h] = out[:, :D]
            w2_s[h] = out[:, D:].astype(BF)
        return 0

    lax.fori_loop(0, ASIDE, aside, 0)

    def wait_pack(i, _):
        pack_copy(lax.rem(me + i, BLOCKS), lax.rem(me + i, BLOCKS)).wait_recv()
        return 0

    lax.fori_loop(1, BLOCKS, wait_pack, 0)

    def s_copy(block, head):
        return pltpu.make_async_remote_copy(
            src_ref=s_snd.at[block], dst_ref=s_rcv.at[head], send_sem=s_ssem.at[block],
            recv_sem=s_rsem.at[head], device_id={"ctx": block}, device_id_type=MESH,
        )

    def g_copy(block, head):
        return pltpu.make_async_remote_copy(
            src_ref=g_snd.at[block], dst_ref=g_rcv.at[head], send_sem=g_ssem.at[block],
            recv_sem=g_rsem.at[head], device_id={"ctx": block}, device_id_type=MESH,
        )

    def send_state(block, state):
        s_snd[block] = state

        @pl.when(block != me)
        def _():
            s_copy(block, me).start()

    zero = jnp.zeros((D, D), F32)
    send_state(0, zero.astype(BF))
    g_snd[BLOCKS - 1] = zero.astype(BF)

    def scalar_of(block):
        t = rcv[block, 3 * D : PACK].astype(F32)
        return t[0:1] + t[1:2] + t[2:3]

    def turn(i, carry):
        state, grad = carry
        b = BLOCKS - 1 - i
        state = (
            scalar_of(i) * state
            - dot(state.astype(BF), rcv[i, 0:D])
            + rcv[i, D : 2 * D].astype(F32)
        )
        grad = (
            scalar_of(b) * grad
            - dot(grad.astype(BF), rcv[b, 0:D], 1, 1)
            + rcv[b, 2 * D : 3 * D].astype(F32)
        )
        send_state(i + 1, state.astype(BF))
        g_snd[b - 1] = grad.astype(BF)
        return state, grad

    lax.fori_loop(0, BLOCKS - 1, turn, (zero, zero))

    def send_grad(i, _):
        other = lax.rem(me + i, BLOCKS)
        g_copy(other, me).start()
        return 0

    lax.fori_loop(1, BLOCKS, send_grad, 0)
    s_rcv[me] = s_snd[me]
    g_rcv[me] = g_snd[me]
    lax.fori_loop(ASIDE, HEADS // HG, aside, 0)

    lane = col
    row8 = row[:8]

    def conv_back(block, piece, half, dm):
        at = pl.ds(half * D, D)
        y = ys[:, lanes(block)]
        sig = 1.0 / (1.0 + jnp.exp(-y))
        dy = dm * (sig * (1.0 + y * (1.0 - sig)))
        red[piece, 3:4, at] = jnp.sum(dy * taps(3, block), axis=0, keepdims=True)
        own = dy * w_ref[3:4, lanes(block)]
        spill = jnp.zeros((8, D), F32)
        for j in range(3):
            ej = dy * links[j]
            red[piece, j : j + 1, at] = jnp.sum(
                ej * xs[pl.ds(5 + j, ROWS), lanes(block)], axis=0, keepdims=True
            )
            turned = pltpu.roll(ej * w_ref[j : j + 1, lanes(block)], ROWS - 3 + j, 0)
            wrapped = row >= ROWS - 3 + j
            own = own + jnp.where(wrapped, 0.0, turned)
            spill = spill + jnp.where(row8 >= 5 + j, turned[ROWS - 8 :], 0.0)
        dmix_ref[:, lanes(block)] = own.astype(BF)
        e_snd[0:8, lanes(block)] = own[ROWS - 8 :]
        e_snd[8:16, lanes(block)] = spill

    def group_of(step):
        group = lax.rem(step + me, HEADS // HG)
        return group, [group * HG + i for i in range(HG)]

    def from_state(step, _):
        _, heads = group_of(step)
        for h in heads:
            @pl.when(h != me)
            def _():
                s_copy(h, h).wait_recv()
        for h in heads:
            s = s_rcv[h]
            do = dcore_ref[:, lanes(h)]
            t = dot(wq_s[h], s, 1, 1)
            u = (uv_s[h] - t[:ROWS]).astype(BF)
            core_ref[:, lanes(h)] = (ol_s[h] + t[ROWS:]).astype(BF)
            u_s[h] = u
            dos_s[h] = dot(do, s)
            dp_s[h] = dot(do, u, 1, 1)
        return 0

    lax.fori_loop(0, HEADS // HG, from_state, 0)

    suffix = jnp.where(row >= col, 1.0, 0.0)
    red[:, 4:8, :] = jnp.zeros((BLOCKS, 4, PIECE), F32)

    def red_copy(piece, source):
        return pltpu.make_async_remote_copy(
            src_ref=red.at[piece], dst_ref=r1.at[source], send_sem=r1_ssem.at[piece],
            recv_sem=r1_rsem.at[source], device_id={"ctx": piece}, device_id_type=MESH,
        )

    def backward(step, _):
        group, heads = group_of(step)
        nq = HG // 2
        qk = [group * nq + i for i in range(nq)]
        q_piece = group * (nq // 2)
        k_piece = BLOCKS // 4 + group * (nq // 2)
        v_piece = BLOCKS // 2 + group * (HG // 2)
        for h in heads:
            @pl.when(h != me)
            def _():
                g_copy(h, h).wait_recv()
        packed = jnp.zeros((ROWS, D), F32)
        colsums, lasts = [], []
        for n, j in enumerate(qk):
            k, q = ks[j], qs[j]
            bs = es = dq = dk = None
            for i in (2 * n, 2 * n + 1):
                h = heads[i]
                _, bet, car, end, bcar = columns(h)
                s, g, u = s_rcv[h], g_rcv[h], u_s[h]
                dos, dp = dos_s[h], dp_s[h]
                r = r0_s[h] + dot(w2_s[h], g, 1, 1)
                rb = r.astype(BF)
                rs = dot(rb, s)
                da = -dot(rb, u, 1, 1)
                ug = dot(u, g)
                spans = d_s[h]
                t1 = da * dkk_s[h]
                f = dp * p_s[h] + bet * t1
                yv = ys[:, lanes(2 * QK + h)]
                v = yv / (1.0 + jnp.exp(-yv))
                krs = car * k * rs
                dkug = end * k * ug
                dbeta = jnp.sum(r * v - krs + t1, axis=1, keepdims=True)
                dc = jnp.sum(f + car * q * dos - bet * krs - dkug, axis=1, keepdims=True)
                packed = packed + jnp.where(lane == i, dc, 0.0)
                packed = packed + jnp.where(lane == HG + i, dbeta, 0.0)
                colsums.append(jnp.sum(f, axis=0, keepdims=True))
                lasts.append(
                    jnp.sum(
                        jnp.sum(dkug, axis=0, keepdims=True)
                        + a_last(h)
                        * jnp.sum(g.astype(F32) * s.astype(F32), axis=0, keepdims=True),
                        axis=1, keepdims=True,
                    )
                )
                bq = dp * spans
                e = jnp.where(strict, bet * da * spans, 0.0)
                dqi = car * dos
                dki = end * ug - bcar * rs
                bs = bq if bs is None else bs + bq
                es = e if es is None else es + e
                dq = dqi if dq is None else dq + dqi
                dk = dki if dk is None else dk + dki
                conv_back(2 * QK + h, v_piece + i // 2, i % 2, bet * r)
            be = jnp.concatenate([bs, es], axis=0).astype(BF)
            kb = k.astype(BF)
            t4 = dot(be, kb)
            t5 = dot(be, jnp.concatenate([q.astype(BF), kb], axis=0), 0, 0)
            dq = dq + t4[:ROWS]
            dk = dk + t4[ROWS:] + t5
            y = ys[:, lanes(j)]
            m = y / (1.0 + jnp.exp(-y))
            rq = lax.rsqrt(jnp.sum(m * m, axis=1, keepdims=True) + 1e-6)
            dm = rq * (D**-0.5) * (dq - m * (rq * rq * jnp.sum(m * dq, axis=1, keepdims=True)))
            conv_back(j, q_piece + n // 2, n % 2, dm)
            y = ys[:, lanes(QK + j)]
            m = y / (1.0 + jnp.exp(-y))
            rk = lax.rsqrt(jnp.sum(m * m, axis=1, keepdims=True) + 1e-6)
            dm = rk * (dk - m * (rk * rk * jnp.sum(m * dk, axis=1, keepdims=True)))
            conv_back(QK + j, k_piece + n // 2, n % 2, dm)
        rows = jnp.transpose(packed)
        lasts = jnp.concatenate(lasts, axis=0)
        dc = rows[:HG] - jnp.concatenate(colsums, axis=0)
        dc = dc + jnp.where(lane[:HG] == D - 1, lasts, 0.0)
        dg = dot_full(dc, suffix)
        dz = dg * gts[1, group]
        bet = gts[2, group]
        dgo[0, group] = dz
        dgo[1, group] = rows[HG : 2 * HG] * bet * (1.0 - bet)
        sums = dot_full(jnp.ones((8, D), F32), jnp.concatenate([dg * gts[0, group], dz], axis=0), 1, 1)
        red[q_piece, 4:5, 0 : 2 * HG] = sums[0:1]
        pieces = (
            [q_piece + i for i in range(nq // 2)]
            + [k_piece + i for i in range(nq // 2)]
            + [v_piece + i for i in range(HG // 2)]
        )
        for piece in pieces:
            @pl.when(piece != me)
            def _():
                red_copy(piece, me).start()

            @pl.when(piece == me)
            def _():
                r1[me] = red[piece]
        return 0

    lax.fori_loop(0, HEADS // HG, backward, 0)

    spill = e_snd[8:16, :]
    h_snd[...] = jnp.concatenate(
        [spill[5 + r : 6 + r, 1024 * p : 1024 * p + 1024] for r in range(3) for p in range(4)]
        + [jnp.zeros((4, 1024), F32)],
        axis=0,
    ).astype(BF)
    back = pltpu.make_async_remote_copy(
        src_ref=h_snd, dst_ref=e_rcv, send_sem=e_sem.at[0], recv_sem=e_sem.at[1],
        device_id={"ctx": lax.rem(me + BLOCKS - 1, BLOCKS)}, device_id_type=MESH,
    )
    back.start()

    def wait_red(i, _):
        other = lax.rem(me + i, BLOCKS)
        red_copy(other, other).wait_recv()
        return 0

    lax.fori_loop(1, BLOCKS, wait_red, 0)
    total = r1[0]
    for i in range(1, BLOCKS):
        total = total + r1[i]
    r2[mine] = total

    def dp_copy(other, source):
        return pltpu.make_async_remote_copy(
            src_ref=r2.at[source], dst_ref=r2.at[source], send_sem=r2_ssem.at[other],
            recv_sem=r2_rsem.at[source], device_id={"dp": other}, device_id_type=MESH,
        )

    def send_dp(i, _):
        dp_copy(lax.rem(mine + i, DP), mine).start()
        return 0

    lax.fori_loop(1, DP, send_dp, 0)

    for n in range(HEADS // HG):
        part = slice(n * HG, n * HG + HG)
        dgate_ref[part, :] = dgo[0, n]
        dgate_ref[HEADS + n * HG : HEADS + n * HG + HG, :] = dgo[1, n]

    def wait_dp(i, _):
        other = lax.rem(mine + i, DP)
        dp_copy(other, other).wait_recv()
        return 0

    lax.fori_loop(1, DP, wait_dp, 0)
    total = r2[0]
    for i in range(1, DP):
        total = total + r2[i]
    r3[me] = total

    def all_copy(other, source):
        return pltpu.make_async_remote_copy(
            src_ref=r3.at[source], dst_ref=r3.at[source], send_sem=r3_ssem.at[other],
            recv_sem=r3_rsem.at[source], device_id={"ctx": other}, device_id_type=MESH,
        )

    def send_all(i, _):
        all_copy(lax.rem(me + i, BLOCKS), me).start()
        return 0

    lax.fori_loop(1, BLOCKS, send_all, 0)

    back.wait()
    before_last = jnp.where(me < BLOCKS - 1, 1.0, 0.0)
    ev = e_rcv[...].astype(F32) * before_last
    for p in range(4):
        pieces = [jnp.zeros((5, 1024), F32)] + [ev[4 * r + p : 4 * r + p + 1] for r in range(3)]
        part = e_snd[0:8, 1024 * p : 1024 * p + 1024] + jnp.concatenate(pieces, axis=0)
        old = dmix_ref[ROWS - 16 :, 1024 * p : 1024 * p + 1024].astype(F32)
        dmix_ref[ROWS - 16 :, 1024 * p : 1024 * p + 1024] = jnp.concatenate(
            [old[:8], part], axis=0
        ).astype(BF)

    def wait_all(i, _):
        other = lax.rem(me + i, BLOCKS)
        all_copy(other, other).wait_recv()
        return 0

    lax.fori_loop(1, BLOCKS, wait_all, 0)
    for p in range(BLOCKS):
        dconv_ref[:, p * PIECE : (p + 1) * PIECE] = r3[p, 0:4]
    for n in range(HEADS // HG):
        part = slice(n * HG, n * HG + HG)
        sums = r3[n * (HG // 4), 4:5]
        dhead_ref[0:1, part] = sums[:, 0:HG]
        dhead_ref[1:2, part] = sums[:, HG : 2 * HG]

    def drain(i, _):
        other = lax.rem(me + i, BLOCKS)
        pack_copy(other, me).wait_send()
        s_copy(other, me).wait_send()
        g_copy(other, me).wait_send()
        red_copy(other, me).wait_send()
        all_copy(other, me).wait_send()
        return 0

    lax.fori_loop(1, BLOCKS, drain, 0)

    def drain_dp(i, _):
        dp_copy(lax.rem(mine + i, DP), mine).wait_send()
        return 0

    lax.fori_loop(1, DP, drain_dp, 0)


def on_device(mixed_in, conv_weight, gate_in, head_params, doc_lengths, d_core):
    vmem = pl.BlockSpec(memory_space=pltpu.VMEM)
    mat = (HEADS, D, D)
    scratch = [
        pltpu.VMEM((ROWS + 8, CH), F32),
        pltpu.VMEM((ROWS, CH), F32),
        pltpu.VMEM((QK, D, D), F32),
        pltpu.VMEM((QK, D, D), F32),
        pltpu.VMEM((3, ROWS, D), F32),
        pltpu.VMEM((ROWS, D), F32),
        pltpu.VMEM((HEADS, 8, D), F32),
        pltpu.VMEM((3, HEADS // HG, HG, D), F32),
        pltpu.VMEM(mat, F32),
        pltpu.VMEM(mat, F32),
        pltpu.VMEM(mat, F32),
        pltpu.VMEM(mat, F32),
        pltpu.VMEM(mat, F32),
        pltpu.VMEM((HEADS, 2 * D, D), BF),
        pltpu.VMEM(mat, BF),
        pltpu.VMEM(mat, F32),
        pltpu.VMEM(mat, F32),
        pltpu.VMEM((HEADS, PACK, D), BF),
        pltpu.VMEM((HEADS, PACK, D), BF),
        pltpu.VMEM(mat, BF),
        pltpu.VMEM(mat, BF),
        pltpu.VMEM(mat, BF),
        pltpu.VMEM(mat, BF),
        pltpu.VMEM((16, 1024), BF),
        pltpu.VMEM((16, 1024), BF),
        pltpu.VMEM((16, CH), F32),
        pltpu.VMEM((16, 1024), BF),
        pltpu.VMEM((2, HEADS // HG, HG, D), F32),
        pltpu.VMEM(mat, BF),
        pltpu.VMEM(mat, F32),
        pltpu.VMEM(mat, F32),
        pltpu.VMEM((BLOCKS, 8, PIECE), F32),
        pltpu.VMEM((BLOCKS, 8, PIECE), F32),
        pltpu.VMEM((DP, 8, PIECE), F32),
        pltpu.VMEM((BLOCKS, 8, PIECE), F32),
        pltpu.SemaphoreType.DMA((BLOCKS,)),
        pltpu.SemaphoreType.DMA((BLOCKS,)),
        pltpu.SemaphoreType.DMA((BLOCKS,)),
        pltpu.SemaphoreType.DMA((BLOCKS,)),
        pltpu.SemaphoreType.DMA((BLOCKS,)),
        pltpu.SemaphoreType.DMA((BLOCKS,)),
        pltpu.SemaphoreType.DMA((2,)),
        pltpu.SemaphoreType.DMA((2,)),
        pltpu.SemaphoreType.DMA((BLOCKS,)),
        pltpu.SemaphoreType.DMA((BLOCKS,)),
        pltpu.SemaphoreType.DMA((DP,)),
        pltpu.SemaphoreType.DMA((DP,)),
        pltpu.SemaphoreType.DMA((BLOCKS,)),
        pltpu.SemaphoreType.DMA((BLOCKS,)),
    ]
    core, dmix, dgate, dconv, dhead = pl.pallas_call(
        kernel,
        out_shape=(
            jax.ShapeDtypeStruct((ROWS, HEADS * D), BF),
            jax.ShapeDtypeStruct((ROWS, CH), BF),
            jax.ShapeDtypeStruct((2 * HEADS, ROWS), F32),
            jax.ShapeDtypeStruct((4, CH), F32),
            jax.ShapeDtypeStruct((2, HEADS), F32),
        ),
        in_specs=[vmem, vmem, vmem, vmem, pl.BlockSpec(memory_space=pltpu.SMEM), vmem],
        out_specs=(vmem,) * 5,
        scratch_shapes=scratch,
        compiler_params=pltpu.CompilerParams(
            collective_id=0, has_side_effects=True, vmem_limit_bytes=56 * 1024 * 1024
        ),
        name="delta_mix",
    )(mixed_in[0], conv_weight, gate_in[0].T, head_params, doc_lengths, d_core[0])
    return core[None], dmix[None], dgate.T[None], dconv, dhead


def solution(mesh):
    return jax.shard_map(
        on_device,
        mesh=mesh,
        in_specs=(
            P("dp", "ctx", None),
            P(),
            P("dp", "ctx", None),
            P(),
            P("dp", None),
            P("dp", "ctx", None),
        ),
        out_specs=(P("dp", "ctx", None), P("dp", "ctx", None), P("dp", "ctx", None), P(), P()),
        check_vma=False,
    )
```

```python
import jax
import jax.numpy as jnp
from jax import lax
from jax.experimental import pallas as pl
from jax.experimental.pallas import tpu as pltpu
from jax.sharding import PartitionSpec as P

HEADS = 16
QK = 8
D = 128
ROWS = 128
CH = 4096
BLOCKS = 16
PACK = 3 * D + 16
HG = 4
GROUPS = HEADS // HG
DP = 8
PIECE = CH // BLOCKS
F32 = jnp.float32
BF = jnp.bfloat16
MESH = pl.DeviceIdType.MESH
HIGHEST = lax.Precision.HIGHEST


def dot(a, b, ca=1, cb=0):
    return lax.dot_general(a, b, (((ca,), (cb,)), ((), ())), preferred_element_type=F32)


def dot_full(a, b, ca=1, cb=0):
    return lax.dot_general(
        a, b, (((ca,), (cb,)), ((), ())), preferred_element_type=F32, precision=HIGHEST
    )


def split(a):
    high = a.astype(BF)
    return high, (a - high.astype(F32)).astype(BF)


def dot3(a, b, ca=1, cb=0):
    left = jnp.concatenate(a, axis=ca)
    wide = jnp.concatenate(b, axis=1 - cb)
    n = b[0].shape[1 - cb]
    t = dot(left, jnp.concatenate([wide, wide], axis=cb), ca, cb)
    return t[:, :n] + t[:, n:]


def iota(shape, dim):
    return lax.broadcasted_iota(jnp.int32, shape, dim)


def inverses(mats):
    row, col = iota((D, D), 0), iota((D, D), 1)
    eye = (row == col).astype(F32)

    def same(bits):
        return (row >> bits) == (col >> bits)

    near = same(3)
    a8 = [jnp.where(near, a, 0.0) for a in mats]
    a8s = [split(a) for a in a8]
    a2 = [dot3(s, s) for s in a8s]
    a2s = [split(a) for a in a2]
    a3 = [dot3(s, t) for s, t in zip(a8s, a2s)]
    a4s = [split(dot3(s, s)) for s in a2s]
    ys = [eye - a + b - c for a, b, c in zip(a8, a2, a3)]
    xs = [y + dot3(split(y), s) for y, s in zip(ys, a4s)]
    for bits in range(3, 7):
        mask = same(bits + 1) & jnp.logical_not(same(bits))
        cs = [split(jnp.where(mask, a, 0.0)) for a in mats]
        xss = [split(x) for x in xs]
        xc = [split(dot3(x, c)) for x, c in zip(xss, cs)]
        xs = [x - dot3(t, s) for x, t, s in zip(xs, xc, xss)]
    return xs


def parts_of(group):
    first, second = 4 * group, 4 * ((group + 2) % 4) + 2
    return [(0, first, first + 2), (2, second, second + 2)]


def kernel(
    x_ref, w_ref, gate_ref, hp_ref, len_ref, dcore_ref,
    core_ref, dmix_ref, dgate_ref, dconv_ref, dhead_ref,
    xs, slope, qs, ks, norms, links, lks, gt, gts, d_s, dkk_s, p_s, x_s, uv_s, wq_s, w2_s, r0_s, ol_s,
    snd, rcv, s_snd, g_snd, s_rcv, g_rcv, h_snd, h_rcv, e_add, e_rcv, dgo, u_s, a_s, v_s, b_s, e_s, ck_s, bck_s, bc_s, ek_s, end_s, dk_s, dcs, red, r1, r2, r3,
    snd_sem, rcv_sem, s_ssem, s_rsem, g_ssem, g_rsem, h_sem, e_sem,
    r1_ssem, r1_rsem, r2_ssem, r2_rsem, r3_ssem, r3_rsem,
):
    me = lax.axis_index("ctx")
    mine = lax.axis_index("dp")
    first_pos = me * ROWS

    own_row = lax.div(me, 4)
    own_pair = lax.rem(lax.div(me, 2), 2)

    def group_of(step):
        group = lax.rem(own_row + step + 2 * own_pair, 4)
        qk = [2 * group, 2 * lax.rem(group + 2, 4) + 1]
        return group, qk, [2 * j + i for j in qk for i in range(2)]

    barrier = pltpu.get_barrier_semaphore()

    def greet(i, _):
        pl.semaphore_signal(
            barrier, inc=1, device_id={"ctx": lax.rem(me + i, BLOCKS)}, device_id_type=MESH
        )
        return 0

    lax.fori_loop(1, BLOCKS, greet, 0, unroll=True)

    def greet_dp(i, _):
        pl.semaphore_signal(
            barrier, inc=1, device_id={"dp": lax.rem(mine + i, DP)}, device_id_type=MESH
        )
        return 0

    lax.fori_loop(1, DP, greet_dp, 0, unroll=True)

    xs[pl.ds(8, ROWS), :] = x_ref[...].astype(F32)
    tail = [
        xs[pl.ds(133 + r, 1), pl.ds(1024 * p, 1024)] for r in range(3) for p in range(4)
    ] + [jnp.zeros((4, 1024), F32)]
    h_snd[...] = jnp.concatenate(tail, axis=0).astype(BF)

    pl.semaphore_wait(barrier, BLOCKS + DP - 2)

    def halo_copy():
        return pltpu.make_async_remote_copy(
            src_ref=h_snd, dst_ref=h_rcv, send_sem=h_sem.at[0], recv_sem=h_sem.at[1],
            device_id={"ctx": lax.rem(me + 1, BLOCKS)}, device_id_type=MESH,
        )

    halo_copy().start()

    row, col = iota((ROWS, D), 0), iota((ROWS, D), 1)
    low = row >= col
    strict = row > col
    ends = []
    total = 0
    for i in range(8):
        total = total + len_ref[0, i]
        ends.append(total)

    def doc_of(pos):
        found = jnp.zeros(pos.shape, jnp.int32)
        for e in ends:
            found = found + jnp.where(e <= pos, 1, 0)
        return found

    doc_col = doc_of(first_pos + row)
    doc_row = doc_of(first_pos + col)
    lks[...] = jnp.where((doc_col == doc_row) & low, 1.0, 0.0)
    for j in range(3):
        links[j] = jnp.where(doc_of(first_pos + row - 3 + j) == doc_col, 1.0, 0.0)
    doc_row16 = doc_row[:HEADS]
    doc_before = doc_of(jnp.full((HEADS, D), first_pos - 1, jnp.int32))
    doc_last = doc_of(jnp.full((HEADS, D), first_pos + ROWS - 1, jnp.int32))

    eye16 = (iota((16, 16), 0) == iota((16, 16), 1)).astype(F32)
    gates = gate_ref[...]
    params = dot_full(eye16, hp_ref[...], 1, 1)
    scale = -jnp.exp(params[:, 0:1])
    z = gates[:HEADS] + params[:, 1:2]
    decay = scale * (jnp.maximum(z, 0.0) + jnp.log1p(jnp.exp(-jnp.abs(z))))
    ez = scale / (1.0 + jnp.exp(-z))
    beta = 1.0 / (1.0 + jnp.exp(-gates[HEADS:]))
    upto = jnp.where(row <= col, 1.0, 0.0)
    summed = dot_full(decay, upto)
    carried = jnp.exp(summed) * (doc_row16 == doc_before).astype(F32)
    to_end = jnp.exp(jnp.minimum(summed[:, D - 1 : D] - summed, 0.0)) * (
        doc_row16 == doc_last
    ).astype(F32)
    for n in range(GROUPS):
        for at, a, b in parts_of(n):
            gts[0, n, at : at + 2] = decay[a:b]
            gts[1, n, at : at + 2] = ez[a:b]
            gts[2, n, at : at + 2] = beta[a:b]
    rows8 = jnp.stack(
        [summed, beta, carried, to_end, beta * carried, summed, summed, summed], axis=1
    )
    gt[...] = rows8

    halo_copy().wait()
    inside = jnp.where(me > 0, 1.0, 0.0)
    hv = h_rcv[...].astype(F32) * inside
    for r in range(3):
        for p in range(4):
            xs[pl.ds(5 + r, 1), pl.ds(1024 * p, 1024)] = hv[4 * r + p : 4 * r + p + 1]

    def lanes(block):
        return pl.ds(pl.multiple_of(block * D, D), D)

    def taps(j, block):
        t = xs[pl.ds(5 + j, ROWS), lanes(block)]
        return t if j == 3 else t * links[j]

    def conv(block):
        y = taps(3, block) * w_ref[3:4, lanes(block)]
        for j in range(3):
            y = y + taps(j, block) * w_ref[j : j + 1, lanes(block)]
        sig = 1.0 / (1.0 + jnp.exp(-y))
        m = y * sig
        slope[:, lanes(block)] = sig + m * (1.0 - sig)
        return m

    def columns(h):
        t = jnp.transpose(gt[h])
        return [t[:, i : i + 1] for i in range(5)]

    def a_last(h):
        return gt[h][2:3, D - 1 : D]

    def pack_copy(h, source):
        return pltpu.make_async_remote_copy(
            src_ref=snd.at[h], dst_ref=rcv.at[source], send_sem=snd_sem.at[h],
            recv_sem=rcv_sem.at[source], device_id={"ctx": h}, device_id_type=MESH,
        )

    def forward(step, _):
        _, qk, heads = group_of(step)
        kk, qq, kf, qf = [], [], [], []
        for j in qk:
            m = conv(j)
            norm = lax.rsqrt(jnp.sum(m * m, axis=1, keepdims=True) + 1e-6) * D**-0.5
            norms[j] = jnp.broadcast_to(norm, (ROWS, D))
            q = m * norm
            m = conv(QK + j)
            norm = lax.rsqrt(jnp.sum(m * m, axis=1, keepdims=True) + 1e-6)
            norms[QK + j] = jnp.broadcast_to(norm, (ROWS, D))
            k = m * norm
            qs[j] = q
            ks[j] = k
            k2, q2 = split(k), split(q)
            kk.append(dot3(k2, k2, 1, 1))
            qq.append(dot3(q2, k2, 1, 1))
            kf.append(k)
            qf.append(q)
        vs = [conv(2 * QK + h) for h in heads]
        cols = [columns(h) for h in heads]
        lk = lks[...]
        mats, ps = [], []
        for i, h in enumerate(heads):
            spans = lk * jnp.exp(jnp.minimum(cols[i][0] - gt[h][0:1], 0.0))
            dkk = jnp.where(strict, spans * kk[i // 2], 0.0)
            p = spans * qq[i // 2]
            mat = cols[i][1] * dkk
            d_s[h] = spans
            dkk_s[h] = dkk
            a_s[h] = mat
            p_s[h] = p
            v_s[h] = vs[i]
            ps.append(p.astype(BF))
            mats.append(mat)
        xinv = inverses(mats)
        for i, h in enumerate(heads):
            x_s[h] = xinv[i]
            right = jnp.concatenate([cols[i][1] * vs[i], cols[i][4] * kf[i // 2]], axis=1)
            uvw = dot3(split(xinv[i]), split(right))
            uvwb = uvw.astype(BF)
            uv_s[h] = uvw[:, :D]
            wq_s[h, 0:ROWS] = uvwb[:, D:]
            pw = dot(ps[i], uvwb)
            ol_s[h] = pw[:, :D]
            qc = (cols[i][2] * qf[i // 2] - pw[:, D:]).astype(BF)
            wq_s[h, ROWS : 2 * ROWS] = qc
            dk = (cols[i][3] * kf[i // 2]).astype(BF)
            nb = dot(uvwb, dk, 0, 0)
            gl = dot(dcore_ref[:, lanes(h)], qc, 0, 0)
            snd[h, 0:D] = nb[D:].astype(BF)
            snd[h, D : 2 * D] = nb[:D].astype(BF)
            snd[h, 2 * D : 3 * D] = gl.astype(BF)
            al = jnp.broadcast_to(a_last(h), (16, D))
            t0 = al.astype(BF).astype(F32)
            t1 = (al - t0).astype(BF).astype(F32)
            t2 = al - t0 - t1
            r16 = iota((16, D), 0)
            snd[h, 3 * D : PACK] = jnp.where(
                r16 == 0, t0, jnp.where(r16 == 1, t1, jnp.where(r16 == 2, t2, 0.0))
            ).astype(BF)
        for h in heads:
            @pl.when(h != me)
            def _():
                pack_copy(h, me).start()
        return 0

    lax.fori_loop(0, GROUPS, forward, 0)
    rcv[me] = snd[me]

    def aside(step, _):
        heads = [step * HG + i for i in range(HG)]
        for i, h in enumerate(heads):
            cols = columns(h)
            zz = dot(p_s[h].astype(BF), dcore_ref[:, lanes(h)], 0, 0)
            k = ks[h // 2]
            dk = cols[3] * k
            b_s[h] = jnp.broadcast_to(cols[1], (ROWS, D))
            e_s[h] = jnp.where(strict, cols[1] * d_s[h], 0.0)
            ck_s[h] = cols[2] * k
            bck_s[h] = cols[4] * k
            bc_s[h] = jnp.broadcast_to(cols[4], (ROWS, D))
            ek_s[h] = dk
            end_s[h] = jnp.broadcast_to(cols[3], (ROWS, D))
            out = dot3(split(x_s[h]), split(jnp.concatenate([zz, dk], axis=1)), 0, 0)
            r0_s[h] = out[:, :D]
            w2_s[h] = out[:, D:].astype(BF)
        return 0


    def s_copy(block, head):
        return pltpu.make_async_remote_copy(
            src_ref=s_snd.at[block], dst_ref=s_rcv.at[head], send_sem=s_ssem.at[block],
            recv_sem=s_rsem.at[head], device_id={"ctx": block}, device_id_type=MESH,
        )

    def g_copy(block, head):
        return pltpu.make_async_remote_copy(
            src_ref=g_snd.at[block], dst_ref=g_rcv.at[head], send_sem=g_ssem.at[block],
            recv_sem=g_rsem.at[head], device_id={"ctx": block}, device_id_type=MESH,
        )

    lax.fori_loop(0, GROUPS, aside, 0)

    def wait_pack(i, _):
        pack_copy(lax.rem(me + i, BLOCKS), lax.rem(me + i, BLOCKS)).wait_recv()
        return 0

    lax.fori_loop(1, BLOCKS, wait_pack, 0, unroll=True)

    zero = jnp.zeros((D, D), F32)
    s_snd[0] = zero.astype(BF)
    g_snd[BLOCKS - 1] = zero.astype(BF)

    def scalar_of(block):
        t = rcv[block, 3 * D : PACK].astype(F32)
        return t[0:1] + t[1:2] + t[2:3]

    def turn(i, carry):
        state, grad = carry
        b = BLOCKS - 1 - i
        state = (
            scalar_of(i) * state
            - dot(state.astype(BF), rcv[i, 0:D])
            + rcv[i, D : 2 * D].astype(F32)
        )
        grad = (
            scalar_of(b) * grad
            - dot(grad.astype(BF), rcv[b, 0:D], 1, 1)
            + rcv[b, 2 * D : 3 * D].astype(F32)
        )
        s_snd[i + 1] = state.astype(BF)
        g_snd[b - 1] = grad.astype(BF)
        return state, grad

    lax.fori_loop(0, BLOCKS - 1, turn, (zero, zero))

    def reader(i):
        step, which = lax.div(i, 4), lax.rem(lax.div(i, 2), 2)
        row = lax.rem(own_row + 8 - step - 2 * which, 4)
        return 4 * row + 2 * lax.rem(own_pair + which, 2) + lax.rem(i, 2)

    def send_state(i, _):
        other = reader(i)

        @pl.when(other != me)
        def _():
            s_copy(other, me).start()
        return 0

    lax.fori_loop(0, BLOCKS, send_state, 0, unroll=True)

    def send_grad(i, _):
        other = reader(i)

        @pl.when(other != me)
        def _():
            g_copy(other, me).start()
        return 0

    lax.fori_loop(0, BLOCKS, send_grad, 0, unroll=True)
    s_rcv[me] = s_snd[me]
    g_rcv[me] = g_snd[me]


    lane = col

    def conv_back(block, piece, half, dm):
        at = pl.ds(half * D, D)
        dy = dm * slope[:, lanes(block)]
        slope[:, lanes(block)] = dy
        for j in range(4):
            red[piece, j : j + 1, at] = jnp.sum(dy * taps(j, block), axis=0, keepdims=True)

    def taps_back(block):
        dy = slope[:, lanes(block)]
        own = dy * w_ref[3:4, lanes(block)]
        for j in range(3):
            turned = pltpu.roll(dy * links[j] * w_ref[j : j + 1, lanes(block)], ROWS - 3 + j, 0)
            own = own + jnp.where(row >= ROWS - 3 + j, 0.0, turned)
        last = own[ROWS - 8 :] + e_add[:, lanes(block)]
        dmix_ref[:, lanes(block)] = jnp.concatenate([own[: ROWS - 8], last], axis=0).astype(BF)

    def results(step, _):
        for i in range(HG):
            h = step * HG + i
            core_ref[:, lanes(h)] = (
                ol_s[h] + dot(wq_s[h, ROWS : 2 * ROWS], s_rcv[h], 1, 1)
            ).astype(BF)
        return 0

    suffix = jnp.where(row >= col, 1.0, 0.0)
    red[:, 4:8, :] = jnp.zeros((BLOCKS, 4, PIECE), F32)

    def red_copy(piece, source):
        return pltpu.make_async_remote_copy(
            src_ref=red.at[piece], dst_ref=r1.at[source], send_sem=r1_ssem.at[piece],
            recv_sem=r1_rsem.at[source], device_id={"ctx": piece}, device_id_type=MESH,
        )

    def send_piece(piece):
        @pl.when(piece != me)
        def _():
            red_copy(piece, me).start()

        @pl.when(piece == me)
        def _():
            r1[me] = red[piece]

    def from_state(step, _):
        group, qk, heads = group_of(step)
        for h in heads:
            @pl.when(h != me)
            def _():
                s_copy(h, h).wait_recv()
        packed = jnp.zeros((ROWS, D), F32)
        colsums = []
        for n, j in enumerate(qk):
            k, q = ks[j], qs[j]
            bs = dq = None
            for i in (2 * n, 2 * n + 1):
                h = heads[i]
                s = s_rcv[h]
                do = dcore_ref[:, lanes(h)]
                u = (uv_s[h] - dot(wq_s[h, 0:ROWS], s, 1, 1)).astype(BF)
                u_s[h] = u
                dos = columns(h)[2] * dot(do, s)
                dp = dot(do, u, 1, 1)
                f = dp * p_s[h]
                packed = packed + jnp.where(
                    lane == i, jnp.sum(f + q * dos, axis=1, keepdims=True), 0.0
                )
                colsums.append(jnp.sum(f, axis=0, keepdims=True))
                bq = dp * d_s[h]
                bs = bq if bs is None else bs + bq
                dq = dos if dq is None else dq + dos
            bs = bs.astype(BF)
            dq = dq + dot(bs, k.astype(BF))
            dk_s[j] = dot(bs, q.astype(BF), 0, 0)
            dm = norms[j] * (dq - q * (D * jnp.sum(q * dq, axis=1, keepdims=True)))
            conv_back(j, group, n, dm)
        dcs[group] = jnp.transpose(packed)[:HG] - jnp.concatenate(colsums, axis=0)
        return 0

    def backward(step, _):
        group, qk, heads = group_of(step)
        q_piece, k_piece, v_piece = group, GROUPS + group, 2 * (GROUPS + group)
        for h in heads:
            @pl.when(h != me)
            def _():
                g_copy(h, h).wait_recv()
        packed = jnp.zeros((ROWS, D), F32)
        colsums, lasts = [], []
        for n, j in enumerate(qk):
            k = ks[j]
            es, dk = None, dk_s[j]
            for i in (2 * n, 2 * n + 1):
                h = heads[i]
                s, g, u = s_rcv[h], g_rcv[h], u_s[h]
                r = r0_s[h] + dot(w2_s[h], g, 1, 1)
                rb = r.astype(BF)
                rs = dot(rb, s)
                da = -dot(rb, u, 1, 1)
                ug = dot(u, g)
                f = da * a_s[h]
                kug = ek_s[h] * ug
                dbeta = jnp.sum(r * v_s[h] - ck_s[h] * rs + da * dkk_s[h], axis=1, keepdims=True)
                dc = jnp.sum(f - bck_s[h] * rs - kug, axis=1, keepdims=True)
                packed = packed + jnp.where(lane == i, dc, 0.0)
                packed = packed + jnp.where(lane == HG + i, dbeta, 0.0)
                colsums.append(jnp.sum(f, axis=0, keepdims=True))
                lasts.append(
                    jnp.sum(
                        jnp.sum(kug, axis=0, keepdims=True)
                        + a_last(h)
                        * jnp.sum(g.astype(F32) * s.astype(F32), axis=0, keepdims=True),
                        axis=1, keepdims=True,
                    )
                )
                e = da * e_s[h]
                es = e if es is None else es + e
                dk = dk + end_s[h] * ug - bc_s[h] * rs
                conv_back(2 * QK + h, v_piece + i // 2, i % 2, b_s[h] * r)
            es = es.astype(BF)
            kb = k.astype(BF)
            dk = dk + dot(es, kb) + dot(es, kb, 0, 0)
            dm = norms[QK + j] * (dk - k * jnp.sum(k * dk, axis=1, keepdims=True))
            conv_back(QK + j, k_piece, n, dm)
        rows = jnp.transpose(packed)
        lasts = jnp.concatenate(lasts, axis=0)
        dc = rows[:HG] - jnp.concatenate(colsums, axis=0) + dcs[group]
        dc = dc + jnp.where(lane[:HG] == D - 1, lasts, 0.0)
        dg = dot_full(dc, suffix)
        dz = dg * gts[1, group]
        bet = gts[2, group]
        dgo[0, group] = dz
        dgo[1, group] = rows[HG : 2 * HG] * bet * (1.0 - bet)
        sums = dot_full(jnp.ones((8, D), F32), jnp.concatenate([dg * gts[0, group], dz], axis=0), 1, 1)
        red[q_piece, 4:5, 0 : 2 * HG] = sums[0:1]
        for piece in (q_piece, k_piece, v_piece, v_piece + 1):
            send_piece(piece)
        return 0

    lax.fori_loop(0, GROUPS, from_state, 0)
    lax.fori_loop(0, GROUPS, results, 0)
    lax.fori_loop(0, GROUPS, backward, 0)

    spill = jnp.zeros((8, CH), F32)
    row8w = iota((8, CH), 0)
    for j in range(3):
        link8 = jnp.concatenate([links[j, 0:8]] * (CH // D), axis=1)
        turned = pltpu.roll(slope[0:8, :] * link8 * w_ref[j : j + 1, :], 5 + j, 0)
        spill = spill + jnp.where(row8w >= 5 + j, turned, 0.0)
    h_snd[...] = jnp.concatenate(
        [spill[5 + r : 6 + r, 1024 * p : 1024 * p + 1024] for r in range(3) for p in range(4)]
        + [jnp.zeros((4, 1024), F32)],
        axis=0,
    ).astype(BF)
    back = pltpu.make_async_remote_copy(
        src_ref=h_snd, dst_ref=e_rcv, send_sem=e_sem.at[0], recv_sem=e_sem.at[1],
        device_id={"ctx": lax.rem(me + BLOCKS - 1, BLOCKS)}, device_id_type=MESH,
    )
    back.start()

    def wait_red(i, _):
        other = lax.rem(me + i, BLOCKS)
        red_copy(other, other).wait_recv()
        return 0

    lax.fori_loop(1, BLOCKS, wait_red, 0, unroll=True)
    total = r1[0]
    for i in range(1, BLOCKS):
        total = total + r1[i]
    r2[mine] = total

    def dp_copy(other, source):
        return pltpu.make_async_remote_copy(
            src_ref=r2.at[source], dst_ref=r2.at[source], send_sem=r2_ssem.at[other],
            recv_sem=r2_rsem.at[source], device_id={"dp": other}, device_id_type=MESH,
        )

    def send_dp(i, _):
        dp_copy(lax.rem(mine + i, DP), mine).start()
        return 0

    lax.fori_loop(1, DP, send_dp, 0, unroll=True)

    back.wait()
    before_last = jnp.where(me < BLOCKS - 1, 1.0, 0.0)
    ev = e_rcv[...].astype(F32) * before_last
    for p in range(4):
        e_add[:, 1024 * p : 1024 * p + 1024] = jnp.concatenate(
            [jnp.zeros((5, 1024), F32)] + [ev[4 * r + p : 4 * r + p + 1] for r in range(3)], axis=0
        )

    def mixed_part(step, _):
        for i in range(4):
            taps_back(4 * step + i)
        return 0

    lax.fori_loop(0, 4, mixed_part, 0)

    for n in range(GROUPS):
        for at, a, b in parts_of(n):
            dgate_ref[a:b, :] = dgo[0, n, at : at + 2]
            dgate_ref[HEADS + a : HEADS + b, :] = dgo[1, n, at : at + 2]

    def wait_dp(i, _):
        other = lax.rem(mine + i, DP)
        dp_copy(other, other).wait_recv()
        return 0

    lax.fori_loop(1, DP, wait_dp, 0, unroll=True)
    total = r2[0]
    for i in range(1, DP):
        total = total + r2[i]
    r3[me] = total

    def all_copy(other, source):
        return pltpu.make_async_remote_copy(
            src_ref=r3.at[source], dst_ref=r3.at[source], send_sem=r3_ssem.at[other],
            recv_sem=r3_rsem.at[source], device_id={"ctx": other}, device_id_type=MESH,
        )

    def send_all(i, _):
        all_copy(lax.rem(me + i, BLOCKS), me).start()
        return 0

    lax.fori_loop(1, BLOCKS, send_all, 0, unroll=True)
    lax.fori_loop(4, 8, mixed_part, 0)

    def drain(i, _):
        other = lax.rem(me + i, BLOCKS)
        pack_copy(other, me).wait_send()
        s_copy(other, me).wait_send()
        g_copy(other, me).wait_send()
        red_copy(other, me).wait_send()
        return 0

    lax.fori_loop(1, BLOCKS, drain, 0, unroll=True)

    def drain_dp(i, _):
        dp_copy(lax.rem(mine + i, DP), mine).wait_send()
        return 0

    lax.fori_loop(1, DP, drain_dp, 0, unroll=True)

    def wait_all(i, _):
        other = lax.rem(me + i, BLOCKS)
        all_copy(other, other).wait_recv()
        return 0

    lax.fori_loop(1, BLOCKS, wait_all, 0, unroll=True)
    for n in range(GROUPS):
        sums = r3[n, 4:5]
        for at, a, b in parts_of(n):
            lo = (at // 2) * D
            dconv_ref[:, a // 2 * D : a // 2 * D + D] = r3[n, 0:4, lo : lo + D]
            dconv_ref[:, (QK + a // 2) * D : (QK + a // 2 + 1) * D] = r3[GROUPS + n, 0:4, lo : lo + D]
            dconv_ref[:, (2 * QK + a) * D : (2 * QK + b) * D] = r3[2 * (GROUPS + n) + at // 2, 0:4]
            dhead_ref[0:1, a:b] = sums[:, at : at + 2]
            dhead_ref[1:2, a:b] = sums[:, HG + at : HG + at + 2]

    def drain_all(i, _):
        all_copy(lax.rem(me + i, BLOCKS), me).wait_send()
        return 0

    lax.fori_loop(1, BLOCKS, drain_all, 0, unroll=True)


def hand_on_kernel(*refs):
    n = len(refs) // 2
    for i in range(n):
        refs[n + i][...] = refs[i][...]


def hand_on(*arrays):
    return pl.pallas_call(
        hand_on_kernel,
        out_shape=tuple(jax.ShapeDtypeStruct(a.shape, a.dtype) for a in arrays),
        in_specs=[pl.BlockSpec(memory_space=pltpu.VMEM)] * len(arrays),
        out_specs=(pl.BlockSpec(memory_space=pltpu.VMEM),) * len(arrays),
        name="hand_on",
    )(*arrays)


def on_device(mixed_in, conv_weight, gate_in, head_params, doc_lengths, d_core):
    vmem = pl.BlockSpec(memory_space=pltpu.VMEM)
    mat = (HEADS, D, D)
    scratch = [
        pltpu.VMEM((ROWS + 8, CH), F32),
        pltpu.VMEM((ROWS, CH), F32),
        pltpu.VMEM((QK, D, D), F32),
        pltpu.VMEM((QK, D, D), F32),
        pltpu.VMEM((2 * QK, D, D), F32),
        pltpu.VMEM((3, ROWS, D), F32),
        pltpu.VMEM((ROWS, D), F32),
        pltpu.VMEM((HEADS, 8, D), F32),
        pltpu.VMEM((3, GROUPS, HG, D), F32),
        pltpu.VMEM(mat, F32),
        pltpu.VMEM(mat, F32),
        pltpu.VMEM(mat, F32),
        pltpu.VMEM(mat, F32),
        pltpu.VMEM(mat, F32),
        pltpu.VMEM((HEADS, 2 * D, D), BF),
        pltpu.VMEM(mat, BF),
        pltpu.VMEM(mat, F32),
        pltpu.VMEM(mat, F32),
        pltpu.VMEM((HEADS, PACK, D), BF),
        pltpu.VMEM((HEADS, PACK, D), BF),
        pltpu.VMEM(mat, BF),
        pltpu.VMEM(mat, BF),
        pltpu.VMEM(mat, BF),
        pltpu.VMEM(mat, BF),
        pltpu.VMEM((16, 1024), BF),
        pltpu.VMEM((16, 1024), BF),
        pltpu.VMEM((8, CH), F32),
        pltpu.VMEM((16, 1024), BF),
        pltpu.VMEM((2, GROUPS, HG, D), F32),
        pltpu.VMEM(mat, BF),
        pltpu.VMEM(mat, F32),
        pltpu.VMEM(mat, F32),
        pltpu.VMEM(mat, F32),
        pltpu.VMEM(mat, F32),
        pltpu.VMEM(mat, F32),
        pltpu.VMEM(mat, F32),
        pltpu.VMEM(mat, F32),
        pltpu.VMEM(mat, F32),
        pltpu.VMEM(mat, F32),
        pltpu.VMEM((QK, D, D), F32),
        pltpu.VMEM((GROUPS, HG, D), F32),
        pltpu.VMEM((BLOCKS, 8, PIECE), F32),
        pltpu.VMEM((BLOCKS, 8, PIECE), F32),
        pltpu.VMEM((DP, 8, PIECE), F32),
        pltpu.VMEM((BLOCKS, 8, PIECE), F32),
        pltpu.SemaphoreType.DMA((BLOCKS,)),
        pltpu.SemaphoreType.DMA((BLOCKS,)),
        pltpu.SemaphoreType.DMA((BLOCKS,)),
        pltpu.SemaphoreType.DMA((BLOCKS,)),
        pltpu.SemaphoreType.DMA((BLOCKS,)),
        pltpu.SemaphoreType.DMA((BLOCKS,)),
        pltpu.SemaphoreType.DMA((2,)),
        pltpu.SemaphoreType.DMA((2,)),
        pltpu.SemaphoreType.DMA((BLOCKS,)),
        pltpu.SemaphoreType.DMA((BLOCKS,)),
        pltpu.SemaphoreType.DMA((DP,)),
        pltpu.SemaphoreType.DMA((DP,)),
        pltpu.SemaphoreType.DMA((BLOCKS,)),
        pltpu.SemaphoreType.DMA((BLOCKS,)),
    ]
    core, dmix, dgate, dconv, dhead = pl.pallas_call(
        kernel,
        out_shape=(
            jax.ShapeDtypeStruct((ROWS, HEADS * D), BF),
            jax.ShapeDtypeStruct((ROWS, CH), BF),
            jax.ShapeDtypeStruct((2 * HEADS, ROWS), F32),
            jax.ShapeDtypeStruct((4, CH), F32),
            jax.ShapeDtypeStruct((2, HEADS), F32),
        ),
        in_specs=[vmem, vmem, vmem, vmem, pl.BlockSpec(memory_space=pltpu.SMEM), vmem],
        out_specs=(vmem,) * 5,
        scratch_shapes=scratch,
        compiler_params=pltpu.CompilerParams(
            collective_id=0, has_side_effects=True, vmem_limit_bytes=56 * 1024 * 1024
        ),
        name="delta_mix",
    )(mixed_in[0], conv_weight, gate_in[0].T, head_params, doc_lengths, d_core[0])
    core, dmix, dgate, dconv, dhead = hand_on(core, dmix, dgate, dconv, dhead)
    return core[None], dmix[None], dgate.T[None], dconv, dhead


def solution(mesh):
    return jax.shard_map(
        on_device,
        mesh=mesh,
        in_specs=(
            P("dp", "ctx", None),
            P(),
            P("dp", "ctx", None),
            P(),
            P("dp", None),
            P("dp", "ctx", None),
        ),
        out_specs=(P("dp", "ctx", None), P("dp", "ctx", None), P("dp", "ctx", None), P(), P()),
        check_vma=False,
    )
```

```python
import jax
import jax.numpy as jnp
from jax import lax
from jax.experimental import pallas as pl
from jax.experimental.pallas import tpu as pltpu
from jax.sharding import PartitionSpec as P

HEADS = 16
QK = 8
D = 128
ROWS = 128
CH = 4096
BLOCKS = 16
PACK = 2 * D + 16
HG = 4
GROUPS = HEADS // HG
DP = 8
PIECE = CH // BLOCKS
F32 = jnp.float32
BF = jnp.bfloat16
MESH = pl.DeviceIdType.MESH
HIGHEST = lax.Precision.HIGHEST


def dot(a, b, ca=1, cb=0):
    return lax.dot_general(a, b, (((ca,), (cb,)), ((), ())), preferred_element_type=F32)


def dot_full(a, b, ca=1, cb=0):
    return lax.dot_general(
        a, b, (((ca,), (cb,)), ((), ())), preferred_element_type=F32, precision=HIGHEST
    )


def split(a):
    high = a.astype(BF)
    return high, (a - high.astype(F32)).astype(BF)


def dot3(a, b, ca=1, cb=0):
    left = jnp.concatenate(a, axis=ca)
    wide = jnp.concatenate(b, axis=1 - cb)
    n = b[0].shape[1 - cb]
    t = dot(left, jnp.concatenate([wide, wide], axis=cb), ca, cb)
    return t[:, :n] + t[:, n:]


def iota(shape, dim):
    return lax.broadcasted_iota(jnp.int32, shape, dim)


def inverses(mats):
    row, col = iota((D, D), 0), iota((D, D), 1)
    eye = (row == col).astype(F32)

    def same(bits):
        return (row >> bits) == (col >> bits)

    near = same(3)
    a8 = [jnp.where(near, a, 0.0) for a in mats]
    a8s = [split(a) for a in a8]
    a2 = [dot3(s, s) for s in a8s]
    a2s = [split(a) for a in a2]
    a3 = [dot3(s, t) for s, t in zip(a8s, a2s)]
    a4s = [split(dot3(s, s)) for s in a2s]
    ys = [eye - a + b - c for a, b, c in zip(a8, a2, a3)]
    xs = [y + dot3(split(y), s) for y, s in zip(ys, a4s)]
    for bits in range(3, 7):
        mask = same(bits + 1) & jnp.logical_not(same(bits))
        cs = [split(jnp.where(mask, a, 0.0)) for a in mats]
        xss = [split(x) for x in xs]
        xc = [split(dot3(x, c)) for x, c in zip(xss, cs)]
        xs = [x - dot3(t, s) for x, t, s in zip(xs, xc, xss)]
    return xs


def parts_of(group):
    first, second = 4 * group, 4 * ((group + 2) % 4) + 2
    return [(0, first, first + 2), (2, second, second + 2)]


def kernel(
    x_hbm, w_ref, gate_ref, hp_ref, len_ref, dcore_hbm,
    core_hbm, dmix_hbm, dgate_ref, dconv_ref, dhead_ref,
    x_ref, dcore_ref, core_ref, dmix_ref, io_sem, xs, slope, qs, ks, norms, links, lks, gt, gts, d_s, dkk_s, p_s, x_s, uv_s, wq_s, w2_s, r0_s, ol_s,
    snd, rcv, snd2, rcv2, s_snd, g_snd, s_rcv, g_rcv, h_snd, h_rcv, e_add, e_rcv, dgo, u_s, a_s, v_s, b_s, e_s, ck_s, bck_s, bc_s, ek_s, end_s, dk_s, dcs, red, r1, r2, r3,
    snd_sem, rcv_sem, snd2_sem, rcv2_sem, s_ssem, s_rsem, g_ssem, g_rsem, h_sem, e_sem,
    r1_ssem, r1_rsem, r2_ssem, r2_rsem, r3_ssem, r3_rsem,
):
    me = lax.axis_index("ctx")
    mine = lax.axis_index("dp")
    first_pos = me * ROWS

    x_copy = pltpu.make_async_copy(x_hbm, x_ref, io_sem.at[0])
    dcore_copy = pltpu.make_async_copy(dcore_hbm, dcore_ref, io_sem.at[1])
    x_copy.start()
    dcore_copy.start()
    own_row = lax.div(me, 4)
    own_pair = lax.rem(lax.div(me, 2), 2)

    def group_of(step):
        group = lax.rem(own_row + step + 2 * own_pair, 4)
        qk = [2 * group, 2 * lax.rem(group + 2, 4) + 1]
        return group, qk, [2 * j + i for j in qk for i in range(2)]

    barrier = pltpu.get_barrier_semaphore()

    def greet(i, _):
        pl.semaphore_signal(
            barrier, inc=1, device_id={"ctx": lax.rem(me + i, BLOCKS)}, device_id_type=MESH
        )
        return 0

    lax.fori_loop(1, BLOCKS, greet, 0, unroll=True)

    def greet_dp(i, _):
        pl.semaphore_signal(
            barrier, inc=1, device_id={"dp": lax.rem(mine + i, DP)}, device_id_type=MESH
        )
        return 0

    lax.fori_loop(1, DP, greet_dp, 0, unroll=True)

    x_copy.wait()
    xs[pl.ds(8, ROWS), :] = x_ref[...].astype(F32)
    xs[0:8, :] = jnp.zeros((8, CH), F32)
    tail = [
        xs[pl.ds(133 + r, 1), pl.ds(1024 * p, 1024)] for r in range(3) for p in range(4)
    ] + [jnp.zeros((4, 1024), F32)]
    h_snd[...] = jnp.concatenate(tail, axis=0).astype(BF)

    pl.semaphore_wait(barrier, BLOCKS + DP - 2)

    def halo_copy():
        return pltpu.make_async_remote_copy(
            src_ref=h_snd, dst_ref=h_rcv, send_sem=h_sem.at[0], recv_sem=h_sem.at[1],
            device_id={"ctx": lax.rem(me + 1, BLOCKS)}, device_id_type=MESH,
        )

    halo_copy().start()

    row, col = iota((ROWS, D), 0), iota((ROWS, D), 1)
    low = row >= col
    strict = row > col
    ends = []
    total = 0
    for i in range(8):
        total = total + len_ref[0, i]
        ends.append(total)

    def doc_of(pos):
        found = jnp.zeros(pos.shape, jnp.int32)
        for e in ends:
            found = found + jnp.where(e <= pos, 1, 0)
        return found

    doc_col = doc_of(first_pos + row)
    doc_row = doc_of(first_pos + col)
    lks[...] = jnp.where((doc_col == doc_row) & low, 1.0, 0.0)
    for j in range(3):
        links[j] = jnp.where(doc_of(first_pos + row - 3 + j) == doc_col, 1.0, 0.0)
    doc_row16 = doc_row[:HEADS]
    doc_before = doc_of(jnp.full((HEADS, D), first_pos - 1, jnp.int32))
    doc_last = doc_of(jnp.full((HEADS, D), first_pos + ROWS - 1, jnp.int32))

    def lanes(block):
        return pl.ds(pl.multiple_of(block * D, D), D)

    def taps(j, block):
        t = xs[pl.ds(5 + j, ROWS), lanes(block)]
        return t if j == 3 else t * links[j]

    def conv_first(step, _):
        for i in range(4):
            block = 4 * step + i
            y = taps(3, block) * w_ref[3:4, lanes(block)]
            for j in range(3):
                y = y + taps(j, block) * w_ref[j : j + 1, lanes(block)]
            slope[:, lanes(block)] = y
        return 0

    lax.fori_loop(0, 8, conv_first, 0)

    def conv(block):
        y = slope[:, lanes(block)]
        sig = 1.0 / (1.0 + jnp.exp(-y))
        m = y * sig
        slope[:, lanes(block)] = sig + m * (1.0 - sig)
        return m

    eye16 = (iota((16, 16), 0) == iota((16, 16), 1)).astype(F32)
    gates = gate_ref[...]
    params = dot_full(eye16, hp_ref[...], 1, 1)
    scale = -jnp.exp(params[:, 0:1])
    z = gates[:HEADS] + params[:, 1:2]
    decay = scale * (jnp.maximum(z, 0.0) + jnp.log1p(jnp.exp(-jnp.abs(z))))
    ez = scale / (1.0 + jnp.exp(-z))
    beta = 1.0 / (1.0 + jnp.exp(-gates[HEADS:]))
    upto = jnp.where(row <= col, 1.0, 0.0)
    summed = dot_full(decay, upto)
    carried = jnp.exp(summed) * (doc_row16 == doc_before).astype(F32)
    to_end = jnp.exp(jnp.minimum(summed[:, D - 1 : D] - summed, 0.0)) * (
        doc_row16 == doc_last
    ).astype(F32)
    for n in range(GROUPS):
        for at, a, b in parts_of(n):
            gts[0, n, at : at + 2] = decay[a:b]
            gts[1, n, at : at + 2] = ez[a:b]
            gts[2, n, at : at + 2] = beta[a:b]
    rows8 = jnp.stack(
        [summed, beta, carried, to_end, beta * carried, summed, summed, summed], axis=1
    )
    gt[...] = rows8

    halo_copy().wait()
    inside = jnp.where(me > 0, 1.0, 0.0)
    hv = h_rcv[...].astype(F32) * inside
    for r in range(3):
        for p in range(4):
            xs[pl.ds(5 + r, 1), pl.ds(1024 * p, 1024)] = hv[4 * r + p : 4 * r + p + 1]
    y8 = xs[8:16, :] * w_ref[3:4, :]
    for j in range(3):
        link8 = jnp.concatenate([links[j, 0:8]] * (CH // D), axis=1)
        y8 = y8 + xs[5 + j : 13 + j, :] * link8 * w_ref[j : j + 1, :]
    slope[0:8, :] = y8
    dcore_copy.wait()


    def columns(h):
        t = jnp.transpose(gt[h])
        return [t[:, i : i + 1] for i in range(5)]

    def a_last(h):
        return gt[h][2:3, D - 1 : D]

    def pack_copy(h, source):
        return pltpu.make_async_remote_copy(
            src_ref=snd.at[h], dst_ref=rcv.at[source], send_sem=snd_sem.at[h],
            recv_sem=rcv_sem.at[source], device_id={"ctx": h}, device_id_type=MESH,
        )

    def grad_pack_copy(h, source):
        return pltpu.make_async_remote_copy(
            src_ref=snd2.at[h], dst_ref=rcv2.at[source], send_sem=snd2_sem.at[h],
            recv_sem=rcv2_sem.at[source], device_id={"ctx": h}, device_id_type=MESH,
        )

    def send_grad_packs(step):
        for h in group_of(step)[2]:
            @pl.when(h != me)
            def _():
                grad_pack_copy(h, me).start()

    def forward(step, _):
        _, qk, heads = group_of(step)
        kk, qq, kf, qf = [], [], [], []
        for j in qk:
            m = conv(j)
            norm = lax.rsqrt(jnp.sum(m * m, axis=1, keepdims=True) + 1e-6) * D**-0.5
            norms[j] = jnp.broadcast_to(norm, (ROWS, D))
            q = m * norm
            m = conv(QK + j)
            norm = lax.rsqrt(jnp.sum(m * m, axis=1, keepdims=True) + 1e-6)
            norms[QK + j] = jnp.broadcast_to(norm, (ROWS, D))
            k = m * norm
            qs[j] = q
            ks[j] = k
            k2, q2 = split(k), split(q)
            kk.append(dot3(k2, k2, 1, 1))
            qq.append(dot3(q2, k2, 1, 1))
            kf.append(k)
            qf.append(q)
        vs = [conv(2 * QK + h) for h in heads]
        cols = [columns(h) for h in heads]
        lk = lks[...]
        mats, ps = [], []
        for i, h in enumerate(heads):
            spans = lk * jnp.exp(jnp.minimum(cols[i][0] - gt[h][0:1], 0.0))
            dkk = jnp.where(strict, spans * kk[i // 2], 0.0)
            p = spans * qq[i // 2]
            mat = cols[i][1] * dkk
            d_s[h] = spans
            dkk_s[h] = dkk
            a_s[h] = mat
            p_s[h] = p
            v_s[h] = vs[i]
            ps.append(p.astype(BF))
            mats.append(mat)
        xinv = inverses(mats)
        for i, h in enumerate(heads):
            x_s[h] = xinv[i]
            right = jnp.concatenate([cols[i][1] * vs[i], cols[i][4] * kf[i // 2]], axis=1)
            uvw = dot3(split(xinv[i]), split(right))
            uvwb = uvw.astype(BF)
            uv_s[h] = uvw[:, :D]
            wq_s[h, 0:ROWS] = uvwb[:, D:]
            pw = dot(ps[i], uvwb)
            ol_s[h] = pw[:, :D]
            qc = (cols[i][2] * qf[i // 2] - pw[:, D:]).astype(BF)
            wq_s[h, ROWS : 2 * ROWS] = qc
            dk = (cols[i][3] * kf[i // 2]).astype(BF)
            nb = dot(uvwb, dk, 0, 0)
            gl = dot(dcore_ref[:, lanes(h)], qc, 0, 0)
            snd[h, 0:D] = nb[D:].astype(BF)
            snd[h, D : 2 * D] = nb[:D].astype(BF)
            snd2[h] = gl.astype(BF)
            al = jnp.broadcast_to(a_last(h), (16, D))
            t0 = al.astype(BF).astype(F32)
            t1 = (al - t0).astype(BF).astype(F32)
            t2 = al - t0 - t1
            r16 = iota((16, D), 0)
            snd[h, 2 * D : PACK] = jnp.where(
                r16 == 0, t0, jnp.where(r16 == 1, t1, jnp.where(r16 == 2, t2, 0.0))
            ).astype(BF)
        for h in heads:
            @pl.when(h != me)
            def _():
                pack_copy(h, me).start()
        return 0

    lax.fori_loop(0, GROUPS, forward, 0)
    for n in range(GROUPS):
        send_grad_packs(n)
    rcv[me] = snd[me]
    rcv2[me] = snd2[me]

    def aside(step, _):
        heads = [step * HG + i for i in range(HG)]
        for i, h in enumerate(heads):
            cols = columns(h)
            zz = dot(p_s[h].astype(BF), dcore_ref[:, lanes(h)], 0, 0)
            k = ks[h // 2]
            dk = cols[3] * k
            b_s[h] = jnp.broadcast_to(cols[1], (ROWS, D))
            e_s[h] = jnp.where(strict, cols[1] * d_s[h], 0.0)
            ck_s[h] = cols[2] * k
            bck_s[h] = cols[4] * k
            bc_s[h] = jnp.broadcast_to(cols[4], (ROWS, D))
            ek_s[h] = dk
            end_s[h] = jnp.broadcast_to(cols[3], (ROWS, D))
            out = dot3(split(x_s[h]), split(jnp.concatenate([zz, dk], axis=1)), 0, 0)
            r0_s[h] = out[:, :D]
            w2_s[h] = out[:, D:].astype(BF)
        return 0


    def s_copy(block, head):
        return pltpu.make_async_remote_copy(
            src_ref=s_snd.at[block], dst_ref=s_rcv.at[head], send_sem=s_ssem.at[block],
            recv_sem=s_rsem.at[head], device_id={"ctx": block}, device_id_type=MESH,
        )

    def g_copy(block, head):
        return pltpu.make_async_remote_copy(
            src_ref=g_snd.at[block], dst_ref=g_rcv.at[head], send_sem=g_ssem.at[block],
            recv_sem=g_rsem.at[head], device_id={"ctx": block}, device_id_type=MESH,
        )

    lax.fori_loop(0, GROUPS, aside, 0)

    def wait_pack(i, _):
        pack_copy(lax.rem(me + i, BLOCKS), lax.rem(me + i, BLOCKS)).wait_recv()
        return 0

    lax.fori_loop(1, BLOCKS, wait_pack, 0, unroll=True)

    zero = jnp.zeros((D, D), F32)
    s_snd[0] = zero.astype(BF)
    g_snd[BLOCKS - 1] = zero.astype(BF)

    def scalar_of(block):
        t = rcv[block, 2 * D : PACK].astype(F32)
        return t[0:1] + t[1:2] + t[2:3]

    def turn(i, state):
        state = (
            scalar_of(i) * state
            - dot(state.astype(BF), rcv[i, 0:D])
            + rcv[i, D : 2 * D].astype(F32)
        )
        s_snd[i + 1] = state.astype(BF)
        return state

    lax.fori_loop(0, BLOCKS - 1, turn, zero, unroll=True)

    def reader(i):
        step, which = lax.div(i, 4), lax.rem(lax.div(i, 2), 2)
        row = lax.rem(own_row + 8 - step - 2 * which, 4)
        return 4 * row + 2 * lax.rem(own_pair + which, 2) + lax.rem(i, 2)

    def send_state(i, _):
        other = reader(i)

        @pl.when(other != me)
        def _():
            s_copy(other, me).start()
        return 0

    lax.fori_loop(0, BLOCKS, send_state, 0, unroll=True)

    def wait_grad_pack(i, _):
        other = lax.rem(me + i, BLOCKS)
        grad_pack_copy(other, other).wait_recv()
        return 0

    lax.fori_loop(1, BLOCKS, wait_grad_pack, 0, unroll=True)

    def turn_back(i, grad):
        b = BLOCKS - 1 - i
        grad = (
            scalar_of(b) * grad
            - dot(grad.astype(BF), rcv[b, 0:D], 1, 1)
            + rcv2[b].astype(F32)
        )
        g_snd[b - 1] = grad.astype(BF)
        return grad

    lax.fori_loop(0, BLOCKS - 1, turn_back, zero, unroll=True)

    def send_grad(i, _):
        other = reader(i)

        @pl.when(other != me)
        def _():
            g_copy(other, me).start()
        return 0

    lax.fori_loop(0, BLOCKS, send_grad, 0, unroll=True)
    s_rcv[me] = s_snd[me]
    g_rcv[me] = g_snd[me]


    lane = col

    def conv_back(block, piece, half, dm):
        at = pl.ds(half * D, D)
        dy = dm * slope[:, lanes(block)]
        slope[:, lanes(block)] = dy
        for j in range(4):
            red[piece, j : j + 1, at] = jnp.sum(dy * taps(j, block), axis=0, keepdims=True)

    def taps_back(block):
        dy = slope[:, lanes(block)]
        own = dy * w_ref[3:4, lanes(block)]
        for j in range(3):
            turned = pltpu.roll(dy * links[j] * w_ref[j : j + 1, lanes(block)], ROWS - 3 + j, 0)
            own = own + jnp.where(row >= ROWS - 3 + j, 0.0, turned)
        last = own[ROWS - 8 :] + e_add[:, lanes(block)]
        dmix_ref[:, lanes(block)] = jnp.concatenate([own[: ROWS - 8], last], axis=0).astype(BF)

    def results(step, _):
        for i in range(HG):
            h = step * HG + i
            core_ref[:, lanes(h)] = (
                ol_s[h] + dot(wq_s[h, ROWS : 2 * ROWS], s_rcv[h], 1, 1)
            ).astype(BF)
        return 0

    suffix = jnp.where(row >= col, 1.0, 0.0)
    red[:, 4:8, :] = jnp.zeros((BLOCKS, 4, PIECE), F32)

    def red_copy(piece, source):
        return pltpu.make_async_remote_copy(
            src_ref=red.at[piece], dst_ref=r1.at[source], send_sem=r1_ssem.at[piece],
            recv_sem=r1_rsem.at[source], device_id={"ctx": piece}, device_id_type=MESH,
        )

    def send_piece(piece):
        @pl.when(piece != me)
        def _():
            red_copy(piece, me).start()

        @pl.when(piece == me)
        def _():
            r1[me] = red[piece]

    def from_state(step, _):
        group, qk, heads = group_of(step)
        for h in heads:
            @pl.when(h != me)
            def _():
                s_copy(h, h).wait_recv()
        packed = jnp.zeros((ROWS, D), F32)
        colsums = []
        for n, j in enumerate(qk):
            k, q = ks[j], qs[j]
            bs = dq = None
            for i in (2 * n, 2 * n + 1):
                h = heads[i]
                s = s_rcv[h]
                do = dcore_ref[:, lanes(h)]
                u = (uv_s[h] - dot(wq_s[h, 0:ROWS], s, 1, 1)).astype(BF)
                u_s[h] = u
                dos = columns(h)[2] * dot(do, s)
                dp = dot(do, u, 1, 1)
                f = dp * p_s[h]
                packed = packed + jnp.where(
                    lane == i, jnp.sum(f + q * dos, axis=1, keepdims=True), 0.0
                )
                colsums.append(jnp.sum(f, axis=0, keepdims=True))
                bq = dp * d_s[h]
                bs = bq if bs is None else bs + bq
                dq = dos if dq is None else dq + dos
            bs = bs.astype(BF)
            dq = dq + dot(bs, k.astype(BF))
            dk_s[j] = dot(bs, q.astype(BF), 0, 0)
            dm = norms[j] * (dq - q * (D * jnp.sum(q * dq, axis=1, keepdims=True)))
            conv_back(j, group, n, dm)
        dcs[group] = jnp.transpose(packed)[:HG] - jnp.concatenate(colsums, axis=0)
        return 0

    def backward(step, _):
        group, qk, heads = group_of(step)
        q_piece, k_piece, v_piece = group, GROUPS + group, 2 * (GROUPS + group)
        for h in heads:
            @pl.when(h != me)
            def _():
                g_copy(h, h).wait_recv()
        packed = jnp.zeros((ROWS, D), F32)
        colsums, lasts = [], []
        for n, j in enumerate(qk):
            k = ks[j]
            es, dk = None, dk_s[j]
            for i in (2 * n, 2 * n + 1):
                h = heads[i]
                s, g, u = s_rcv[h], g_rcv[h], u_s[h]
                r = r0_s[h] + dot(w2_s[h], g, 1, 1)
                rb = r.astype(BF)
                rs = dot(rb, s)
                da = -dot(rb, u, 1, 1)
                ug = dot(u, g)
                f = da * a_s[h]
                kug = ek_s[h] * ug
                dbeta = jnp.sum(r * v_s[h] - ck_s[h] * rs + da * dkk_s[h], axis=1, keepdims=True)
                dc = jnp.sum(f - bck_s[h] * rs - kug, axis=1, keepdims=True)
                packed = packed + jnp.where(lane == i, dc, 0.0)
                packed = packed + jnp.where(lane == HG + i, dbeta, 0.0)
                colsums.append(jnp.sum(f, axis=0, keepdims=True))
                lasts.append(
                    jnp.sum(
                        jnp.sum(kug, axis=0, keepdims=True)
                        + a_last(h)
                        * jnp.sum(g.astype(F32) * s.astype(F32), axis=0, keepdims=True),
                        axis=1, keepdims=True,
                    )
                )
                e = da * e_s[h]
                es = e if es is None else es + e
                dk = dk + end_s[h] * ug - bc_s[h] * rs
                conv_back(2 * QK + h, v_piece + i // 2, i % 2, b_s[h] * r)
            es = es.astype(BF)
            kb = k.astype(BF)
            dk = dk + dot(es, kb) + dot(es, kb, 0, 0)
            dm = norms[QK + j] * (dk - k * jnp.sum(k * dk, axis=1, keepdims=True))
            conv_back(QK + j, k_piece, n, dm)
        rows = jnp.transpose(packed)
        lasts = jnp.concatenate(lasts, axis=0)
        dc = rows[:HG] - jnp.concatenate(colsums, axis=0) + dcs[group]
        dc = dc + jnp.where(lane[:HG] == D - 1, lasts, 0.0)
        dg = dot_full(dc, suffix)
        dz = dg * gts[1, group]
        bet = gts[2, group]
        dgo[0, group] = dz
        dgo[1, group] = rows[HG : 2 * HG] * bet * (1.0 - bet)
        sums = dot_full(jnp.ones((8, D), F32), jnp.concatenate([dg * gts[0, group], dz], axis=0), 1, 1)
        red[q_piece, 4:5, 0 : 2 * HG] = sums[0:1]
        for piece in (q_piece, k_piece, v_piece, v_piece + 1):
            send_piece(piece)
        return 0

    lax.fori_loop(0, GROUPS, from_state, 0)
    lax.fori_loop(0, GROUPS, results, 0)
    core_copy = pltpu.make_async_copy(core_ref, core_hbm, io_sem.at[2])
    core_copy.start()
    lax.fori_loop(0, GROUPS, backward, 0)

    spill = jnp.zeros((8, CH), F32)
    row8w = iota((8, CH), 0)
    for j in range(3):
        link8 = jnp.concatenate([links[j, 0:8]] * (CH // D), axis=1)
        turned = pltpu.roll(slope[0:8, :] * link8 * w_ref[j : j + 1, :], 5 + j, 0)
        spill = spill + jnp.where(row8w >= 5 + j, turned, 0.0)
    h_snd[...] = jnp.concatenate(
        [spill[5 + r : 6 + r, 1024 * p : 1024 * p + 1024] for r in range(3) for p in range(4)]
        + [jnp.zeros((4, 1024), F32)],
        axis=0,
    ).astype(BF)
    back = pltpu.make_async_remote_copy(
        src_ref=h_snd, dst_ref=e_rcv, send_sem=e_sem.at[0], recv_sem=e_sem.at[1],
        device_id={"ctx": lax.rem(me + BLOCKS - 1, BLOCKS)}, device_id_type=MESH,
    )
    back.start()

    def wait_red(i, _):
        other = lax.rem(me + i, BLOCKS)
        red_copy(other, other).wait_recv()
        return 0

    lax.fori_loop(1, BLOCKS, wait_red, 0, unroll=True)
    total = r1[0]
    for i in range(1, BLOCKS):
        total = total + r1[i]
    r2[mine] = total

    def dp_copy(other, source):
        return pltpu.make_async_remote_copy(
            src_ref=r2.at[source], dst_ref=r2.at[source], send_sem=r2_ssem.at[other],
            recv_sem=r2_rsem.at[source], device_id={"dp": other}, device_id_type=MESH,
        )

    def send_dp(i, _):
        dp_copy(lax.rem(mine + i, DP), mine).start()
        return 0

    lax.fori_loop(1, DP, send_dp, 0, unroll=True)

    back.wait()
    before_last = jnp.where(me < BLOCKS - 1, 1.0, 0.0)
    ev = e_rcv[...].astype(F32) * before_last
    for p in range(4):
        e_add[:, 1024 * p : 1024 * p + 1024] = jnp.concatenate(
            [jnp.zeros((5, 1024), F32)] + [ev[4 * r + p : 4 * r + p + 1] for r in range(3)], axis=0
        )

    def mixed_part(step, _):
        for i in range(4):
            taps_back(4 * step + i)
        return 0

    lax.fori_loop(0, 4, mixed_part, 0)

    def mixed_copy(half):
        part = pl.ds(half * (CH // 2), CH // 2)
        return pltpu.make_async_copy(
            dmix_ref.at[:, part], dmix_hbm.at[:, part], io_sem.at[3 + half]
        )

    mixed_copy(0).start()

    for n in range(GROUPS):
        for at, a, b in parts_of(n):
            dgate_ref[a:b, :] = dgo[0, n, at : at + 2]
            dgate_ref[HEADS + a : HEADS + b, :] = dgo[1, n, at : at + 2]

    def wait_dp(i, _):
        other = lax.rem(mine + i, DP)
        dp_copy(other, other).wait_recv()
        return 0

    lax.fori_loop(1, DP, wait_dp, 0, unroll=True)
    total = r2[0]
    for i in range(1, DP):
        total = total + r2[i]
    r3[me] = total

    def all_copy(other, source):
        return pltpu.make_async_remote_copy(
            src_ref=r3.at[source], dst_ref=r3.at[source], send_sem=r3_ssem.at[other],
            recv_sem=r3_rsem.at[source], device_id={"ctx": other}, device_id_type=MESH,
        )

    def send_all(i, _):
        all_copy(lax.rem(me + i, BLOCKS), me).start()
        return 0

    lax.fori_loop(1, BLOCKS, send_all, 0, unroll=True)
    lax.fori_loop(4, 8, mixed_part, 0)
    mixed_copy(1).start()

    def drain(i, _):
        other = lax.rem(me + i, BLOCKS)
        pack_copy(other, me).wait_send()
        grad_pack_copy(other, me).wait_send()
        s_copy(other, me).wait_send()
        g_copy(other, me).wait_send()
        red_copy(other, me).wait_send()
        return 0

    lax.fori_loop(1, BLOCKS, drain, 0, unroll=True)

    def drain_dp(i, _):
        dp_copy(lax.rem(mine + i, DP), mine).wait_send()
        return 0

    lax.fori_loop(1, DP, drain_dp, 0, unroll=True)

    def wait_all(i, _):
        other = lax.rem(me + i, BLOCKS)
        all_copy(other, other).wait_recv()
        return 0

    lax.fori_loop(1, BLOCKS, wait_all, 0, unroll=True)
    for n in range(GROUPS):
        sums = r3[n, 4:5]
        for at, a, b in parts_of(n):
            lo = (at // 2) * D
            dconv_ref[:, a // 2 * D : a // 2 * D + D] = r3[n, 0:4, lo : lo + D]
            dconv_ref[:, (QK + a // 2) * D : (QK + a // 2 + 1) * D] = r3[GROUPS + n, 0:4, lo : lo + D]
            dconv_ref[:, (2 * QK + a) * D : (2 * QK + b) * D] = r3[2 * (GROUPS + n) + at // 2, 0:4]
            dhead_ref[0:1, a:b] = sums[:, at : at + 2]
            dhead_ref[1:2, a:b] = sums[:, HG + at : HG + at + 2]

    def drain_all(i, _):
        all_copy(lax.rem(me + i, BLOCKS), me).wait_send()
        return 0

    lax.fori_loop(1, BLOCKS, drain_all, 0, unroll=True)
    core_copy.wait()
    mixed_copy(0).wait()
    mixed_copy(1).wait()


def hand_on_kernel(*refs):
    n = len(refs) // 2
    for i in range(n):
        refs[n + i][...] = refs[i][...]


def hand_on(*arrays):
    return pl.pallas_call(
        hand_on_kernel,
        out_shape=tuple(jax.ShapeDtypeStruct(a.shape, a.dtype) for a in arrays),
        in_specs=[pl.BlockSpec(memory_space=pltpu.VMEM)] * len(arrays),
        out_specs=(pl.BlockSpec(memory_space=pltpu.VMEM),) * len(arrays),
        name="hand_on",
    )(*arrays)


def on_device(mixed_in, conv_weight, gate_in, head_params, doc_lengths, d_core):
    vmem = pl.BlockSpec(memory_space=pltpu.VMEM)
    any_ = pl.BlockSpec(memory_space=pl.ANY)
    mat = (HEADS, D, D)
    scratch = [
        pltpu.VMEM((ROWS, CH), BF),
        pltpu.VMEM((ROWS, HEADS * D), BF),
        pltpu.VMEM((ROWS, HEADS * D), BF),
        pltpu.VMEM((ROWS, CH), BF),
        pltpu.SemaphoreType.DMA((5,)),
        pltpu.VMEM((ROWS + 8, CH), F32),
        pltpu.VMEM((ROWS, CH), F32),
        pltpu.VMEM((QK, D, D), F32),
        pltpu.VMEM((QK, D, D), F32),
        pltpu.VMEM((2 * QK, D, D), F32),
        pltpu.VMEM((3, ROWS, D), F32),
        pltpu.VMEM((ROWS, D), F32),
        pltpu.VMEM((HEADS, 8, D), F32),
        pltpu.VMEM((3, GROUPS, HG, D), F32),
        pltpu.VMEM(mat, F32),
        pltpu.VMEM(mat, F32),
        pltpu.VMEM(mat, F32),
        pltpu.VMEM(mat, F32),
        pltpu.VMEM(mat, F32),
        pltpu.VMEM((HEADS, 2 * D, D), BF),
        pltpu.VMEM(mat, BF),
        pltpu.VMEM(mat, F32),
        pltpu.VMEM(mat, F32),
        pltpu.VMEM((HEADS, PACK, D), BF),
        pltpu.VMEM((HEADS, PACK, D), BF),
        pltpu.VMEM(mat, BF),
        pltpu.VMEM(mat, BF),
        pltpu.VMEM(mat, BF),
        pltpu.VMEM(mat, BF),
        pltpu.VMEM(mat, BF),
        pltpu.VMEM(mat, BF),
        pltpu.VMEM((16, 1024), BF),
        pltpu.VMEM((16, 1024), BF),
        pltpu.VMEM((8, CH), F32),
        pltpu.VMEM((16, 1024), BF),
        pltpu.VMEM((2, GROUPS, HG, D), F32),
        pltpu.VMEM(mat, BF),
        pltpu.VMEM(mat, F32),
        pltpu.VMEM(mat, F32),
        pltpu.VMEM(mat, F32),
        pltpu.VMEM(mat, F32),
        pltpu.VMEM(mat, F32),
        pltpu.VMEM(mat, F32),
        pltpu.VMEM(mat, F32),
        pltpu.VMEM(mat, F32),
        pltpu.VMEM(mat, F32),
        pltpu.VMEM((QK, D, D), F32),
        pltpu.VMEM((GROUPS, HG, D), F32),
        pltpu.VMEM((BLOCKS, 8, PIECE), F32),
        pltpu.VMEM((BLOCKS, 8, PIECE), F32),
        pltpu.VMEM((DP, 8, PIECE), F32),
        pltpu.VMEM((BLOCKS, 8, PIECE), F32),
        pltpu.SemaphoreType.DMA((BLOCKS,)),
        pltpu.SemaphoreType.DMA((BLOCKS,)),
        pltpu.SemaphoreType.DMA((BLOCKS,)),
        pltpu.SemaphoreType.DMA((BLOCKS,)),
        pltpu.SemaphoreType.DMA((BLOCKS,)),
        pltpu.SemaphoreType.DMA((BLOCKS,)),
        pltpu.SemaphoreType.DMA((BLOCKS,)),
        pltpu.SemaphoreType.DMA((BLOCKS,)),
        pltpu.SemaphoreType.DMA((2,)),
        pltpu.SemaphoreType.DMA((2,)),
        pltpu.SemaphoreType.DMA((BLOCKS,)),
        pltpu.SemaphoreType.DMA((BLOCKS,)),
        pltpu.SemaphoreType.DMA((DP,)),
        pltpu.SemaphoreType.DMA((DP,)),
        pltpu.SemaphoreType.DMA((BLOCKS,)),
        pltpu.SemaphoreType.DMA((BLOCKS,)),
    ]
    core, dmix, dgate, dconv, dhead = pl.pallas_call(
        kernel,
        out_shape=(
            jax.ShapeDtypeStruct((ROWS, HEADS * D), BF),
            jax.ShapeDtypeStruct((ROWS, CH), BF),
            jax.ShapeDtypeStruct((2 * HEADS, ROWS), F32),
            jax.ShapeDtypeStruct((4, CH), F32),
            jax.ShapeDtypeStruct((2, HEADS), F32),
        ),
        in_specs=[any_, vmem, vmem, vmem, pl.BlockSpec(memory_space=pltpu.SMEM), any_],
        out_specs=(any_, any_, vmem, vmem, vmem),
        scratch_shapes=scratch,
        compiler_params=pltpu.CompilerParams(
            collective_id=0, has_side_effects=True, vmem_limit_bytes=56 * 1024 * 1024
        ),
        name="delta_mix",
    )(mixed_in[0], conv_weight, gate_in[0].T, head_params, doc_lengths, d_core[0])
    core, dmix, dgate, dconv, dhead = hand_on(core, dmix, dgate, dconv, dhead)
    return core[None], dmix[None], dgate.T[None], dconv, dhead


def solution(mesh):
    return jax.shard_map(
        on_device,
        mesh=mesh,
        in_specs=(
            P("dp", "ctx", None),
            P(),
            P("dp", "ctx", None),
            P(),
            P("dp", None),
            P("dp", "ctx", None),
        ),
        out_specs=(P("dp", "ctx", None), P("dp", "ctx", None), P("dp", "ctx", None), P(), P()),
        check_vma=False,
    )
```

```python
import functools

import jax
import jax.numpy as jnp
from jax import lax
from jax.experimental import pallas as pl
from jax.experimental.pallas import tpu as pltpu
from jax.sharding import PartitionSpec as P

HEADS = 16
QK = 8
D = 128
ROWS = 128
CH = 4096
BLOCKS = 16
PACK = 2 * D + 16
HG = 4
GROUPS = HEADS // HG
DP = 8
PIECE = CH // BLOCKS
F32 = jnp.float32
BF = jnp.bfloat16
MESH = pl.DeviceIdType.MESH
HIGHEST = lax.Precision.HIGHEST


def dot(a, b, ca=1, cb=0):
    return lax.dot_general(a, b, (((ca,), (cb,)), ((), ())), preferred_element_type=F32)


def dot_full(a, b, ca=1, cb=0):
    return lax.dot_general(
        a, b, (((ca,), (cb,)), ((), ())), preferred_element_type=F32, precision=HIGHEST
    )


def split(a):
    high = a.astype(BF)
    return high, (a - high.astype(F32)).astype(BF)


def dot3(a, b, ca=1, cb=0):
    left = jnp.concatenate(a, axis=ca)
    wide = jnp.concatenate(b, axis=1 - cb)
    n = b[0].shape[1 - cb]
    t = dot(left, jnp.concatenate([wide, wide], axis=cb), ca, cb)
    return t[:, :n] + t[:, n:]


def iota(shape, dim):
    return lax.broadcasted_iota(jnp.int32, shape, dim)


def inverses(mats):
    row, col = iota((D, D), 0), iota((D, D), 1)
    eye = (row == col).astype(F32)

    def same(bits):
        return (row >> bits) == (col >> bits)

    near = same(3)
    a8 = [jnp.where(near, a, 0.0) for a in mats]
    a8s = [split(a) for a in a8]
    a2 = [dot3(s, s) for s in a8s]
    a2s = [split(a) for a in a2]
    a3 = [dot3(s, t) for s, t in zip(a8s, a2s)]
    a4s = [split(dot3(s, s)) for s in a2s]
    ys = [eye - a + b - c for a, b, c in zip(a8, a2, a3)]
    xs = [y + dot3(split(y), s) for y, s in zip(ys, a4s)]
    for bits in range(3, 7):
        mask = same(bits + 1) & jnp.logical_not(same(bits))
        cs = [split(jnp.where(mask, a, 0.0)) for a in mats]
        xss = [split(x) for x in xs]
        xc = [split(dot3(x, c)) for x, c in zip(xss, cs)]
        xs = [x - dot3(t, s) for x, t, s in zip(xs, xc, xss)]
    return xs


def parts_of(group):
    first, second = 4 * group, 4 * ((group + 2) % 4) + 2
    return [(0, first, first + 2), (2, second, second + 2)]


def kernel(
    x_hbm, w_ref, gate_ref, hp_ref, len_ref, dcore_hbm,
    core_hbm, dmix_hbm, dgate_ref, dconv_ref, dhead_ref,
    x_ref, dcore_ref, core_ref, dmix_ref, io_sem, xs, slope, qs, ks, norms, links, lks, gt, gts, d_s, dkk_s, p_s, x_s, uv_s, wq_s, w2_s, r0_s, ol_s,
    snd, rcv, snd2, rcv2, s_snd, g_snd, s_rcv, g_rcv, h_snd, h_rcv, e_add, e_rcv, dgo, u_s, a_s, v_s, b_s, e_s, ck_s, bck_s, bc_s, ek_s, end_s, dk_s, dcs, red, r1, r2, r3,
    snd_sem, rcv_sem, snd2_sem, rcv2_sem, s_ssem, s_rsem, g_ssem, g_rsem, h_sem, e_sem,
    r1_ssem, r1_rsem, r2_ssem, r2_rsem, r3_ssem, r3_rsem,
):
    me = lax.axis_index("ctx")
    mine = lax.axis_index("dp")
    first_pos = me * ROWS

    x_copy = pltpu.make_async_copy(x_hbm, x_ref, io_sem.at[0])
    dcore_copy = pltpu.make_async_copy(dcore_hbm, dcore_ref, io_sem.at[1])
    x_copy.start()
    dcore_copy.start()
    own_row = lax.div(me, 4)
    own_pair = lax.rem(lax.div(me, 2), 2)

    def group_of(step):
        group = lax.rem(own_row + step + 2 * own_pair, 4)
        qk = [2 * group, 2 * lax.rem(group + 2, 4) + 1]
        return group, qk, [2 * j + i for j in qk for i in range(2)]

    barrier = pltpu.get_barrier_semaphore()

    def greet(i, _):
        pl.semaphore_signal(
            barrier, inc=1, device_id={"ctx": lax.rem(me + i, BLOCKS)}, device_id_type=MESH
        )
        return 0

    lax.fori_loop(1, BLOCKS, greet, 0, unroll=True)

    def greet_dp(i, _):
        pl.semaphore_signal(
            barrier, inc=1, device_id={"dp": lax.rem(mine + i, DP)}, device_id_type=MESH
        )
        return 0

    lax.fori_loop(1, DP, greet_dp, 0, unroll=True)

    x_copy.wait()
    xs[pl.ds(8, ROWS), :] = x_ref[...].astype(F32)
    xs[0:8, :] = jnp.zeros((8, CH), F32)
    tail = [
        xs[pl.ds(133 + r, 1), pl.ds(1024 * p, 1024)] for r in range(3) for p in range(4)
    ] + [jnp.zeros((4, 1024), F32)]
    h_snd[...] = jnp.concatenate(tail, axis=0).astype(BF)

    pl.semaphore_wait(barrier, BLOCKS + DP - 2)

    def halo_copy():
        return pltpu.make_async_remote_copy(
            src_ref=h_snd, dst_ref=h_rcv, send_sem=h_sem.at[0], recv_sem=h_sem.at[1],
            device_id={"ctx": lax.rem(me + 1, BLOCKS)}, device_id_type=MESH,
        )

    halo_copy().start()

    row, col = iota((ROWS, D), 0), iota((ROWS, D), 1)
    low = row >= col
    strict = row > col
    ends = []
    total = 0
    for i in range(8):
        total = total + len_ref[0, i]
        ends.append(total)

    def doc_of(pos):
        found = jnp.zeros(pos.shape, jnp.int32)
        for e in ends:
            found = found + jnp.where(e <= pos, 1, 0)
        return found

    doc_col = doc_of(first_pos + row)
    doc_row = doc_of(first_pos + col)
    lks[...] = jnp.where((doc_col == doc_row) & low, 1.0, 0.0)
    for j in range(3):
        links[j] = jnp.where(doc_of(first_pos + row - 3 + j) == doc_col, 1.0, 0.0)
    doc_row16 = doc_row[:HEADS]
    doc_before = doc_of(jnp.full((HEADS, D), first_pos - 1, jnp.int32))
    doc_last = doc_of(jnp.full((HEADS, D), first_pos + ROWS - 1, jnp.int32))

    def lanes(block):
        return pl.ds(pl.multiple_of(block * D, D), D)

    def taps(j, block):
        t = xs[pl.ds(5 + j, ROWS), lanes(block)]
        return t if j == 3 else t * links[j]

    def conv_first(step, _):
        for i in range(4):
            block = 4 * step + i
            y = taps(3, block) * w_ref[3:4, lanes(block)]
            for j in range(3):
                y = y + taps(j, block) * w_ref[j : j + 1, lanes(block)]
            slope[:, lanes(block)] = y
        return 0

    lax.fori_loop(0, 8, conv_first, 0)

    def conv(block):
        y = slope[:, lanes(block)]
        sig = 1.0 / (1.0 + jnp.exp(-y))
        m = y * sig
        slope[:, lanes(block)] = sig + m * (1.0 - sig)
        return m

    eye16 = (iota((16, 16), 0) == iota((16, 16), 1)).astype(F32)
    gates = gate_ref[...]
    params = dot_full(eye16, hp_ref[...], 1, 1)
    scale = -jnp.exp(params[:, 0:1])
    z = gates[:HEADS] + params[:, 1:2]
    decay = scale * (jnp.maximum(z, 0.0) + jnp.log1p(jnp.exp(-jnp.abs(z))))
    ez = scale / (1.0 + jnp.exp(-z))
    beta = 1.0 / (1.0 + jnp.exp(-gates[HEADS:]))
    upto = jnp.where(row <= col, 1.0, 0.0)
    summed = dot_full(decay, upto)
    carried = jnp.exp(summed) * (doc_row16 == doc_before).astype(F32)
    to_end = jnp.exp(jnp.minimum(summed[:, D - 1 : D] - summed, 0.0)) * (
        doc_row16 == doc_last
    ).astype(F32)
    for n in range(GROUPS):
        for at, a, b in parts_of(n):
            gts[0, n, at : at + 2] = decay[a:b]
            gts[1, n, at : at + 2] = ez[a:b]
            gts[2, n, at : at + 2] = beta[a:b]
    rows8 = jnp.stack(
        [summed, beta, carried, to_end, beta * carried, summed, summed, summed], axis=1
    )
    gt[...] = rows8

    halo_copy().wait()
    inside = jnp.where(me > 0, 1.0, 0.0)
    hv = h_rcv[...].astype(F32) * inside
    for r in range(3):
        for p in range(4):
            xs[pl.ds(5 + r, 1), pl.ds(1024 * p, 1024)] = hv[4 * r + p : 4 * r + p + 1]
    y8 = xs[8:16, :] * w_ref[3:4, :]
    for j in range(3):
        link8 = jnp.concatenate([links[j, 0:8]] * (CH // D), axis=1)
        y8 = y8 + xs[5 + j : 13 + j, :] * link8 * w_ref[j : j + 1, :]
    slope[0:8, :] = y8
    dcore_copy.wait()


    def columns(h):
        t = jnp.transpose(gt[h])
        return [t[:, i : i + 1] for i in range(5)]

    def a_last(h):
        return gt[h][2:3, D - 1 : D]

    def pack_copy(h, source):
        return pltpu.make_async_remote_copy(
            src_ref=snd.at[h], dst_ref=rcv.at[source], send_sem=snd_sem.at[h],
            recv_sem=rcv_sem.at[source], device_id={"ctx": h}, device_id_type=MESH,
        )

    def grad_pack_copy(h, source):
        return pltpu.make_async_remote_copy(
            src_ref=snd2.at[h], dst_ref=rcv2.at[source], send_sem=snd2_sem.at[h],
            recv_sem=rcv2_sem.at[source], device_id={"ctx": h}, device_id_type=MESH,
        )

    def send_grad_packs(step):
        for h in group_of(step)[2]:
            @pl.when(h != me)
            def _():
                grad_pack_copy(h, me).start()

    def forward(step, _):
        _, qk, heads = group_of(step)
        kk, qq, kf, qf = [], [], [], []
        for j in qk:
            m = conv(j)
            norm = lax.rsqrt(jnp.sum(m * m, axis=1, keepdims=True) + 1e-6) * D**-0.5
            norms[j] = jnp.broadcast_to(norm, (ROWS, D))
            q = m * norm
            m = conv(QK + j)
            norm = lax.rsqrt(jnp.sum(m * m, axis=1, keepdims=True) + 1e-6)
            norms[QK + j] = jnp.broadcast_to(norm, (ROWS, D))
            k = m * norm
            qs[j] = q
            ks[j] = k
            k2, q2 = split(k), split(q)
            kk.append(dot3(k2, k2, 1, 1))
            qq.append(dot3(q2, k2, 1, 1))
            kf.append(k)
            qf.append(q)
        vs = [conv(2 * QK + h) for h in heads]
        cols = [columns(h) for h in heads]
        lk = lks[...]
        mats, ps = [], []
        for i, h in enumerate(heads):
            spans = lk * jnp.exp(jnp.minimum(cols[i][0] - gt[h][0:1], 0.0))
            dkk = jnp.where(strict, spans * kk[i // 2], 0.0)
            p = spans * qq[i // 2]
            mat = cols[i][1] * dkk
            d_s[h] = spans
            dkk_s[h] = dkk
            a_s[h] = mat
            p_s[h] = p
            v_s[h] = vs[i]
            ps.append(p.astype(BF))
            mats.append(mat)
        xinv = inverses(mats)
        for i, h in enumerate(heads):
            x_s[h] = xinv[i]
            right = jnp.concatenate([cols[i][1] * vs[i], cols[i][4] * kf[i // 2]], axis=1)
            uvw = dot3(split(xinv[i]), split(right))
            uvwb = uvw.astype(BF)
            uv_s[h] = uvw[:, :D]
            wq_s[h, 0:ROWS] = uvwb[:, D:]
            pw = dot(ps[i], uvwb)
            ol_s[h] = pw[:, :D]
            qc = (cols[i][2] * qf[i // 2] - pw[:, D:]).astype(BF)
            wq_s[h, ROWS : 2 * ROWS] = qc
            dk = (cols[i][3] * kf[i // 2]).astype(BF)
            nb = dot(uvwb, dk, 0, 0)
            gl = dot(dcore_ref[:, lanes(h)], qc, 0, 0)
            snd[h, 0:D] = nb[D:].astype(BF)
            snd[h, D : 2 * D] = nb[:D].astype(BF)
            snd2[h] = gl.astype(BF)
            al = jnp.broadcast_to(a_last(h), (16, D))
            t0 = al.astype(BF).astype(F32)
            t1 = (al - t0).astype(BF).astype(F32)
            t2 = al - t0 - t1
            r16 = iota((16, D), 0)
            snd[h, 2 * D : PACK] = jnp.where(
                r16 == 0, t0, jnp.where(r16 == 1, t1, jnp.where(r16 == 2, t2, 0.0))
            ).astype(BF)
        for h in heads:
            @pl.when(h != me)
            def _():
                pack_copy(h, me).start()
        return 0

    lax.fori_loop(0, GROUPS, forward, 0)
    for n in range(GROUPS):
        send_grad_packs(n)
    rcv[me] = snd[me]
    rcv2[me] = snd2[me]

    def aside(step, _):
        heads = [step * HG + i for i in range(HG)]
        for i, h in enumerate(heads):
            cols = columns(h)
            zz = dot(p_s[h].astype(BF), dcore_ref[:, lanes(h)], 0, 0)
            k = ks[h // 2]
            dk = cols[3] * k
            b_s[h] = jnp.broadcast_to(cols[1], (ROWS, D))
            e_s[h] = jnp.where(strict, cols[1] * d_s[h], 0.0)
            ck_s[h] = cols[2] * k
            bck_s[h] = cols[4] * k
            bc_s[h] = jnp.broadcast_to(cols[4], (ROWS, D))
            ek_s[h] = dk
            end_s[h] = jnp.broadcast_to(cols[3], (ROWS, D))
            out = dot3(split(x_s[h]), split(jnp.concatenate([zz, dk], axis=1)), 0, 0)
            r0_s[h] = out[:, :D]
            w2_s[h] = out[:, D:].astype(BF)
        return 0


    def s_copy(block, head):
        return pltpu.make_async_remote_copy(
            src_ref=s_snd.at[block], dst_ref=s_rcv.at[head], send_sem=s_ssem.at[block],
            recv_sem=s_rsem.at[head], device_id={"ctx": block}, device_id_type=MESH,
        )

    def g_copy(block, head):
        return pltpu.make_async_remote_copy(
            src_ref=g_snd.at[block], dst_ref=g_rcv.at[head], send_sem=g_ssem.at[block],
            recv_sem=g_rsem.at[head], device_id={"ctx": block}, device_id_type=MESH,
        )

    lax.fori_loop(0, GROUPS, aside, 0)

    def wait_pack(i, _):
        pack_copy(lax.rem(me + i, BLOCKS), lax.rem(me + i, BLOCKS)).wait_recv()
        return 0

    lax.fori_loop(1, BLOCKS, wait_pack, 0, unroll=True)

    zero = jnp.zeros((D, D), F32)
    s_snd[0] = zero.astype(BF)
    g_snd[BLOCKS - 1] = zero.astype(BF)

    def scalar_of(block):
        t = rcv[block, 2 * D : PACK].astype(F32)
        return t[0:1] + t[1:2] + t[2:3]

    def turn(i, state):
        state = (
            scalar_of(i) * state
            - dot(state.astype(BF), rcv[i, 0:D])
            + rcv[i, D : 2 * D].astype(F32)
        )
        s_snd[i + 1] = state.astype(BF)
        return state

    lax.fori_loop(0, BLOCKS - 1, turn, zero, unroll=True)

    def reader(i):
        step, which = lax.div(i, 4), lax.rem(lax.div(i, 2), 2)
        row = lax.rem(own_row + 8 - step - 2 * which, 4)
        return 4 * row + 2 * lax.rem(own_pair + which, 2) + lax.rem(i, 2)

    def send_state(i, _):
        other = reader(i)

        @pl.when(other != me)
        def _():
            s_copy(other, me).start()
        return 0

    lax.fori_loop(0, BLOCKS, send_state, 0, unroll=True)

    def wait_grad_pack(i, _):
        other = lax.rem(me + i, BLOCKS)
        grad_pack_copy(other, other).wait_recv()
        return 0

    lax.fori_loop(1, BLOCKS, wait_grad_pack, 0, unroll=True)

    def turn_back(i, grad):
        b = BLOCKS - 1 - i
        grad = (
            scalar_of(b) * grad
            - dot(grad.astype(BF), rcv[b, 0:D], 1, 1)
            + rcv2[b].astype(F32)
        )
        g_snd[b - 1] = grad.astype(BF)
        return grad

    lax.fori_loop(0, BLOCKS - 1, turn_back, zero, unroll=True)

    def send_grad(i, _):
        other = reader(i)

        @pl.when(other != me)
        def _():
            g_copy(other, me).start()
        return 0

    lax.fori_loop(0, BLOCKS, send_grad, 0, unroll=True)
    s_rcv[me] = s_snd[me]
    g_rcv[me] = g_snd[me]


    lane = col

    def conv_back(block, piece, half, dm):
        at = pl.ds(half * D, D)
        dy = dm * slope[:, lanes(block)]
        slope[:, lanes(block)] = dy
        for j in range(4):
            red[piece, j : j + 1, at] = jnp.sum(dy * taps(j, block), axis=0, keepdims=True)

    def taps_back(block):
        dy = slope[:, lanes(block)]
        own = dy * w_ref[3:4, lanes(block)]
        for j in range(3):
            turned = pltpu.roll(dy * links[j] * w_ref[j : j + 1, lanes(block)], ROWS - 3 + j, 0)
            own = own + jnp.where(row >= ROWS - 3 + j, 0.0, turned)
        last = own[ROWS - 8 :] + e_add[:, lanes(block)]
        dmix_ref[:, lanes(block)] = jnp.concatenate([own[: ROWS - 8], last], axis=0).astype(BF)

    def results(step, _):
        for i in range(HG):
            h = step * HG + i
            core_ref[:, lanes(h)] = (
                ol_s[h] + dot(wq_s[h, ROWS : 2 * ROWS], s_rcv[h], 1, 1)
            ).astype(BF)
        return 0

    suffix = jnp.where(row >= col, 1.0, 0.0)
    red[:, 4:8, :] = jnp.zeros((BLOCKS, 4, PIECE), F32)

    def red_copy(piece, source):
        return pltpu.make_async_remote_copy(
            src_ref=red.at[piece], dst_ref=r1.at[source], send_sem=r1_ssem.at[piece],
            recv_sem=r1_rsem.at[source], device_id={"ctx": piece}, device_id_type=MESH,
        )

    def send_piece(piece):
        @pl.when(piece != me)
        def _():
            red_copy(piece, me).start()

        @pl.when(piece == me)
        def _():
            r1[me] = red[piece]

    def from_state(step, _):
        group, qk, heads = group_of(step)
        for h in heads:
            @pl.when(h != me)
            def _():
                s_copy(h, h).wait_recv()
        packed = jnp.zeros((ROWS, D), F32)
        colsums = []
        for n, j in enumerate(qk):
            k, q = ks[j], qs[j]
            bs = dq = None
            for i in (2 * n, 2 * n + 1):
                h = heads[i]
                s = s_rcv[h]
                do = dcore_ref[:, lanes(h)]
                u = (uv_s[h] - dot(wq_s[h, 0:ROWS], s, 1, 1)).astype(BF)
                u_s[h] = u
                dos = columns(h)[2] * dot(do, s)
                dp = dot(do, u, 1, 1)
                f = dp * p_s[h]
                packed = packed + jnp.where(
                    lane == i, jnp.sum(f + q * dos, axis=1, keepdims=True), 0.0
                )
                colsums.append(jnp.sum(f, axis=0, keepdims=True))
                bq = dp * d_s[h]
                bs = bq if bs is None else bs + bq
                dq = dos if dq is None else dq + dos
            bs = bs.astype(BF)
            dq = dq + dot(bs, k.astype(BF))
            dk_s[j] = dot(bs, q.astype(BF), 0, 0)
            dm = norms[j] * (dq - q * (D * jnp.sum(q * dq, axis=1, keepdims=True)))
            conv_back(j, group, n, dm)
        dcs[group] = jnp.transpose(packed)[:HG] - jnp.concatenate(colsums, axis=0)

        @pl.when(group > 0)
        def _():
            send_piece(group)
        return 0

    def backward(step, _):
        group, qk, heads = group_of(step)
        k_piece, v_piece = GROUPS + group, 2 * (GROUPS + group)
        for h in heads:
            @pl.when(h != me)
            def _():
                g_copy(h, h).wait_recv()
        packed = jnp.zeros((ROWS, D), F32)
        colsums, lasts = [], []
        for n, j in enumerate(qk):
            k = ks[j]
            es, dk = None, dk_s[j]
            for i in (2 * n, 2 * n + 1):
                h = heads[i]
                s, g, u = s_rcv[h], g_rcv[h], u_s[h]
                r = r0_s[h] + dot(w2_s[h], g, 1, 1)
                rb = r.astype(BF)
                rs = dot(rb, s)
                da = -dot(rb, u, 1, 1)
                ug = dot(u, g)
                f = da * a_s[h]
                kug = ek_s[h] * ug
                dbeta = jnp.sum(r * v_s[h] - ck_s[h] * rs + da * dkk_s[h], axis=1, keepdims=True)
                dc = jnp.sum(f - bck_s[h] * rs - kug, axis=1, keepdims=True)
                packed = packed + jnp.where(lane == i, dc, 0.0)
                packed = packed + jnp.where(lane == HG + i, dbeta, 0.0)
                colsums.append(jnp.sum(f, axis=0, keepdims=True))
                lasts.append(
                    jnp.sum(
                        jnp.sum(kug, axis=0, keepdims=True)
                        + a_last(h)
                        * jnp.sum(g.astype(F32) * s.astype(F32), axis=0, keepdims=True),
                        axis=1, keepdims=True,
                    )
                )
                e = da * e_s[h]
                es = e if es is None else es + e
                dk = dk + end_s[h] * ug - bc_s[h] * rs
                conv_back(2 * QK + h, v_piece + i // 2, i % 2, b_s[h] * r)
            es = es.astype(BF)
            kb = k.astype(BF)
            dk = dk + dot(es, kb) + dot(es, kb, 0, 0)
            dm = norms[QK + j] * (dk - k * jnp.sum(k * dk, axis=1, keepdims=True))
            conv_back(QK + j, k_piece, n, dm)
        rows = jnp.transpose(packed)
        lasts = jnp.concatenate(lasts, axis=0)
        dc = rows[:HG] - jnp.concatenate(colsums, axis=0) + dcs[group]
        dgo[0, group] = dc + jnp.where(lane[:HG] == D - 1, lasts, 0.0)
        dgo[1, group] = rows[HG : 2 * HG]
        for piece in (k_piece, v_piece, v_piece + 1):
            send_piece(piece)
        return 0

    lax.fori_loop(0, GROUPS, from_state, 0)
    lax.fori_loop(0, GROUPS, results, 0)
    core_copy = pltpu.make_async_copy(core_ref, core_hbm, io_sem.at[2])
    core_copy.start()
    lax.fori_loop(0, GROUPS, backward, 0)

    def all_groups(ref, which):
        return jnp.concatenate([ref[which, n] for n in range(GROUPS)], axis=0)

    dg = dot_full(all_groups(dgo, 0), suffix)
    dz = dg * all_groups(gts, 1)
    bet = all_groups(gts, 2)
    sums = dot_full(
        jnp.ones((8, D), F32), jnp.concatenate([dg * all_groups(gts, 0), dz], axis=0), 1, 1
    )
    red[0, 4:5, 0 : 2 * HEADS] = sums[0:1]
    send_piece(0)
    dbet = all_groups(dgo, 1) * bet * (1.0 - bet)
    for n in range(GROUPS):
        for at, a, b in parts_of(n):
            lo = n * HG + at
            dgate_ref[a:b, :] = dz[lo : lo + 2]
            dgate_ref[HEADS + a : HEADS + b, :] = dbet[lo : lo + 2]

    spill = jnp.zeros((8, CH), F32)
    row8w = iota((8, CH), 0)
    for j in range(3):
        link8 = jnp.concatenate([links[j, 0:8]] * (CH // D), axis=1)
        turned = pltpu.roll(slope[0:8, :] * link8 * w_ref[j : j + 1, :], 5 + j, 0)
        spill = spill + jnp.where(row8w >= 5 + j, turned, 0.0)
    h_snd[...] = jnp.concatenate(
        [spill[5 + r : 6 + r, 1024 * p : 1024 * p + 1024] for r in range(3) for p in range(4)]
        + [jnp.zeros((4, 1024), F32)],
        axis=0,
    ).astype(BF)
    back = pltpu.make_async_remote_copy(
        src_ref=h_snd, dst_ref=e_rcv, send_sem=e_sem.at[0], recv_sem=e_sem.at[1],
        device_id={"ctx": lax.rem(me + BLOCKS - 1, BLOCKS)}, device_id_type=MESH,
    )
    back.start()

    def wait_red(i, _):
        other = lax.rem(me + i, BLOCKS)
        red_copy(other, other).wait_recv()
        return 0

    lax.fori_loop(1, BLOCKS, wait_red, 0, unroll=True)
    total = r1[0]
    for i in range(1, BLOCKS):
        total = total + r1[i]
    r2[mine] = total

    def dp_copy(other, source):
        return pltpu.make_async_remote_copy(
            src_ref=r2.at[source], dst_ref=r2.at[source], send_sem=r2_ssem.at[other],
            recv_sem=r2_rsem.at[source], device_id={"dp": other}, device_id_type=MESH,
        )

    def send_dp(i, _):
        dp_copy(lax.rem(mine + i, DP), mine).start()
        return 0

    lax.fori_loop(1, DP, send_dp, 0, unroll=True)

    back.wait()
    before_last = jnp.where(me < BLOCKS - 1, 1.0, 0.0)
    ev = e_rcv[...].astype(F32) * before_last
    for p in range(4):
        e_add[:, 1024 * p : 1024 * p + 1024] = jnp.concatenate(
            [jnp.zeros((5, 1024), F32)] + [ev[4 * r + p : 4 * r + p + 1] for r in range(3)], axis=0
        )

    def mixed_part(step, _):
        for i in range(4):
            taps_back(4 * step + i)
        return 0

    lax.fori_loop(0, 4, mixed_part, 0)

    def mixed_copy(half):
        part = pl.ds(half * (CH // 2), CH // 2)
        return pltpu.make_async_copy(
            dmix_ref.at[:, part], dmix_hbm.at[:, part], io_sem.at[3 + half]
        )

    mixed_copy(0).start()

    def wait_dp(i, _):
        other = lax.rem(mine + i, DP)
        dp_copy(other, other).wait_recv()
        return 0

    lax.fori_loop(1, DP, wait_dp, 0, unroll=True)
    total = r2[0]
    for i in range(1, DP):
        total = total + r2[i]
    r3[me] = total

    def all_copy(other, source):
        return pltpu.make_async_remote_copy(
            src_ref=r3.at[source], dst_ref=r3.at[source], send_sem=r3_ssem.at[other],
            recv_sem=r3_rsem.at[source], device_id={"ctx": other}, device_id_type=MESH,
        )

    def send_all(i, _):
        all_copy(lax.rem(me + i, BLOCKS), me).start()
        return 0

    lax.fori_loop(1, BLOCKS, send_all, 0, unroll=True)
    lax.fori_loop(4, 8, mixed_part, 0)
    mixed_copy(1).start()

    def drain(i, _):
        other = lax.rem(me + i, BLOCKS)
        pack_copy(other, me).wait_send()
        grad_pack_copy(other, me).wait_send()
        s_copy(other, me).wait_send()
        g_copy(other, me).wait_send()
        red_copy(other, me).wait_send()
        return 0

    lax.fori_loop(1, BLOCKS, drain, 0, unroll=True)

    def drain_dp(i, _):
        dp_copy(lax.rem(mine + i, DP), mine).wait_send()
        return 0

    lax.fori_loop(1, DP, drain_dp, 0, unroll=True)

    def wait_all(i, _):
        other = lax.rem(me + i, BLOCKS)
        all_copy(other, other).wait_recv()
        return 0

    lax.fori_loop(1, BLOCKS, wait_all, 0, unroll=True)
    for n in range(GROUPS):
        sums = r3[0, 4:5]
        for at, a, b in parts_of(n):
            lo = (at // 2) * D
            dconv_ref[:, a // 2 * D : a // 2 * D + D] = r3[n, 0:4, lo : lo + D]
            dconv_ref[:, (QK + a // 2) * D : (QK + a // 2 + 1) * D] = r3[GROUPS + n, 0:4, lo : lo + D]
            dconv_ref[:, (2 * QK + a) * D : (2 * QK + b) * D] = r3[2 * (GROUPS + n) + at // 2, 0:4]
            at += n * HG
            dhead_ref[0:1, a:b] = sums[:, at : at + 2]
            dhead_ref[1:2, a:b] = sums[:, HEADS + at : HEADS + at + 2]

    def drain_all(i, _):
        all_copy(lax.rem(me + i, BLOCKS), me).wait_send()
        return 0

    lax.fori_loop(1, BLOCKS, drain_all, 0, unroll=True)
    core_copy.wait()
    mixed_copy(0).wait()
    mixed_copy(1).wait()


def hand_on_kernel(n, *refs):
    ins, outs, bufs, sems = refs[:n], refs[n : 2 * n], refs[2 * n : 3 * n], refs[3 * n]
    parts = []
    for i in range(n):
        rows = ins[i].shape[0]
        size = 32 if rows == ROWS else rows
        parts += [(i, pl.ds(at, size)) for at in range(0, rows, size)]
    into = [
        pltpu.make_async_copy(ins[i].at[at], bufs[i].at[at], sems.at[0, m])
        for m, (i, at) in enumerate(parts)
    ]
    out = [
        pltpu.make_async_copy(bufs[i].at[at], outs[i].at[at], sems.at[1, m])
        for m, (i, at) in enumerate(parts)
    ]
    for c in into:
        c.start()
    for a, b in zip(into, out):
        a.wait()
        b.start()
    for c in out:
        c.wait()


def hand_on(*arrays):
    n = len(arrays)
    return pl.pallas_call(
        functools.partial(hand_on_kernel, n),
        out_shape=tuple(jax.ShapeDtypeStruct(a.shape, a.dtype) for a in arrays),
        in_specs=[pl.BlockSpec(memory_space=pl.ANY)] * n,
        out_specs=(pl.BlockSpec(memory_space=pl.ANY),) * n,
        scratch_shapes=[pltpu.VMEM(a.shape, a.dtype) for a in arrays]
        + [pltpu.SemaphoreType.DMA((2, 16))],
        name="hand_on",
    )(*arrays)


def on_device(mixed_in, conv_weight, gate_in, head_params, doc_lengths, d_core):
    vmem = pl.BlockSpec(memory_space=pltpu.VMEM)
    any_ = pl.BlockSpec(memory_space=pl.ANY)
    mat = (HEADS, D, D)
    scratch = [
        pltpu.VMEM((ROWS, CH), BF),
        pltpu.VMEM((ROWS, HEADS * D), BF),
        pltpu.VMEM((ROWS, HEADS * D), BF),
        pltpu.VMEM((ROWS, CH), BF),
        pltpu.SemaphoreType.DMA((5,)),
        pltpu.VMEM((ROWS + 8, CH), F32),
        pltpu.VMEM((ROWS, CH), F32),
        pltpu.VMEM((QK, D, D), F32),
        pltpu.VMEM((QK, D, D), F32),
        pltpu.VMEM((2 * QK, D, D), F32),
        pltpu.VMEM((3, ROWS, D), F32),
        pltpu.VMEM((ROWS, D), F32),
        pltpu.VMEM((HEADS, 8, D), F32),
        pltpu.VMEM((3, GROUPS, HG, D), F32),
        pltpu.VMEM(mat, F32),
        pltpu.VMEM(mat, F32),
        pltpu.VMEM(mat, F32),
        pltpu.VMEM(mat, F32),
        pltpu.VMEM(mat, F32),
        pltpu.VMEM((HEADS, 2 * D, D), BF),
        pltpu.VMEM(mat, BF),
        pltpu.VMEM(mat, F32),
        pltpu.VMEM(mat, F32),
        pltpu.VMEM((HEADS, PACK, D), BF),
        pltpu.VMEM((HEADS, PACK, D), BF),
        pltpu.VMEM(mat, BF),
        pltpu.VMEM(mat, BF),
        pltpu.VMEM(mat, BF),
        pltpu.VMEM(mat, BF),
        pltpu.VMEM(mat, BF),
        pltpu.VMEM(mat, BF),
        pltpu.VMEM((16, 1024), BF),
        pltpu.VMEM((16, 1024), BF),
        pltpu.VMEM((8, CH), F32),
        pltpu.VMEM((16, 1024), BF),
        pltpu.VMEM((2, GROUPS, HG, D), F32),
        pltpu.VMEM(mat, BF),
        pltpu.VMEM(mat, F32),
        pltpu.VMEM(mat, F32),
        pltpu.VMEM(mat, F32),
        pltpu.VMEM(mat, F32),
        pltpu.VMEM(mat, F32),
        pltpu.VMEM(mat, F32),
        pltpu.VMEM(mat, F32),
        pltpu.VMEM(mat, F32),
        pltpu.VMEM(mat, F32),
        pltpu.VMEM((QK, D, D), F32),
        pltpu.VMEM((GROUPS, HG, D), F32),
        pltpu.VMEM((BLOCKS, 8, PIECE), F32),
        pltpu.VMEM((BLOCKS, 8, PIECE), F32),
        pltpu.VMEM((DP, 8, PIECE), F32),
        pltpu.VMEM((BLOCKS, 8, PIECE), F32),
        pltpu.SemaphoreType.DMA((BLOCKS,)),
        pltpu.SemaphoreType.DMA((BLOCKS,)),
        pltpu.SemaphoreType.DMA((BLOCKS,)),
        pltpu.SemaphoreType.DMA((BLOCKS,)),
        pltpu.SemaphoreType.DMA((BLOCKS,)),
        pltpu.SemaphoreType.DMA((BLOCKS,)),
        pltpu.SemaphoreType.DMA((BLOCKS,)),
        pltpu.SemaphoreType.DMA((BLOCKS,)),
        pltpu.SemaphoreType.DMA((2,)),
        pltpu.SemaphoreType.DMA((2,)),
        pltpu.SemaphoreType.DMA((BLOCKS,)),
        pltpu.SemaphoreType.DMA((BLOCKS,)),
        pltpu.SemaphoreType.DMA((DP,)),
        pltpu.SemaphoreType.DMA((DP,)),
        pltpu.SemaphoreType.DMA((BLOCKS,)),
        pltpu.SemaphoreType.DMA((BLOCKS,)),
    ]
    core, dmix, dgate, dconv, dhead = pl.pallas_call(
        kernel,
        out_shape=(
            jax.ShapeDtypeStruct((ROWS, HEADS * D), BF),
            jax.ShapeDtypeStruct((ROWS, CH), BF),
            jax.ShapeDtypeStruct((2 * HEADS, ROWS), F32),
            jax.ShapeDtypeStruct((4, CH), F32),
            jax.ShapeDtypeStruct((2, HEADS), F32),
        ),
        in_specs=[any_, vmem, vmem, vmem, pl.BlockSpec(memory_space=pltpu.SMEM), any_],
        out_specs=(any_, any_, vmem, vmem, vmem),
        scratch_shapes=scratch,
        compiler_params=pltpu.CompilerParams(
            collective_id=0, has_side_effects=True, vmem_limit_bytes=56 * 1024 * 1024
        ),
        name="delta_mix",
    )(mixed_in[0], conv_weight, gate_in[0].T, head_params, doc_lengths, d_core[0])
    core, dmix, dgate, dconv, dhead = hand_on(core, dmix, dgate, dconv, dhead)
    return core[None], dmix[None], dgate.T[None], dconv, dhead


def solution(mesh):
    return jax.shard_map(
        on_device,
        mesh=mesh,
        in_specs=(
            P("dp", "ctx", None),
            P(),
            P("dp", "ctx", None),
            P(),
            P("dp", None),
            P("dp", "ctx", None),
        ),
        out_specs=(P("dp", "ctx", None), P("dp", "ctx", None), P("dp", "ctx", None), P(), P()),
        check_vma=False,
    )
```

```python
import functools

import jax
import jax.numpy as jnp
from jax import lax
from jax.experimental import pallas as pl
from jax.experimental.pallas import tpu as pltpu
from jax.sharding import PartitionSpec as P

HEADS = 16
QK = 8
D = 128
ROWS = 128
CH = 4096
BLOCKS = 16
PACK = 2 * D + 16
HG = 4
GROUPS = HEADS // HG
DP = 8
PIECE = CH // BLOCKS
F32 = jnp.float32
BF = jnp.bfloat16
MESH = pl.DeviceIdType.MESH
HIGHEST = lax.Precision.HIGHEST


def dot(a, b, ca=1, cb=0):
    return lax.dot_general(a, b, (((ca,), (cb,)), ((), ())), preferred_element_type=F32)


def dot_full(a, b, ca=1, cb=0):
    return lax.dot_general(
        a, b, (((ca,), (cb,)), ((), ())), preferred_element_type=F32, precision=HIGHEST
    )


def split(a):
    high = a.astype(BF)
    return high, (a - high.astype(F32)).astype(BF)


def dot3(a, b, ca=1, cb=0):
    left = jnp.concatenate(a, axis=ca)
    wide = jnp.concatenate(b, axis=1 - cb)
    n = b[0].shape[1 - cb]
    t = dot(left, jnp.concatenate([wide, wide], axis=cb), ca, cb)
    return t[:, :n] + t[:, n:]


def iota(shape, dim):
    return lax.broadcasted_iota(jnp.int32, shape, dim)


def inverses(mats):
    row, col = iota((D, D), 0), iota((D, D), 1)
    eye = (row == col).astype(F32)

    def same(bits):
        return (row >> bits) == (col >> bits)

    near = same(3)
    a8 = [jnp.where(near, a, 0.0) for a in mats]
    a8s = [split(a) for a in a8]
    a2 = [dot3(s, s) for s in a8s]
    a2s = [split(a) for a in a2]
    a3 = [dot3(s, t) for s, t in zip(a8s, a2s)]
    a4s = [split(dot3(s, s)) for s in a2s]
    ys = [eye - a + b - c for a, b, c in zip(a8, a2, a3)]
    xs = [y + dot3(split(y), s) for y, s in zip(ys, a4s)]
    for bits in range(3, 7):
        mask = same(bits + 1) & jnp.logical_not(same(bits))
        cs = [split(jnp.where(mask, a, 0.0)) for a in mats]
        xss = [split(x) for x in xs]
        xc = [split(dot3(x, c)) for x, c in zip(xss, cs)]
        xs = [x - dot3(t, s) for x, t, s in zip(xs, xc, xss)]
    return xs


def parts_of(group):
    first, second = 4 * group, 4 * ((group + 2) % 4) + 2
    return [(0, first, first + 2), (2, second, second + 2)]


def kernel(
    x_hbm, w_ref, gate_ref, hp_ref, len_ref, dcore_hbm,
    core_hbm, dmix_hbm, dgate_ref, dconv_ref, dhead_ref,
    x_ref, dcore_ref, core_ref, dmix_ref, io_sem, xs, slope, qs, ks, norms, links, lks, gt, gts, d_s, dkk_s, p_s, x_s, uv_s, wq_s, w2_s, r0_s, ol_s,
    snd, rcv, snd2, rcv2, s_snd, g_snd, s_rcv, g_rcv, h_snd, h_rcv, e_add, e_rcv, dgo, u_s, a_s, v_s, b_s, e_s, ck_s, bck_s, bc_s, ek_s, end_s, dk_s, dcs, red, r1, r2, r3,
    snd_sem, rcv_sem, snd2_sem, rcv2_sem, s_ssem, s_rsem, g_ssem, g_rsem, h_sem, e_sem,
    r1_ssem, r1_rsem, r2_ssem, r2_rsem, r3_ssem, r3_rsem,
):
    me = lax.axis_index("ctx")
    mine = lax.axis_index("dp")
    first_pos = me * ROWS

    x_copy = pltpu.make_async_copy(x_hbm, x_ref, io_sem.at[0])
    dcore_copy = pltpu.make_async_copy(dcore_hbm, dcore_ref, io_sem.at[1])
    x_copy.start()
    dcore_copy.start()
    own_row = lax.div(me, 4)
    own_pair = lax.rem(lax.div(me, 2), 2)

    def group_of(step):
        group = lax.rem(own_row + step + 2 * own_pair, 4)
        qk = [2 * group, 2 * lax.rem(group + 2, 4) + 1]
        return group, qk, [2 * j + i for j in qk for i in range(2)]

    barrier = pltpu.get_barrier_semaphore()

    def greet(i, _):
        pl.semaphore_signal(
            barrier, inc=1, device_id={"ctx": lax.rem(me + i, BLOCKS)}, device_id_type=MESH
        )
        return 0

    lax.fori_loop(1, BLOCKS, greet, 0, unroll=True)

    def greet_dp(i, _):
        pl.semaphore_signal(
            barrier, inc=1, device_id={"dp": lax.rem(mine + i, DP)}, device_id_type=MESH
        )
        return 0

    lax.fori_loop(1, DP, greet_dp, 0, unroll=True)

    x_copy.wait()
    xs[pl.ds(8, ROWS), :] = x_ref[...].astype(F32)
    xs[0:8, :] = jnp.zeros((8, CH), F32)
    tail = [
        xs[pl.ds(133 + r, 1), pl.ds(1024 * p, 1024)] for r in range(3) for p in range(4)
    ] + [jnp.zeros((4, 1024), F32)]
    h_snd[...] = jnp.concatenate(tail, axis=0).astype(BF)

    pl.semaphore_wait(barrier, BLOCKS + DP - 2)

    def halo_copy():
        return pltpu.make_async_remote_copy(
            src_ref=h_snd, dst_ref=h_rcv, send_sem=h_sem.at[0], recv_sem=h_sem.at[1],
            device_id={"ctx": lax.rem(me + 1, BLOCKS)}, device_id_type=MESH,
        )

    halo_copy().start()

    row, col = iota((ROWS, D), 0), iota((ROWS, D), 1)
    low = row >= col
    strict = row > col
    ends = []
    total = 0
    for i in range(8):
        total = total + len_ref[0, i]
        ends.append(total)

    def doc_of(pos):
        found = jnp.zeros(pos.shape, jnp.int32)
        for e in ends:
            found = found + jnp.where(e <= pos, 1, 0)
        return found

    doc_col = doc_of(first_pos + row)
    doc_row = doc_of(first_pos + col)
    lks[...] = jnp.where((doc_col == doc_row) & low, 1.0, 0.0)
    for j in range(3):
        links[j] = jnp.where(doc_of(first_pos + row - 3 + j) == doc_col, 1.0, 0.0)
    doc_row16 = doc_row[:HEADS]
    doc_before = doc_of(jnp.full((HEADS, D), first_pos - 1, jnp.int32))
    doc_last = doc_of(jnp.full((HEADS, D), first_pos + ROWS - 1, jnp.int32))

    def lanes(block):
        return pl.ds(pl.multiple_of(block * D, D), D)

    def taps(j, block):
        t = xs[pl.ds(5 + j, ROWS), lanes(block)]
        return t if j == 3 else t * links[j]

    def conv_first(step, _):
        for i in range(4):
            block = 4 * step + i
            y = taps(3, block) * w_ref[3:4, lanes(block)]
            for j in range(3):
                y = y + taps(j, block) * w_ref[j : j + 1, lanes(block)]
            slope[:, lanes(block)] = y
        return 0

    lax.fori_loop(0, 8, conv_first, 0, unroll=2)

    def conv(block):
        y = slope[:, lanes(block)]
        sig = 1.0 / (1.0 + jnp.exp(-y))
        m = y * sig
        slope[:, lanes(block)] = sig + m * (1.0 - sig)
        return m

    eye16 = (iota((16, 16), 0) == iota((16, 16), 1)).astype(F32)
    gates = gate_ref[...]
    params = dot_full(eye16, hp_ref[...], 1, 1)
    scale = -jnp.exp(params[:, 0:1])
    z = gates[:HEADS] + params[:, 1:2]
    decay = scale * (jnp.maximum(z, 0.0) + jnp.log1p(jnp.exp(-jnp.abs(z))))
    ez = scale / (1.0 + jnp.exp(-z))
    beta = 1.0 / (1.0 + jnp.exp(-gates[HEADS:]))
    upto = jnp.where(row <= col, 1.0, 0.0)
    summed = dot_full(decay, upto)
    carried = jnp.exp(summed) * (doc_row16 == doc_before).astype(F32)
    to_end = jnp.exp(jnp.minimum(summed[:, D - 1 : D] - summed, 0.0)) * (
        doc_row16 == doc_last
    ).astype(F32)
    for n in range(GROUPS):
        for at, a, b in parts_of(n):
            gts[0, n, at : at + 2] = decay[a:b]
            gts[1, n, at : at + 2] = ez[a:b]
            gts[2, n, at : at + 2] = beta[a:b]
    rows8 = jnp.stack(
        [summed, beta, carried, to_end, beta * carried, summed, summed, summed], axis=1
    )
    gt[...] = rows8

    halo_copy().wait()
    inside = jnp.where(me > 0, 1.0, 0.0)
    hv = h_rcv[...].astype(F32) * inside
    for r in range(3):
        for p in range(4):
            xs[pl.ds(5 + r, 1), pl.ds(1024 * p, 1024)] = hv[4 * r + p : 4 * r + p + 1]
    y8 = xs[8:16, :] * w_ref[3:4, :]
    for j in range(3):
        link8 = jnp.concatenate([links[j, 0:8]] * (CH // D), axis=1)
        y8 = y8 + xs[5 + j : 13 + j, :] * link8 * w_ref[j : j + 1, :]
    slope[0:8, :] = y8
    dcore_copy.wait()


    def columns(h):
        t = jnp.transpose(gt[h])
        return [t[:, i : i + 1] for i in range(5)]

    def a_last(h):
        return gt[h][2:3, D - 1 : D]

    def pack_copy(h, source):
        return pltpu.make_async_remote_copy(
            src_ref=snd.at[h], dst_ref=rcv.at[source], send_sem=snd_sem.at[h],
            recv_sem=rcv_sem.at[source], device_id={"ctx": h}, device_id_type=MESH,
        )

    def grad_pack_copy(h, source):
        return pltpu.make_async_remote_copy(
            src_ref=snd2.at[h], dst_ref=rcv2.at[source], send_sem=snd2_sem.at[h],
            recv_sem=rcv2_sem.at[source], device_id={"ctx": h}, device_id_type=MESH,
        )

    def send_grad_packs(step):
        for h in group_of(step)[2]:
            @pl.when(h != me)
            def _():
                grad_pack_copy(h, me).start()

    def forward(step, _):
        _, qk, heads = group_of(step)
        kk, qq, kf, qf = [], [], [], []
        for j in qk:
            m = conv(j)
            norm = lax.rsqrt(jnp.sum(m * m, axis=1, keepdims=True) + 1e-6) * D**-0.5
            norms[j] = jnp.broadcast_to(norm, (ROWS, D))
            q = m * norm
            m = conv(QK + j)
            norm = lax.rsqrt(jnp.sum(m * m, axis=1, keepdims=True) + 1e-6)
            norms[QK + j] = jnp.broadcast_to(norm, (ROWS, D))
            k = m * norm
            qs[j] = q
            ks[j] = k
            k2, q2 = split(k), split(q)
            kk.append(dot3(k2, k2, 1, 1))
            qq.append(dot3(q2, k2, 1, 1))
            kf.append(k)
            qf.append(q)
        vs = [conv(2 * QK + h) for h in heads]
        cols = [columns(h) for h in heads]
        lk = lks[...]
        mats, ps = [], []
        for i, h in enumerate(heads):
            spans = lk * jnp.exp(jnp.minimum(cols[i][0] - gt[h][0:1], 0.0))
            dkk = jnp.where(strict, spans * kk[i // 2], 0.0)
            p = spans * qq[i // 2]
            mat = cols[i][1] * dkk
            d_s[h] = spans
            dkk_s[h] = dkk
            a_s[h] = mat
            p_s[h] = p
            v_s[h] = vs[i]
            ps.append(p.astype(BF))
            mats.append(mat)
        xinv = inverses(mats)
        for i, h in enumerate(heads):
            x_s[h] = xinv[i]
            right = jnp.concatenate([cols[i][1] * vs[i], cols[i][4] * kf[i // 2]], axis=1)
            uvw = dot3(split(xinv[i]), split(right))
            uvwb = uvw.astype(BF)
            uv_s[h] = uvw[:, :D]
            wq_s[h, 0:ROWS] = uvwb[:, D:]
            pw = dot(ps[i], uvwb)
            ol_s[h] = pw[:, :D]
            qc = (cols[i][2] * qf[i // 2] - pw[:, D:]).astype(BF)
            wq_s[h, ROWS : 2 * ROWS] = qc
            dk = (cols[i][3] * kf[i // 2]).astype(BF)
            nb = dot(uvwb, dk, 0, 0)
            gl = dot(dcore_ref[:, lanes(h)], qc, 0, 0)
            snd[h, 0:D] = nb[D:].astype(BF)
            snd[h, D : 2 * D] = nb[:D].astype(BF)
            snd2[h] = gl.astype(BF)
            al = jnp.broadcast_to(a_last(h), (16, D))
            t0 = al.astype(BF).astype(F32)
            t1 = (al - t0).astype(BF).astype(F32)
            t2 = al - t0 - t1
            r16 = iota((16, D), 0)
            snd[h, 2 * D : PACK] = jnp.where(
                r16 == 0, t0, jnp.where(r16 == 1, t1, jnp.where(r16 == 2, t2, 0.0))
            ).astype(BF)
        for h in heads:
            @pl.when(h != me)
            def _():
                pack_copy(h, me).start()
        return 0

    lax.fori_loop(0, GROUPS, forward, 0)
    for n in range(GROUPS):
        send_grad_packs(n)
    rcv[me] = snd[me]
    rcv2[me] = snd2[me]

    def aside(step, _):
        heads = [step * HG + i for i in range(HG)]
        for i, h in enumerate(heads):
            cols = columns(h)
            zz = dot(p_s[h].astype(BF), dcore_ref[:, lanes(h)], 0, 0)
            k = ks[h // 2]
            dk = cols[3] * k
            b_s[h] = jnp.broadcast_to(cols[1], (ROWS, D))
            e_s[h] = jnp.where(strict, cols[1] * d_s[h], 0.0)
            ck_s[h] = cols[2] * k
            bck_s[h] = cols[4] * k
            bc_s[h] = jnp.broadcast_to(cols[4], (ROWS, D))
            ek_s[h] = dk
            end_s[h] = jnp.broadcast_to(cols[3], (ROWS, D))
            out = dot3(split(x_s[h]), split(jnp.concatenate([zz, dk], axis=1)), 0, 0)
            r0_s[h] = out[:, :D]
            w2_s[h] = out[:, D:].astype(BF)
        return 0


    def s_copy(block, head):
        return pltpu.make_async_remote_copy(
            src_ref=s_snd.at[block], dst_ref=s_rcv.at[head], send_sem=s_ssem.at[block],
            recv_sem=s_rsem.at[head], device_id={"ctx": block}, device_id_type=MESH,
        )

    def g_copy(block, head):
        return pltpu.make_async_remote_copy(
            src_ref=g_snd.at[block], dst_ref=g_rcv.at[head], send_sem=g_ssem.at[block],
            recv_sem=g_rsem.at[head], device_id={"ctx": block}, device_id_type=MESH,
        )

    lax.fori_loop(0, GROUPS, aside, 0)

    def wait_pack(i, _):
        pack_copy(lax.rem(me + i, BLOCKS), lax.rem(me + i, BLOCKS)).wait_recv()
        return 0

    lax.fori_loop(1, BLOCKS, wait_pack, 0, unroll=True)

    zero = jnp.zeros((D, D), F32)
    s_snd[0] = zero.astype(BF)
    g_snd[BLOCKS - 1] = zero.astype(BF)

    def scalar_of(block):
        t = rcv[block, 2 * D : PACK].astype(F32)
        return t[0:1] + t[1:2] + t[2:3]

    def turn(i, state):
        state = (
            scalar_of(i) * state
            - dot(state.astype(BF), rcv[i, 0:D])
            + rcv[i, D : 2 * D].astype(F32)
        )
        s_snd[i + 1] = state.astype(BF)
        return state

    lax.fori_loop(0, BLOCKS - 1, turn, zero, unroll=True)

    def reader(i):
        step, which = lax.div(i, 4), lax.rem(lax.div(i, 2), 2)
        row = lax.rem(own_row + 8 - step - 2 * which, 4)
        return 4 * row + 2 * lax.rem(own_pair + which, 2) + lax.rem(i, 2)

    def send_state(i, _):
        other = reader(i)

        @pl.when(other != me)
        def _():
            s_copy(other, me).start()
        return 0

    lax.fori_loop(0, BLOCKS, send_state, 0, unroll=True)

    def wait_grad_pack(i, _):
        other = lax.rem(me + i, BLOCKS)
        grad_pack_copy(other, other).wait_recv()
        return 0

    lax.fori_loop(1, BLOCKS, wait_grad_pack, 0, unroll=True)

    def turn_back(i, grad):
        b = BLOCKS - 1 - i
        grad = (
            scalar_of(b) * grad
            - dot(grad.astype(BF), rcv[b, 0:D], 1, 1)
            + rcv2[b].astype(F32)
        )
        g_snd[b - 1] = grad.astype(BF)
        return grad

    lax.fori_loop(0, BLOCKS - 1, turn_back, zero, unroll=True)

    def send_grad(i, _):
        other = reader(i)

        @pl.when(other != me)
        def _():
            g_copy(other, me).start()
        return 0

    lax.fori_loop(0, BLOCKS, send_grad, 0, unroll=True)
    s_rcv[me] = s_snd[me]
    g_rcv[me] = g_snd[me]


    lane = col

    def conv_back(block, piece, half, dm):
        at = pl.ds(half * D, D)
        dy = dm * slope[:, lanes(block)]
        slope[:, lanes(block)] = dy
        for j in range(4):
            red[piece, j : j + 1, at] = jnp.sum(dy * taps(j, block), axis=0, keepdims=True)

    def taps_back(block):
        dy = slope[:, lanes(block)]
        own = dy * w_ref[3:4, lanes(block)]
        for j in range(3):
            turned = pltpu.roll(dy * links[j] * w_ref[j : j + 1, lanes(block)], ROWS - 3 + j, 0)
            own = own + jnp.where(row >= ROWS - 3 + j, 0.0, turned)
        last = own[ROWS - 8 :] + e_add[:, lanes(block)]
        dmix_ref[:, lanes(block)] = jnp.concatenate([own[: ROWS - 8], last], axis=0).astype(BF)

    def results(step, _):
        for i in range(HG):
            h = step * HG + i
            core_ref[:, lanes(h)] = (
                ol_s[h] + dot(wq_s[h, ROWS : 2 * ROWS], s_rcv[h], 1, 1)
            ).astype(BF)
        return 0

    suffix = jnp.where(row >= col, 1.0, 0.0)
    red[:, 4:8, :] = jnp.zeros((BLOCKS, 4, PIECE), F32)

    def red_copy(piece, source):
        return pltpu.make_async_remote_copy(
            src_ref=red.at[piece], dst_ref=r1.at[source], send_sem=r1_ssem.at[piece],
            recv_sem=r1_rsem.at[source], device_id={"ctx": piece}, device_id_type=MESH,
        )

    def send_piece(piece):
        @pl.when(piece != me)
        def _():
            red_copy(piece, me).start()

        @pl.when(piece == me)
        def _():
            r1[me] = red[piece]

    def from_state(step, _):
        group, qk, heads = group_of(step)
        for h in heads:
            @pl.when(h != me)
            def _():
                s_copy(h, h).wait_recv()
        packed = jnp.zeros((ROWS, D), F32)
        colsums = []
        for n, j in enumerate(qk):
            k, q = ks[j], qs[j]
            bs = dq = None
            for i in (2 * n, 2 * n + 1):
                h = heads[i]
                s = s_rcv[h]
                do = dcore_ref[:, lanes(h)]
                u = (uv_s[h] - dot(wq_s[h, 0:ROWS], s, 1, 1)).astype(BF)
                u_s[h] = u
                dos = columns(h)[2] * dot(do, s)
                dp = dot(do, u, 1, 1)
                f = dp * p_s[h]
                packed = packed + jnp.where(
                    lane == i, jnp.sum(f + q * dos, axis=1, keepdims=True), 0.0
                )
                colsums.append(jnp.sum(f, axis=0, keepdims=True))
                bq = dp * d_s[h]
                bs = bq if bs is None else bs + bq
                dq = dos if dq is None else dq + dos
            bs = bs.astype(BF)
            dq = dq + dot(bs, k.astype(BF))
            dk_s[j] = dot(bs, q.astype(BF), 0, 0)
            dm = norms[j] * (dq - q * (D * jnp.sum(q * dq, axis=1, keepdims=True)))
            conv_back(j, group, n, dm)
        dcs[group] = jnp.transpose(packed)[:HG] - jnp.concatenate(colsums, axis=0)

        @pl.when(group > 0)
        def _():
            send_piece(group)
        return 0

    def backward(step, _):
        group, qk, heads = group_of(step)
        k_piece, v_piece = GROUPS + group, 2 * (GROUPS + group)
        for h in heads:
            @pl.when(h != me)
            def _():
                g_copy(h, h).wait_recv()
        packed = jnp.zeros((ROWS, D), F32)
        colsums, lasts = [], []
        for n, j in enumerate(qk):
            k = ks[j]
            es, dk = None, dk_s[j]
            for i in (2 * n, 2 * n + 1):
                h = heads[i]
                s, g, u = s_rcv[h], g_rcv[h], u_s[h]
                r = r0_s[h] + dot(w2_s[h], g, 1, 1)
                rb = r.astype(BF)
                rs = dot(rb, s)
                da = -dot(rb, u, 1, 1)
                ug = dot(u, g)
                f = da * a_s[h]
                kug = ek_s[h] * ug
                dbeta = jnp.sum(r * v_s[h] - ck_s[h] * rs + da * dkk_s[h], axis=1, keepdims=True)
                dc = jnp.sum(f - bck_s[h] * rs - kug, axis=1, keepdims=True)
                packed = packed + jnp.where(lane == i, dc, 0.0)
                packed = packed + jnp.where(lane == HG + i, dbeta, 0.0)
                colsums.append(jnp.sum(f, axis=0, keepdims=True))
                lasts.append(
                    jnp.sum(
                        jnp.sum(kug, axis=0, keepdims=True)
                        + a_last(h)
                        * jnp.sum(g.astype(F32) * s.astype(F32), axis=0, keepdims=True),
                        axis=1, keepdims=True,
                    )
                )
                e = da * e_s[h]
                es = e if es is None else es + e
                dk = dk + end_s[h] * ug - bc_s[h] * rs
                conv_back(2 * QK + h, v_piece + i // 2, i % 2, b_s[h] * r)
            es = es.astype(BF)
            kb = k.astype(BF)
            dk = dk + dot(es, kb) + dot(es, kb, 0, 0)
            dm = norms[QK + j] * (dk - k * jnp.sum(k * dk, axis=1, keepdims=True))
            conv_back(QK + j, k_piece, n, dm)
        rows = jnp.transpose(packed)
        lasts = jnp.concatenate(lasts, axis=0)
        dc = rows[:HG] - jnp.concatenate(colsums, axis=0) + dcs[group]
        dgo[0, group] = dc + jnp.where(lane[:HG] == D - 1, lasts, 0.0)
        dgo[1, group] = rows[HG : 2 * HG]
        for piece in (k_piece, v_piece, v_piece + 1):
            send_piece(piece)
        return 0

    lax.fori_loop(0, GROUPS, from_state, 0)
    lax.fori_loop(0, GROUPS, results, 0)
    core_copy = pltpu.make_async_copy(core_ref, core_hbm, io_sem.at[2])
    core_copy.start()
    lax.fori_loop(0, GROUPS, backward, 0)

    def all_groups(ref, which):
        return jnp.concatenate([ref[which, n] for n in range(GROUPS)], axis=0)

    dg = dot_full(all_groups(dgo, 0), suffix)
    dz = dg * all_groups(gts, 1)
    bet = all_groups(gts, 2)
    sums = dot_full(
        jnp.ones((8, D), F32), jnp.concatenate([dg * all_groups(gts, 0), dz], axis=0), 1, 1
    )
    red[0, 4:5, 0 : 2 * HEADS] = sums[0:1]
    send_piece(0)
    dbet = all_groups(dgo, 1) * bet * (1.0 - bet)
    for n in range(GROUPS):
        for at, a, b in parts_of(n):
            lo = n * HG + at
            dgate_ref[a:b, :] = dz[lo : lo + 2]
            dgate_ref[HEADS + a : HEADS + b, :] = dbet[lo : lo + 2]

    spill = jnp.zeros((8, CH), F32)
    row8w = iota((8, CH), 0)
    for j in range(3):
        link8 = jnp.concatenate([links[j, 0:8]] * (CH // D), axis=1)
        turned = pltpu.roll(slope[0:8, :] * link8 * w_ref[j : j + 1, :], 5 + j, 0)
        spill = spill + jnp.where(row8w >= 5 + j, turned, 0.0)
    h_snd[...] = jnp.concatenate(
        [spill[5 + r : 6 + r, 1024 * p : 1024 * p + 1024] for r in range(3) for p in range(4)]
        + [jnp.zeros((4, 1024), F32)],
        axis=0,
    ).astype(BF)
    back = pltpu.make_async_remote_copy(
        src_ref=h_snd, dst_ref=e_rcv, send_sem=e_sem.at[0], recv_sem=e_sem.at[1],
        device_id={"ctx": lax.rem(me + BLOCKS - 1, BLOCKS)}, device_id_type=MESH,
    )
    back.start()

    def wait_red(i, _):
        other = lax.rem(me + i, BLOCKS)
        red_copy(other, other).wait_recv()
        return 0

    lax.fori_loop(1, BLOCKS, wait_red, 0, unroll=True)
    total = r1[0]
    for i in range(1, BLOCKS):
        total = total + r1[i]
    r2[mine] = total

    def dp_copy(other, source):
        return pltpu.make_async_remote_copy(
            src_ref=r2.at[source], dst_ref=r2.at[source], send_sem=r2_ssem.at[other],
            recv_sem=r2_rsem.at[source], device_id={"dp": other}, device_id_type=MESH,
        )

    def send_dp(i, _):
        dp_copy(lax.rem(mine + i, DP), mine).start()
        return 0

    lax.fori_loop(1, DP, send_dp, 0, unroll=True)

    back.wait()
    before_last = jnp.where(me < BLOCKS - 1, 1.0, 0.0)
    ev = e_rcv[...].astype(F32) * before_last
    for p in range(4):
        e_add[:, 1024 * p : 1024 * p + 1024] = jnp.concatenate(
            [jnp.zeros((5, 1024), F32)] + [ev[4 * r + p : 4 * r + p + 1] for r in range(3)], axis=0
        )

    def mixed_part(step, _):
        for i in range(4):
            taps_back(4 * step + i)
        return 0

    lax.fori_loop(0, 4, mixed_part, 0, unroll=2)

    def mixed_copy(half):
        part = pl.ds(half * (CH // 2), CH // 2)
        return pltpu.make_async_copy(
            dmix_ref.at[:, part], dmix_hbm.at[:, part], io_sem.at[3 + half]
        )

    mixed_copy(0).start()

    def wait_dp(i, _):
        other = lax.rem(mine + i, DP)
        dp_copy(other, other).wait_recv()
        return 0

    lax.fori_loop(1, DP, wait_dp, 0, unroll=True)
    total = r2[0]
    for i in range(1, DP):
        total = total + r2[i]
    r3[me] = total

    def all_copy(other, source):
        return pltpu.make_async_remote_copy(
            src_ref=r3.at[source], dst_ref=r3.at[source], send_sem=r3_ssem.at[other],
            recv_sem=r3_rsem.at[source], device_id={"ctx": other}, device_id_type=MESH,
        )

    def send_all(i, _):
        all_copy(lax.rem(me + i, BLOCKS), me).start()
        return 0

    lax.fori_loop(1, BLOCKS, send_all, 0, unroll=True)
    lax.fori_loop(4, 8, mixed_part, 0, unroll=2)
    mixed_copy(1).start()

    def drain(i, _):
        other = lax.rem(me + i, BLOCKS)
        pack_copy(other, me).wait_send()
        grad_pack_copy(other, me).wait_send()
        s_copy(other, me).wait_send()
        g_copy(other, me).wait_send()
        red_copy(other, me).wait_send()
        return 0

    lax.fori_loop(1, BLOCKS, drain, 0, unroll=True)

    def drain_dp(i, _):
        dp_copy(lax.rem(mine + i, DP), mine).wait_send()
        return 0

    lax.fori_loop(1, DP, drain_dp, 0, unroll=True)

    def wait_all(i, _):
        other = lax.rem(me + i, BLOCKS)
        all_copy(other, other).wait_recv()
        return 0

    lax.fori_loop(1, BLOCKS, wait_all, 0, unroll=True)
    for n in range(GROUPS):
        sums = r3[0, 4:5]
        for at, a, b in parts_of(n):
            lo = (at // 2) * D
            dconv_ref[:, a // 2 * D : a // 2 * D + D] = r3[n, 0:4, lo : lo + D]
            dconv_ref[:, (QK + a // 2) * D : (QK + a // 2 + 1) * D] = r3[GROUPS + n, 0:4, lo : lo + D]
            dconv_ref[:, (2 * QK + a) * D : (2 * QK + b) * D] = r3[2 * (GROUPS + n) + at // 2, 0:4]
            at += n * HG
            dhead_ref[0:1, a:b] = sums[:, at : at + 2]
            dhead_ref[1:2, a:b] = sums[:, HEADS + at : HEADS + at + 2]

    def drain_all(i, _):
        all_copy(lax.rem(me + i, BLOCKS), me).wait_send()
        return 0

    lax.fori_loop(1, BLOCKS, drain_all, 0, unroll=True)
    core_copy.wait()
    mixed_copy(0).wait()
    mixed_copy(1).wait()


def hand_on_kernel(n, *refs):
    ins, outs, bufs, sems = refs[:n], refs[n : 2 * n], refs[2 * n : 3 * n], refs[3 * n]
    parts = []
    for i in range(n):
        rows = ins[i].shape[0]
        size = 32 if rows == ROWS else rows
        parts += [(i, pl.ds(at, size)) for at in range(0, rows, size)]
    into = [
        pltpu.make_async_copy(ins[i].at[at], bufs[i].at[at], sems.at[0, m])
        for m, (i, at) in enumerate(parts)
    ]
    out = [
        pltpu.make_async_copy(bufs[i].at[at], outs[i].at[at], sems.at[1, m])
        for m, (i, at) in enumerate(parts)
    ]
    for c in into:
        c.start()
    for a, b in zip(into, out):
        a.wait()
        b.start()
    for c in out:
        c.wait()


def hand_on(*arrays):
    n = len(arrays)
    return pl.pallas_call(
        functools.partial(hand_on_kernel, n),
        out_shape=tuple(jax.ShapeDtypeStruct(a.shape, a.dtype) for a in arrays),
        in_specs=[pl.BlockSpec(memory_space=pl.ANY)] * n,
        out_specs=(pl.BlockSpec(memory_space=pl.ANY),) * n,
        scratch_shapes=[pltpu.VMEM(a.shape, a.dtype) for a in arrays]
        + [pltpu.SemaphoreType.DMA((2, 16))],
        name="hand_on",
    )(*arrays)


def on_device(mixed_in, conv_weight, gate_in, head_params, doc_lengths, d_core):
    vmem = pl.BlockSpec(memory_space=pltpu.VMEM)
    any_ = pl.BlockSpec(memory_space=pl.ANY)
    mat = (HEADS, D, D)
    scratch = [
        pltpu.VMEM((ROWS, CH), BF),
        pltpu.VMEM((ROWS, HEADS * D), BF),
        pltpu.VMEM((ROWS, HEADS * D), BF),
        pltpu.VMEM((ROWS, CH), BF),
        pltpu.SemaphoreType.DMA((5,)),
        pltpu.VMEM((ROWS + 8, CH), F32),
        pltpu.VMEM((ROWS, CH), F32),
        pltpu.VMEM((QK, D, D), F32),
        pltpu.VMEM((QK, D, D), F32),
        pltpu.VMEM((2 * QK, D, D), F32),
        pltpu.VMEM((3, ROWS, D), F32),
        pltpu.VMEM((ROWS, D), F32),
        pltpu.VMEM((HEADS, 8, D), F32),
        pltpu.VMEM((3, GROUPS, HG, D), F32),
        pltpu.VMEM(mat, F32),
        pltpu.VMEM(mat, F32),
        pltpu.VMEM(mat, F32),
        pltpu.VMEM(mat, F32),
        pltpu.VMEM(mat, F32),
        pltpu.VMEM((HEADS, 2 * D, D), BF),
        pltpu.VMEM(mat, BF),
        pltpu.VMEM(mat, F32),
        pltpu.VMEM(mat, F32),
        pltpu.VMEM((HEADS, PACK, D), BF),
        pltpu.VMEM((HEADS, PACK, D), BF),
        pltpu.VMEM(mat, BF),
        pltpu.VMEM(mat, BF),
        pltpu.VMEM(mat, BF),
        pltpu.VMEM(mat, BF),
        pltpu.VMEM(mat, BF),
        pltpu.VMEM(mat, BF),
        pltpu.VMEM((16, 1024), BF),
        pltpu.VMEM((16, 1024), BF),
        pltpu.VMEM((8, CH), F32),
        pltpu.VMEM((16, 1024), BF),
        pltpu.VMEM((2, GROUPS, HG, D), F32),
        pltpu.VMEM(mat, BF),
        pltpu.VMEM(mat, F32),
        pltpu.VMEM(mat, F32),
        pltpu.VMEM(mat, F32),
        pltpu.VMEM(mat, F32),
        pltpu.VMEM(mat, F32),
        pltpu.VMEM(mat, F32),
        pltpu.VMEM(mat, F32),
        pltpu.VMEM(mat, F32),
        pltpu.VMEM(mat, F32),
        pltpu.VMEM((QK, D, D), F32),
        pltpu.VMEM((GROUPS, HG, D), F32),
        pltpu.VMEM((BLOCKS, 8, PIECE), F32),
        pltpu.VMEM((BLOCKS, 8, PIECE), F32),
        pltpu.VMEM((DP, 8, PIECE), F32),
        pltpu.VMEM((BLOCKS, 8, PIECE), F32),
        pltpu.SemaphoreType.DMA((BLOCKS,)),
        pltpu.SemaphoreType.DMA((BLOCKS,)),
        pltpu.SemaphoreType.DMA((BLOCKS,)),
        pltpu.SemaphoreType.DMA((BLOCKS,)),
        pltpu.SemaphoreType.DMA((BLOCKS,)),
        pltpu.SemaphoreType.DMA((BLOCKS,)),
        pltpu.SemaphoreType.DMA((BLOCKS,)),
        pltpu.SemaphoreType.DMA((BLOCKS,)),
        pltpu.SemaphoreType.DMA((2,)),
        pltpu.SemaphoreType.DMA((2,)),
        pltpu.SemaphoreType.DMA((BLOCKS,)),
        pltpu.SemaphoreType.DMA((BLOCKS,)),
        pltpu.SemaphoreType.DMA((DP,)),
        pltpu.SemaphoreType.DMA((DP,)),
        pltpu.SemaphoreType.DMA((BLOCKS,)),
        pltpu.SemaphoreType.DMA((BLOCKS,)),
    ]
    core, dmix, dgate, dconv, dhead = pl.pallas_call(
        kernel,
        out_shape=(
            jax.ShapeDtypeStruct((ROWS, HEADS * D), BF),
            jax.ShapeDtypeStruct((ROWS, CH), BF),
            jax.ShapeDtypeStruct((2 * HEADS, ROWS), F32),
            jax.ShapeDtypeStruct((4, CH), F32),
            jax.ShapeDtypeStruct((2, HEADS), F32),
        ),
        in_specs=[any_, vmem, vmem, vmem, pl.BlockSpec(memory_space=pltpu.SMEM), any_],
        out_specs=(any_, any_, vmem, vmem, vmem),
        scratch_shapes=scratch,
        compiler_params=pltpu.CompilerParams(
            collective_id=0, has_side_effects=True, vmem_limit_bytes=56 * 1024 * 1024
        ),
        name="delta_mix",
    )(mixed_in[0], conv_weight, gate_in[0].T, head_params, doc_lengths, d_core[0])
    core, dmix, dgate, dconv, dhead = hand_on(core, dmix, dgate, dconv, dhead)
    return core[None], dmix[None], dgate.T[None], dconv, dhead


def solution(mesh):
    return jax.shard_map(
        on_device,
        mesh=mesh,
        in_specs=(
            P("dp", "ctx", None),
            P(),
            P("dp", "ctx", None),
            P(),
            P("dp", None),
            P("dp", "ctx", None),
        ),
        out_specs=(P("dp", "ctx", None), P("dp", "ctx", None), P("dp", "ctx", None), P(), P()),
        check_vma=False,
    )
```
